32 devices in a mesh: groups: 2 (over y), vocab: 4 (over z), ctx: 2 (over x), dp: 2 (over core).
Axes of the slice: x: 2, y: 2, z: 4, core: 2. Of those that a mesh axis runs over, the one named last changes fastest.
Arguments:
- hidden: bfloat16 [4096, 4, 2, 128], P('vocab', ('groups', 'dp'), None, 'ctx'), parts along dimension 1, may hold values from -36 to 36, as said below
- head_weight: bfloat16 [4096, 8192], P(None, ('vocab', 'ctx', 'dp')), may hold values from -3 to 3, as said below
- targets: int32 [4, 2, 128], P('groups'), parts along dimension 0, may hold values from 0 to 8191
- response_start: int32 [4], P('groups'), parts along dimension 0, may hold values from 0 to 63
- other_sums: float32 [4, 2], P('groups'), parts along dimension 0, may hold values from -12 to 12
- ref_logp: float32 [4, 2], P('groups'), parts along dimension 0, may hold values from -12 to 12
- loss_cotangent: float32 [4], P('groups'), parts along dimension 0, may hold values from 130 to 516
Outputs:
- grad_hidden: bfloat16 [4096, 4, 2, 128], P('vocab', ('groups', 'dp'), None, 'ctx'), parts along dimension 1
- grad_head: bfloat16 [8192, 8192], P('groups', ('vocab', 'ctx', 'dp')), parts along dimension 0
- pair_loss: float32 [4], P('groups'), parts along dimension 0
The draws below stay inside these ranges and needn't reach their ends.
There are 2 independent parts, one for each index of `groups`. The reference program is written for one: setup_inputs(seed, part) draws one part's arguments, and reference() takes and returns one part's arrays. A program takes and returns all parts, laid end to end along the dimension named above; an argument that names none is the same for every part. Nothing has to cross between parts.
Inputs may be any that keep to these rules, and one draw needn't show every extreme that they name: `hidden`: entries of order one, a few of larger size. `head_weight`: entries of order 3 * 4096 ** -0.5.
All inputs are finite; a program needn't handle non-finite values.
Results may differ from the reference program's by a relative error of at most 0.0057.
Values may be sent and summed in bfloat16 or wider, within the bound.
No kernel may reach another device: no remote copies, remote signals or barrier semaphores. Data moves between devices by JAX's collectives and lax.ppermute only.
A program may use at most 128 MiB of HBM per device.

```python
import math
import jax
import jax.numpy as jnp
import numpy as np
from jax import lax

D = 4096
PAIRS = 2
SEQ = 128
VOCAB = 8192


def draw_hidden(key, part):
    key = jax.random.fold_in(key, 5)
    values = jnp.clip(jax.random.normal(key, (D, PAIRS, 2, SEQ), jnp.float32), -6.0, 6.0)
    return values.astype(jnp.bfloat16)


def draw_head_weight(key, part):
    key = jax.random.fold_in(key, 11)
    values = jnp.clip(jax.random.normal(key, (D, VOCAB), jnp.float32), -6.0, 6.0) * (3.0 / math.sqrt(D))
    return values.astype(jnp.bfloat16)


def touch_ends(drawn, rng, least, high):
    spot = [jax.random.randint(jax.random.fold_in(rng, axis), (), 0, length) for axis, length in enumerate(drawn.shape)]
    main_axis = drawn.shape.index(max(drawn.shape))
    beside = spot[:main_axis] + [(spot[main_axis] + 1) % drawn.shape[main_axis]] + spot[main_axis + 1:]
    return drawn.at[tuple(spot)].set(least).at[tuple(beside)].set(high)


def rank_bounds(count, slope):
    portions = [(1 << 20) // math.isqrt(grade ** slope) + 1 for grade in range(1, count + 1)]
    spread = 1 + sum(portions) // (1 << 30)
    return np.cumsum(np.array([max(1, weight // spread) for weight in portions]))


def skewed_ids(key, dims, count, skew):
    listing = rank_bounds(count, skew)
    ticket = jax.random.randint(jax.random.fold_in(key, 1), dims, 0, int(listing[count - 1]))
    standing = jnp.searchsorted(jnp.asarray(listing, jnp.int32), ticket, side="right")
    return jax.random.permutation(jax.random.fold_in(key, 2), count)[standing].astype(jnp.int32)


def centred(rng, shape, spread, reach, kind=jnp.bfloat16):
    result = spread * jax.random.normal(rng, shape, jnp.float32)
    return jnp.clip(result, min=-reach, max=reach).astype(kind)


def setup_inputs(seed: int = 0, part: int = 0) -> dict:
    key_list = jax.random.split(jax.random.key(seed), 8)
    part_splits = jax.random.split(jax.random.fold_in(key_list[7], part), 8)
    hidden = draw_hidden(jax.random.fold_in(jax.random.fold_in(key_list[7], part), 71), part)
    head_weight = draw_head_weight(jax.random.fold_in(key_list[7], 71), part)
    targets = touch_ends(skewed_ids(part_splits[2], (PAIRS, 2, SEQ), VOCAB, 1), jax.random.fold_in(part_splits[2], 3), 0, VOCAB - 1).astype(jnp.int32)
    response_start = jax.random.randint(part_splits[3], (PAIRS,), 0, SEQ // 2).astype(jnp.int32)
    other_sums = centred(part_splits[4], (PAIRS, 2), 3.0, 12.0, jnp.float32)
    ref_logp = centred(part_splits[5], (PAIRS, 2), 3.0, 12.0, jnp.float32)
    loss_cotangent = jnp.clip(jax.random.uniform(part_splits[6], (PAIRS,), jnp.float32, 130.0, 516.0), 130.0, 516.0)
    return {"hidden": hidden, "head_weight": head_weight, "targets": targets, "response_start": response_start, "other_sums": other_sums, "ref_logp": ref_logp, "loss_cotangent": loss_cotangent}


BETA = 0.1


def reference(hidden, head_weight, targets, response_start, other_sums, ref_logp, loss_cotangent):
    width = hidden.shape[0]
    pair_count = hidden.shape[1]
    side_count = hidden.shape[2]
    seq_len = hidden.shape[3]
    row_count = pair_count * side_count * seq_len
    flat_hidden = hidden.reshape(width, row_count)
    logits = jnp.dot(flat_hidden.T, head_weight, preferred_element_type=jnp.float32)
    row_max = jnp.max(logits, axis=1)
    shifted = jnp.exp(logits - row_max[:, None])
    sum_exp = jnp.sum(shifted, axis=1)
    column = lax.broadcasted_iota(jnp.int32, logits.shape, 1)
    hit = column == targets.reshape(row_count).astype(jnp.int32)[:, None]
    picked = jnp.sum(jnp.where(hit, logits, jnp.zeros_like(logits)), axis=1)
    token_logp = (picked - row_max - jnp.log(sum_exp)).reshape(pair_count, side_count, seq_len)
    position = lax.broadcasted_iota(jnp.int32, (pair_count, seq_len), 1)
    mask = (position >= response_start.astype(jnp.int32)[:, None]).astype(jnp.float32)[:, None, :]
    seq_logp = other_sums + jnp.sum(mask * token_logp, axis=2)
    ratios = seq_logp - ref_logp
    margin = BETA * (ratios[:, 0] - ratios[:, 1])
    pair_loss = jax.nn.softplus(-margin)
    factor = -BETA * jax.nn.sigmoid(-margin) * loss_cotangent
    side_sign = jnp.array([1.0, -1.0], dtype=jnp.float32)
    row_weight = (factor[:, None, None] * side_sign[None, :, None] * mask).reshape(row_count)
    grad_logits = (row_weight[:, None] * (hit.astype(jnp.float32) - shifted / sum_exp[:, None])).astype(jnp.bfloat16)
    grad_hidden = jnp.dot(head_weight, grad_logits.T, preferred_element_type=jnp.float32)
    grad_hidden = grad_hidden.astype(jnp.bfloat16).reshape(hidden.shape)
    grad_head = jnp.dot(flat_hidden, grad_logits, preferred_element_type=jnp.float32).astype(jnp.bfloat16)
    return (grad_hidden, grad_head, pair_loss)
```

```python
import jax
import jax.numpy as jnp
from jax import lax
from jax.sharding import PartitionSpec as P

BETA = 0.1


def ring(count, shift):
    return [(i, (i + shift) % count) for i in range(count)]


def shards(hidden, head_weight, targets, response_start, other_sums, ref_logp, loss_cotangent):
    f32, bf16 = jnp.float32, jnp.bfloat16
    n_voc, n_ctx, n_dp = lax.axis_size("vocab"), lax.axis_size("ctx"), lax.axis_size("dp")
    me_voc, me_ctx, me_dp = lax.axis_index("vocab"), lax.axis_index("ctx"), lax.axis_index("dp")
    part, pairs_here, sides, window = hidden.shape
    rows = pairs_here * sides * window
    width, columns = head_weight.shape
    seq_len = window * n_ctx

    weights = [head_weight]
    for t in range(1, n_dp):
        weights.append(lax.ppermute(head_weight, "dp", ring(n_dp, -t)))
    owners = [(me_dp + t) % n_dp for t in range(n_dp)]
    x = lax.all_gather(
        hidden.reshape(part, rows), ("ctx", "vocab"), axis=0, tiled=True
    ).reshape(n_ctx, width, rows)
    x_pairs = [x]
    for t in range(1, n_dp):
        x_pairs.append(lax.ppermute(x, "dp", ring(n_dp, -t)))

    mine = lambda a: lax.dynamic_slice_in_dim(a, me_dp * pairs_here, pairs_here, 0)
    by_block = lambda a: a.reshape(pairs_here, sides, n_ctx, window).transpose(2, 0, 1, 3).reshape(n_ctx, rows)
    target = by_block(mine(targets))

    logits, hits = [], []
    for w, owner in zip(weights, owners):
        part_logits = lax.dot_general(x, w, (((1,), (0,)), ((), ())), preferred_element_type=f32)
        first = ((me_voc * n_ctx + me_ctx) * n_dp + owner) * columns
        column = lax.broadcasted_iota(jnp.int32, part_logits.shape, 2) + first
        logits.append(part_logits)
        hits.append(column == target[:, :, None])
    top = logits[0].max(axis=2)
    for l in logits[1:]:
        top = jnp.maximum(top, l.max(axis=2))
    total = sum(jnp.exp(l - top[:, :, None]).sum(axis=2) for l in logits)
    picked = sum(jnp.where(h, l, jnp.zeros_like(l)).sum(axis=2) for h, l in zip(hits, logits))
    for axis, count in (("ctx", n_ctx), ("vocab", n_voc)):
        stats = jnp.stack([top, total, picked])
        seen = [stats] + [lax.ppermute(stats, axis, ring(count, s)) for s in range(1, count)]
        top = seen[0][0]
        for s in seen[1:]:
            top = jnp.maximum(top, s[0])
        total = sum(s[1] * jnp.exp(s[0] - top) for s in seen)
        picked = sum(s[2] for s in seen)

    token_logp = (picked - top - jnp.log(total)).reshape(n_ctx, pairs_here, sides, window)
    position = (
        lax.broadcasted_iota(jnp.int32, (n_ctx, pairs_here, 1, window), 0) * window
        + lax.broadcasted_iota(jnp.int32, (n_ctx, pairs_here, 1, window), 3)
    )
    mask = (position >= mine(response_start)[None, :, None, None]).astype(f32)
    seq_logp = mine(other_sums) + jnp.sum(mask * token_logp, axis=(0, 3))
    ratios = seq_logp - mine(ref_logp)
    margin = BETA * (ratios[:, 0] - ratios[:, 1])
    loss_here = jax.nn.softplus(-margin)
    factor = -BETA * jax.nn.sigmoid(-margin) * mine(loss_cotangent)
    side_sign = jnp.array([1.0, -1.0], dtype=f32)
    row_weight = (factor[None, :, None, None] * side_sign[None, None, :, None] * mask).reshape(n_ctx, rows)
    grads = [
        (row_weight[:, :, None] * (h.astype(f32) - jnp.exp(l - top[:, :, None]) / total[:, :, None])).astype(bf16)
        for h, l in zip(hits, logits)
    ]

    summed = None
    for s in list(range(1, n_voc)) + [0]:
        start = ((me_voc + s) % n_voc) * part
        here = sum(
            lax.dot_general(
                lax.dynamic_slice_in_dim(w, start, part, 0), g, (((1,), (2,)), ((), ())), preferred_element_type=f32
            )
            for w, g in zip(weights, grads)
        )
        block = lambda t: lax.dynamic_index_in_dim(here, (me_ctx + t) % n_ctx, 1, keepdims=False)
        kept = block(0)
        for t in range(1, n_ctx):
            kept = kept + lax.ppermute(block(t).astype(bf16), "ctx", ring(n_ctx, t)).astype(f32)
        if s:
            kept = lax.ppermute(kept.astype(bf16), "vocab", ring(n_voc, s)).astype(f32)
        summed = kept if summed is None else summed + kept
    grad_hidden = summed.astype(bf16).reshape(hidden.shape)

    grad_head = lax.dot_general(x, grads[0], (((0, 2), (0, 1)), ((), ())), preferred_element_type=f32)
    losses = [loss_here]
    for t in range(1, n_dp):
        theirs = lax.ppermute(grads[t], "dp", ring(n_dp, t))
        xt = x_pairs[n_dp - t]
        grad_head = grad_head + lax.dot_general(
            xt, theirs, (((0, 2), (0, 1)), ((), ())), preferred_element_type=f32
        )
        losses.append(lax.ppermute(loss_here, "dp", ring(n_dp, t)))
    pair_loss = jnp.zeros((n_dp, pairs_here), f32)
    for t, loss in enumerate(losses):
        owner = (me_dp - t) % n_dp
        pair_loss = jnp.where(
            lax.broadcasted_iota(jnp.int32, (n_dp, 1), 0) == owner, loss[None, :], pair_loss
        )
    return (grad_hidden, grad_head.astype(bf16), pair_loss.reshape(n_dp * pairs_here))


def solution(mesh):
    placed = (
        P("vocab", ("groups", "dp"), None, "ctx"),
        P(None, ("vocab", "ctx", "dp")),
        P("groups", None, None),
        P("groups"),
        P("groups", None),
        P("groups", None),
        P("groups"),
    )
    return jax.shard_map(
        shards,
        mesh=mesh,
        in_specs=placed,
        out_specs=(
            P("vocab", ("groups", "dp"), None, "ctx"),
            P("groups", ("vocab", "ctx", "dp")),
            P("groups"),
        ),
        check_vma=False,
    )
```

```python
import functools

import jax
import jax.numpy as jnp
from jax import lax
from jax.experimental import pallas as pl
from jax.experimental.pallas import tpu as pltpu
from jax.sharding import PartitionSpec as P

BETA = 0.1
F32, BF16 = jnp.float32, jnp.bfloat16
VMEM_BYTES = 32 * 1024 * 1024


def ring(count, shift):
    return [(i, (i + shift) % count) for i in range(count)]


def whole(shape):
    return pl.BlockSpec(shape, lambda *_: (0,) * len(shape))


def params():
    return pltpu.CompilerParams(vmem_limit_bytes=VMEM_BYTES)


def cost(flops, moved):
    return pl.CostEstimate(flops=int(flops), bytes_accessed=int(moved), transcendentals=0)


def size_of(*arrays):
    return sum(a.size * a.dtype.itemsize for a in arrays)


def logits_kernel(steps, has_acc, with_stats, columns, meta, *refs):
    count = sum(len(s) for s in steps)
    chunks, refs = refs[:count], refs[count:]
    w_own, w_far = refs[:2]
    refs = refs[2:]
    acc = None
    if has_acc:
        acc, refs = refs[0], refs[1:]
    if with_stats:
        target, refs = refs[0], refs[1:]
    out = refs[0]
    step = pl.program_id(0)

    @pl.when(step == 0)
    def _():
        if has_acc:
            out[...] = acc[...]
        else:
            out[...] = jnp.zeros_like(out)

    first_chunk = 0
    for i, blocks in enumerate(steps):
        here = [(t, chunks[first_chunk + j]) for j, t in enumerate(blocks)]
        first_chunk += len(blocks)

        @pl.when(step == i)
        def _():
            for t, chunk in here:
                x = chunk[...]
                out[t, :, :columns] += jnp.dot(x, w_own[...], preferred_element_type=F32)
                out[t, :, columns:] += jnp.dot(x, w_far[...], preferred_element_type=F32)

    if with_stats:
        stats = refs[1]

        @pl.when(step == len(steps) - 1)
        def _():
            n_blocks, rows, _ = out.shape
            for t in range(n_blocks):
                own, far = out[t, :, :columns], out[t, :, columns:]
                top = jnp.max(jnp.maximum(own, far), axis=1, keepdims=True)
                total = jnp.sum(jnp.exp(own - top) + jnp.exp(far - top), axis=1, keepdims=True)
                column = lax.broadcasted_iota(jnp.int32, own.shape, 1)
                wanted = target[t * rows:(t + 1) * rows, :]
                zero = jnp.zeros_like(own)
                picked = jnp.sum(
                    jnp.where(column + meta[len(steps)] == wanted, own, zero)
                    + jnp.where(column + meta[len(steps) + 1] == wanted, far, zero),
                    axis=1,
                    keepdims=True,
                )
                lane = lax.broadcasted_iota(jnp.int32, (rows, 128), 1)
                packed = jnp.where(lane == 0, top, jnp.where(lane == 1, total, picked))
                stats[:, t * rows:(t + 1) * rows] = packed.T[:8, :]


def logits_call(steps, chunks, k_ids, weights, acc, target, firsts, part, columns):
    n_blocks = max(max(s) for s in steps) + 1 if acc is None else acc.shape[0]
    rows = chunks[0].shape[0]
    meta = jnp.stack(list(k_ids) + list(firsts)).astype(jnp.int32)
    with_stats = target is not None
    out_shape = [jax.ShapeDtypeStruct((n_blocks, rows, 2 * columns), F32)]
    if with_stats:
        out_shape.append(jax.ShapeDtypeStruct((8, n_blocks * rows), F32))
    operands = list(chunks) + list(weights)
    specs = [whole(c.shape) for c in chunks]
    specs += [pl.BlockSpec((part, columns), lambda i, meta: (meta[i], 0))] * 2
    if acc is not None:
        operands.append(acc)
        specs.append(whole(acc.shape))
    if with_stats:
        operands.append(target)
        specs.append(whole(target.shape))
    return pl.pallas_call(
        functools.partial(logits_kernel, steps, acc is not None, with_stats, columns),
        out_shape=out_shape,
        grid_spec=pltpu.PrefetchScalarGridSpec(
            num_scalar_prefetch=1,
            grid=(len(steps),),
            in_specs=specs,
            out_specs=[whole(s.shape) for s in out_shape],
        ),
        compiler_params=params(),
        cost_estimate=cost(
            2 * len(chunks) * rows * part * 2 * columns,
            size_of(*chunks) + len(steps) * 4 * part * columns + n_blocks * rows * columns * 16,
        ),
    )(meta, *operands)


def spread(grads_own, grads_far, w_own, w_far, send, kept):
    n_blocks, rows, columns = grads_own.shape
    flat = (n_blocks * rows, columns)
    over = (((1,), (1,)), ((), ()))
    here = lax.dot_general(grads_own[...].reshape(flat), w_own[...], over, preferred_element_type=F32)
    here += lax.dot_general(grads_far[...].reshape(flat), w_far[...], over, preferred_element_type=F32)
    kept[...] = here[:rows]
    for t in range(1, n_blocks):
        send[t - 1] = here[t * rows:(t + 1) * rows].astype(BF16)


def grads_kernel(n_stats, columns, meta, logits, target, info, scalars, *refs):
    stats, refs = refs[:n_stats], refs[n_stats:]
    w_own, w_far, grads_own, grads_far, send, kept, loss = refs
    n_blocks, rows, _ = logits.shape
    top = stats[0][0:1, :]
    for s in stats[1:]:
        top = jnp.maximum(top, s[0:1, :])
    total = jnp.zeros_like(top)
    picked = jnp.zeros_like(top)
    for s in stats:
        total += s[1:2, :] * jnp.exp(s[0:1, :] - top)
        picked += s[2:3, :]
    signed_mask = info[0:1, :]
    token_logp = picked - top - jnp.log(total)
    margin = BETA * (jnp.sum(signed_mask * token_logp, axis=1, keepdims=True) + scalars[0:1, :])
    loss[...] = jnp.maximum(-margin, 0.0) + jnp.log1p(jnp.exp(-jnp.abs(margin)))
    factor = -BETA * (1.0 / (1.0 + jnp.exp(margin))) * scalars[1:2, :]
    weight = factor[:, 0:1] * signed_mask
    lines = lax.broadcasted_iota(jnp.int32, (128, top.shape[1]), 0)
    packed = jnp.where(lines == 0, top, jnp.where(lines == 1, weight, 1.0 / total)).T
    for t in range(n_blocks):
        at = slice(t * rows, (t + 1) * rows)
        top_t, weight_t, inverse_t = packed[at, 0:1], packed[at, 1:2], packed[at, 2:3]
        wanted = target[at, :]
        for j, grads in enumerate((grads_own, grads_far)):
            l = logits[t, :, j * columns:(j + 1) * columns]
            column = lax.broadcasted_iota(jnp.int32, l.shape, 1) + meta[1 + j]
            hit = jnp.where(column == wanted, 1.0, 0.0)
            grads[t] = (weight_t * (hit - jnp.exp(l - top_t) * inverse_t)).astype(BF16)
    spread(grads_own, grads_far, w_own, w_far, send, kept)


def spread_kernel(meta, grads_own, grads_far, w_own, w_far, send, kept):
    spread(grads_own, grads_far, w_own, w_far, send, kept)


def spread_shapes(n_blocks, rows, part):
    return [
        jax.ShapeDtypeStruct((n_blocks - 1, rows, part), BF16),
        jax.ShapeDtypeStruct((rows, part), F32),
    ]


def grads_call(logits, target, info, scalars, stats, weights, k_id, firsts, part, columns):
    n_blocks, rows, _ = logits.shape
    meta = jnp.stack([k_id] + list(firsts)).astype(jnp.int32)
    grads = jax.ShapeDtypeStruct((n_blocks, rows, columns), BF16)
    out_shape = [grads, grads] + spread_shapes(n_blocks, rows, part) + [jax.ShapeDtypeStruct((1, 128), F32)]
    small = [logits, target, info, scalars] + list(stats)
    return pl.pallas_call(
        functools.partial(grads_kernel, len(stats), columns),
        out_shape=out_shape,
        grid_spec=pltpu.PrefetchScalarGridSpec(
            num_scalar_prefetch=1,
            grid=(1,),
            in_specs=[whole(a.shape) for a in small]
            + [pl.BlockSpec((part, columns), lambda i, meta: (meta[0], 0))] * 2,
            out_specs=[whole(s.shape) for s in out_shape],
        ),
        compiler_params=params(),
        cost_estimate=cost(4 * n_blocks * rows * part * columns, size_of(logits) + 4 * part * columns),
    )(meta, *small, *weights)


def spread_call(grads_own, grads_far, weights, k_id, part, columns):
    n_blocks, rows, _ = grads_own.shape
    out_shape = spread_shapes(n_blocks, rows, part)
    return pl.pallas_call(
        spread_kernel,
        out_shape=out_shape,
        grid_spec=pltpu.PrefetchScalarGridSpec(
            num_scalar_prefetch=1,
            grid=(1,),
            in_specs=[whole(grads_own.shape)] * 2
            + [pl.BlockSpec((part, columns), lambda i, meta: (meta[0], 0))] * 2,
            out_specs=[whole(s.shape) for s in out_shape],
        ),
        compiler_params=params(),
        cost_estimate=cost(4 * n_blocks * rows * part * columns, 4 * part * columns),
    )(k_id.reshape(1).astype(jnp.int32), grads_own, grads_far, *weights)


def head_kernel(n_pairs, meta, *refs):
    xs, grads, out = refs[:n_pairs], refs[n_pairs:2 * n_pairs], refs[2 * n_pairs]
    total = None
    for x, g in zip(xs, grads):
        n_blocks, rows, columns = g.shape
        product = lax.dot_general(
            x[...].reshape(n_blocks * rows, x.shape[3]),
            g[...].reshape(n_blocks * rows, columns),
            (((0,), (0,)), ((), ())),
            preferred_element_type=F32,
        )
        total = product if total is None else total + product
    out[...] = total.astype(BF16)


def head_call(xs, grads, k_ids):
    n_blocks, n_parts, rows, part = xs[0].shape
    columns = grads[0].shape[2]
    return pl.pallas_call(
        functools.partial(head_kernel, len(xs)),
        out_shape=jax.ShapeDtypeStruct((n_parts * part, columns), BF16),
        grid_spec=pltpu.PrefetchScalarGridSpec(
            num_scalar_prefetch=1,
            grid=(n_parts,),
            in_specs=[pl.BlockSpec((n_blocks, 1, rows, part), lambda i, meta: (0, i, 0, 0))] * len(xs)
            + [whole(g.shape) for g in grads],
            out_specs=pl.BlockSpec((part, columns), lambda i, meta: (meta[i], 0)),
        ),
        compiler_params=params(),
        cost_estimate=cost(
            2 * len(xs) * n_blocks * rows * n_parts * part * columns,
            size_of(*xs, *grads) + 2 * n_parts * part * columns,
        ),
    )(jnp.stack(k_ids).astype(jnp.int32), *xs, *grads)


def shards(hidden, head_weight, targets, response_start, other_sums, ref_logp, loss_cotangent):
    n_voc, n_ctx, n_dp = lax.axis_size("vocab"), lax.axis_size("ctx"), lax.axis_size("dp")
    me_voc, me_ctx, me_dp = lax.axis_index("vocab"), lax.axis_index("ctx"), lax.axis_index("dp")
    part, _, sides, window = hidden.shape
    rows = sides * window
    columns = head_weight.shape[1]

    weights = (head_weight, lax.ppermute(head_weight, "dp", ring(n_dp, 1)))
    firsts = [
        ((me_voc * n_ctx + me_ctx) * n_dp + owner) * columns for owner in (me_dp, (me_dp + 1) % n_dp)
    ]
    part_of = [(me_voc - s) % n_voc for s in range(n_voc)]

    own = hidden.transpose(1, 2, 3, 0).reshape(rows, part)
    order = [0]
    for s in range(1, n_voc // 2 + 1):
        order += [s] if 2 * s == n_voc else [s, n_voc - s]
    chunk = {(0, 0): own}
    for t in range(1, n_ctx):
        chunk[t, 0] = lax.ppermute(own, "ctx", ring(n_ctx, t))
    source = own
    for i, s in enumerate(order[1:]):
        chunk[0, s] = lax.ppermute(source, "vocab", ring(n_voc, s))
        if i % 2:
            held = lax.optimization_barrier((source, chunk[0, order[i]], chunk[0, s]))
            source, chunk[0, order[i]], chunk[0, s] = held
    for s in order[1:]:
        for t in range(1, n_ctx):
            chunk[t, s] = lax.ppermute(chunk[0, s], "ctx", ring(n_ctx, t))

    blocks_of = [(me_ctx - t) % n_ctx for t in range(n_ctx)]
    by_block = lambda a: jnp.concatenate(
        [lax.dynamic_slice_in_dim(a, b * window, window, 1).reshape(rows) for b in blocks_of]
    )
    mine = lambda a: lax.dynamic_index_in_dim(a, me_dp, 0, keepdims=False)
    target = by_block(mine(targets))[:, None]
    position = lax.broadcasted_iota(jnp.int32, (sides, window * n_ctx), 1)
    side_sign = jnp.array([1.0, -1.0], dtype=F32)[:, None]
    signed_mask = jnp.where(position >= mine(response_start), side_sign, 0.0)
    info = jnp.broadcast_to(by_block(signed_mask)[None, :], (8, n_ctx * rows))
    ratio = mine(other_sums) - mine(ref_logp)
    scalars = jnp.stack([ratio[0] - ratio[1], mine(loss_cotangent)])
    scalars = jnp.broadcast_to(jnp.pad(scalars, (0, 6))[:, None], (8, 128))

    call = functools.partial(logits_call, part=part, columns=columns)
    early = order[:3]
    last = order[-1]
    everything = list(range(n_ctx))
    first_steps = [everything] + [[0] for _ in early[1:]]
    logits, = call(
        first_steps,
        [chunk[t, s] for s, ts in zip(early, first_steps) for t in ts],
        [part_of[s] for s in early],
        weights, None, None, firsts,
    )
    middle_steps = [everything[1:] for _ in early[1:]] + [everything for _ in order[3:-1]] + [[0]]
    logits, = call(
        middle_steps,
        [chunk[t, s] for s, ts in zip(order[1:], middle_steps) for t in ts],
        [part_of[s] for s in order[1:]],
        weights, logits, None, firsts,
    )
    logits, stats = call(
        [everything[1:]],
        [chunk[t, last] for t in everything[1:]],
        [part_of[last]],
        weights, logits, target, firsts,
    )

    others = [lax.ppermute(stats, "ctx", ring(n_ctx, t)) for t in range(1, n_ctx)]
    top = stats[0]
    for o in others:
        top = jnp.maximum(top, o[0])
    def turn(o, t):
        return jnp.roll(o.reshape(8, n_ctx, rows), t, axis=1).reshape(8, n_ctx * rows)
    others = [turn(o, t) for t, o in enumerate(others, 1)]
    top = stats[0]
    for o in others:
        top = jnp.maximum(top, o[0])
    total = sum(o[1] * jnp.exp(o[0] - top) for o in [stats] + others)
    picked = sum(o[2] for o in [stats] + others)
    stats = jnp.pad(jnp.stack([top, total, picked]), ((0, 5), (0, 0)))
    all_stats = [stats] + [lax.ppermute(stats, "vocab", ring(n_voc, s)) for s in range(1, n_voc)]

    goes_to = [(me_voc + s) % n_voc for s in range(n_voc)]
    leave = order[::-1]
    grads_own, grads_far, send, kept, loss = grads_call(
        logits, target, info, scalars, all_stats, weights, goes_to[leave[0]], firsts, part, columns
    )
    theirs = lax.ppermute(grads_far, "dp", ring(n_dp, 1))
    summed = None
    for i, s in enumerate(leave):
        if i:
            send, kept = spread_call(grads_own, grads_far, weights, goes_to[s], part, columns)
        for t in range(1, n_ctx):
            kept = kept + lax.ppermute(send[t - 1], "ctx", ring(n_ctx, -t)).astype(F32)
        if s:
            kept = lax.ppermute(kept.astype(BF16), "vocab", ring(n_voc, s)).astype(F32)
        summed = kept if summed is None else summed + kept
    grad_hidden = summed.astype(BF16).reshape(1, sides, window, part).transpose(3, 0, 1, 2)

    stacked = jnp.stack([jnp.stack([chunk[t, s] for s in range(n_voc)]) for t in range(n_ctx)])
    far_stacked = lax.ppermute(stacked, "dp", ring(n_dp, 1))
    grad_head = head_call([stacked, far_stacked], [grads_own, theirs], part_of)

    far_loss = lax.ppermute(loss, "dp", ring(n_dp, 1))
    pair = lax.broadcasted_iota(jnp.int32, (n_dp,), 0)
    pair_loss = jnp.where(pair == me_dp, loss[0, :n_dp], far_loss[0, :n_dp])
    return (grad_hidden, grad_head, pair_loss)


def solution(mesh):
    placed = (
        P("vocab", ("groups", "dp"), None, "ctx"),
        P(None, ("vocab", "ctx", "dp")),
        P("groups", None, None),
        P("groups"),
        P("groups", None),
        P("groups", None),
        P("groups"),
    )
    return jax.shard_map(
        shards,
        mesh=mesh,
        in_specs=placed,
        out_specs=(
            P("vocab", ("groups", "dp"), None, "ctx"),
            P("groups", ("vocab", "ctx", "dp")),
            P("groups"),
        ),
        check_vma=False,
    )
```

```python
import functools

import jax
import jax.numpy as jnp
from jax import lax
from jax.experimental import pallas as pl
from jax.experimental.pallas import tpu as pltpu
from jax.sharding import PartitionSpec as P

BETA = 0.1
F32, BF16 = jnp.float32, jnp.bfloat16
VMEM_BYTES = 16 * 1024 * 1024
IN_VMEM = pl.BlockSpec(memory_space=pltpu.VMEM)
IN_SMEM = pl.BlockSpec(memory_space=pltpu.SMEM)


def ring(count, shift):
    return [(i, (i + shift) % count) for i in range(count)]


def params():
    return pltpu.CompilerParams(vmem_limit_bytes=VMEM_BYTES)


def cost(flops, moved):
    return pl.CostEstimate(flops=int(flops), bytes_accessed=int(moved), transcendentals=0)


def shape_of(shape, kind):
    return jax.ShapeDtypeStruct(shape, kind)


def row_stats(own, far, wanted, first_own, first_far):
    top = jnp.max(jnp.maximum(own, far), axis=1, keepdims=True)
    total = jnp.sum(jnp.exp(own - top) + jnp.exp(far - top), axis=1, keepdims=True)
    column = lax.broadcasted_iota(jnp.int32, own.shape, 1)
    zero = jnp.zeros_like(own)
    picked = jnp.sum(
        jnp.where(column + first_own == wanted, own, zero) + jnp.where(column + first_far == wanted, far, zero),
        axis=1,
        keepdims=True,
    )
    lane = lax.broadcasted_iota(jnp.int32, (own.shape[0], 128), 1)
    return jnp.where(lane == 0, top, jnp.where(lane == 1, total, picked)).T[:8, :]


def logits_kernel(plan, columns, part, meta, w_own, w_far, *refs):
    refs = list(refs)
    chunks = {(t, i): refs.pop(0) for t, slots, _, _ in plan for i in range(len(slots))}
    accs = {t: refs.pop(0) for t, _, has_acc, _ in plan if has_acc}
    wanted = {t: refs.pop(0) for t, _, _, done in plan if done}
    for t, slots, has_acc, done in plan:
        out = refs.pop(0)
        halves = []
        for j, w in enumerate((w_own, w_far)):
            at = slice(j * columns, (j + 1) * columns)
            total = accs[t][:, at] if has_acc else None
            for i, slot in enumerate(slots):
                start = pl.multiple_of(meta[slot] * part, part)
                product = jnp.dot(chunks[t, i][...], w[pl.ds(start, part), :], preferred_element_type=F32)
                total = product if total is None else total + product
            out[:, at] = total
            halves.append(total)
        if done:
            stats = refs.pop(0)
            stats[...] = row_stats(halves[0], halves[1], wanted[t][...], meta[-2 + meta.shape[0]], meta[-1 + meta.shape[0]])


def logits_call(plan, meta, weights, part):
    columns = weights[0].shape[1]
    chunks = [c for _, slots, _, _ in plan for _, c in slots]
    accs = [acc for _, _, acc, _ in plan if acc is not None]
    wanted = [w for _, _, _, w in plan if w is not None]
    rows = chunks[0].shape[0]
    out_shape = []
    for _, _, _, w in plan:
        out_shape.append(shape_of((rows, 2 * columns), F32))
        if w is not None:
            out_shape.append(shape_of((8, rows), F32))
    kernel_plan = [(t, [slot for slot, _ in slots], acc is not None, w is not None) for t, slots, acc, w in plan]
    operands = list(weights) + chunks + accs + wanted
    return pl.pallas_call(
        functools.partial(logits_kernel, kernel_plan, columns, part),
        out_shape=out_shape,
        in_specs=[IN_SMEM] + [IN_VMEM] * len(operands),
        out_specs=[IN_VMEM] * len(out_shape),
        compiler_params=params(),
        cost_estimate=cost(4 * len(chunks) * rows * part * columns, len(chunks) * (2 * rows * part + 4 * part * columns)),
    )(meta, *operands)


def spread(start, part, grads_own, grads_far, w_own, w_far, send, kept):
    n_blocks, rows, columns = grads_own.shape
    flat = (n_blocks * rows, columns)
    over = (((1,), (1,)), ((), ()))
    here = lax.dot_general(
        grads_own[...].reshape(flat), w_own[pl.ds(start, part), :], over, preferred_element_type=F32
    )
    here += lax.dot_general(
        grads_far[...].reshape(flat), w_far[pl.ds(start, part), :], over, preferred_element_type=F32
    )
    kept[...] = here[:rows]
    for t in range(1, n_blocks):
        send[t - 1][...] = here[t * rows:(t + 1) * rows].astype(BF16)


def grads_kernel(n_blocks, n_stats, columns, part, meta, *refs):
    refs = list(refs)
    logits = [refs.pop(0) for _ in range(n_blocks)]
    target, info, scalars = refs.pop(0), refs.pop(0), refs.pop(0)
    stats = [refs.pop(0) for _ in range(n_stats)]
    w_own, w_far, grads_own, grads_far, loss, kept = refs[:6]
    send = refs[6:]
    rows = logits[0].shape[0]
    top = stats[0][0:1, :]
    for s in stats[1:]:
        top = jnp.maximum(top, s[0:1, :])
    total = jnp.zeros_like(top)
    picked = jnp.zeros_like(top)
    for s in stats:
        total += s[1:2, :] * jnp.exp(s[0:1, :] - top)
        picked += s[2:3, :]
    signed_mask = info[0:1, :]
    token_logp = picked - top - jnp.log(total)
    margin = BETA * (jnp.sum(signed_mask * token_logp, axis=1, keepdims=True) + scalars[0:1, :])
    loss[...] = jnp.maximum(-margin, 0.0) + jnp.log1p(jnp.exp(-jnp.abs(margin)))
    factor = -BETA * (1.0 / (1.0 + jnp.exp(margin))) * scalars[1:2, :]
    weight = factor[:, 0:1] * signed_mask
    lines = lax.broadcasted_iota(jnp.int32, (128, top.shape[1]), 0)
    packed = jnp.where(lines == 0, top, jnp.where(lines == 1, weight, 1.0 / total)).T
    for t in range(n_blocks):
        at = slice(t * rows, (t + 1) * rows)
        top_t, weight_t, inverse_t = packed[at, 0:1], packed[at, 1:2], packed[at, 2:3]
        wanted = target[at, :]
        for j, grads in enumerate((grads_own, grads_far)):
            l = logits[t][:, j * columns:(j + 1) * columns]
            column = lax.broadcasted_iota(jnp.int32, l.shape, 1) + meta[1 + j]
            hit = jnp.where(column == wanted, 1.0, 0.0)
            grads[t] = (weight_t * (hit - jnp.exp(l - top_t) * inverse_t)).astype(BF16)
    start = pl.multiple_of(meta[0] * part, part)
    spread(start, part, grads_own, grads_far, w_own, w_far, send, kept)


def spread_kernel(part, meta, grads_own, grads_far, w_own, w_far, kept, *send):
    start = pl.multiple_of(meta[0] * part, part)
    spread(start, part, grads_own, grads_far, w_own, w_far, send, kept)


def spread_shapes(n_blocks, rows, part):
    return [shape_of((rows, part), F32)] + [shape_of((rows, part), BF16)] * (n_blocks - 1)


def grads_call(logits, target, info, scalars, stats, weights, k_id, firsts, part):
    n_blocks, rows, columns = len(logits), logits[0].shape[0], weights[0].shape[1]
    meta = jnp.stack([k_id] + list(firsts)).astype(jnp.int32)
    grads = shape_of((n_blocks, rows, columns), BF16)
    out_shape = [grads, grads, shape_of((1, 128), F32)] + spread_shapes(n_blocks, rows, part)
    operands = list(logits) + [target, info, scalars] + list(stats) + list(weights)
    return pl.pallas_call(
        functools.partial(grads_kernel, n_blocks, len(stats), columns, part),
        out_shape=out_shape,
        in_specs=[IN_SMEM] + [IN_VMEM] * len(operands),
        out_specs=[IN_VMEM] * len(out_shape),
        compiler_params=params(),
        cost_estimate=cost(4 * n_blocks * rows * part * columns, 8 * part * columns),
    )(meta, *operands)


def spread_call(grads_own, grads_far, weights, k_id, part):
    n_blocks, rows, columns = grads_own.shape
    out_shape = spread_shapes(n_blocks, rows, part)
    return pl.pallas_call(
        functools.partial(spread_kernel, part),
        out_shape=out_shape,
        in_specs=[IN_SMEM] + [IN_VMEM] * 4,
        out_specs=[IN_VMEM] * len(out_shape),
        compiler_params=params(),
        cost_estimate=cost(4 * n_blocks * rows * part * columns, 4 * part * columns),
    )(k_id.reshape(1).astype(jnp.int32), grads_own, grads_far, *weights)


def head_kernel(near_keys, far_keys, n_parts, part, meta, *refs):
    refs = list(refs)
    grads = [refs.pop(0), refs.pop(0)]
    near = {k: refs.pop(0) for k in near_keys}
    stacks = [refs.pop(0) for _ in far_keys]
    far = {k: stack.at[i] for stack, keys in zip(stacks, far_keys) for i, k in enumerate(keys)}
    out, slots, sems = refs
    n_blocks, rows, columns = grads[0].shape
    right = jnp.concatenate([g[...].reshape(n_blocks * rows, columns) for g in grads])
    copies = []
    for i in range(n_parts):
        left = jnp.concatenate([x[t, i][...] for x in (near, far) for t in range(n_blocks)])
        product = lax.dot_general(left, right, (((0,), (0,)), ((), ())), preferred_element_type=F32)
        if i >= 2:
            copies[i - 2].wait()
        slots[i % 2] = product.astype(BF16)
        start = pl.multiple_of(meta[i] * part, part)
        copies.append(pltpu.make_async_copy(slots.at[i % 2], out.at[pl.ds(start, part), :], sems.at[i % 2]))
        copies[-1].start()
    for copy in copies[-2:]:
        copy.wait()


def head_call(near, far, grads, meta):
    n_blocks, rows, columns = grads[0].shape
    n_parts = len(near) // n_blocks
    part = near[0, 0].shape[1]
    operands = list(grads) + list(near.values()) + [stack for _, stack in far]
    return pl.pallas_call(
        functools.partial(head_kernel, list(near), [keys for keys, _ in far], n_parts, part),
        out_shape=shape_of((n_parts * part, columns), BF16),
        in_specs=[IN_SMEM] + [IN_VMEM] * len(operands),
        out_specs=pl.BlockSpec(memory_space=pl.ANY),
        scratch_shapes=[pltpu.VMEM((2, part, columns), BF16), pltpu.SemaphoreType.DMA((2,))],
        compiler_params=params(),
        cost_estimate=cost(
            4 * n_blocks * rows * n_parts * part * columns,
            4 * n_blocks * n_parts * rows * part + 2 * n_parts * part * columns,
        ),
    )(meta, *operands)


def shards(hidden, head_weight, targets, response_start, other_sums, ref_logp, loss_cotangent):
    n_voc, n_ctx, n_dp = lax.axis_size("vocab"), lax.axis_size("ctx"), lax.axis_size("dp")
    me_voc, me_ctx, me_dp = lax.axis_index("vocab"), lax.axis_index("ctx"), lax.axis_index("dp")
    part, _, sides, window = hidden.shape
    rows = sides * window
    columns = head_weight.shape[1]

    weights = (head_weight, lax.ppermute(head_weight, "dp", ring(n_dp, 1)))
    firsts = [
        ((me_voc * n_ctx + me_ctx) * n_dp + owner) * columns for owner in (me_dp, (me_dp + 1) % n_dp)
    ]
    part_of = [(me_voc - s) % n_voc for s in range(n_voc)]
    meta = jnp.stack(part_of + firsts).astype(jnp.int32)

    blocks_of = [(me_ctx - t) % n_ctx for t in range(n_ctx)]
    block = lambda a, b: lax.dynamic_slice_in_dim(a, b * window, window, 1).reshape(rows)
    mine = lambda a: lax.dynamic_index_in_dim(a, me_dp, 0, keepdims=False)
    wanted = [block(mine(targets), b)[:, None] for b in blocks_of]
    target = jnp.concatenate(wanted)
    position = lax.broadcasted_iota(jnp.int32, (sides, window * n_ctx), 1)
    side_sign = jnp.array([1.0, -1.0], dtype=F32)[:, None]
    signed_mask = jnp.where(position >= mine(response_start), side_sign, 0.0)
    info = jnp.concatenate([block(signed_mask, b) for b in blocks_of])
    info = jnp.broadcast_to(info[None, :], (8, n_ctx * rows))
    ratio = mine(other_sums) - mine(ref_logp)
    scalars = jnp.stack([ratio[0] - ratio[1], mine(loss_cotangent)])
    scalars = jnp.broadcast_to(jnp.pad(scalars, (0, 6))[:, None], (8, 128))

    own = hidden.transpose(1, 2, 3, 0).reshape(rows, part)
    order = [0]
    for s in range(1, n_voc // 2 + 1):
        order += [s] if 2 * s == n_voc else [s, n_voc - s]
    near, rest = order[1:3], order[3:]
    chunk = {(0, 0): own}
    for s in near:
        chunk[0, s] = lax.ppermute(own, "vocab", ring(n_voc, s))
    for t in range(1, n_ctx):
        chunk[t, 0] = lax.ppermute(own, "ctx", ring(n_ctx, t))
    held = lax.optimization_barrier([own] + [chunk[0, s] for s in near])
    for s, c in zip(near, held[1:]):
        chunk[0, s] = c
    for s in rest:
        chunk[0, s] = lax.ppermute(held[0], "vocab", ring(n_voc, s))
    for s in near:
        for t in range(1, n_ctx):
            chunk[t, s] = lax.ppermute(chunk[0, s], "ctx", ring(n_ctx, t))

    beyond = list(range(1, n_ctx))
    call = functools.partial(logits_call, meta=meta, weights=weights, part=part)
    logits = call(
        [(0, [(s, chunk[0, s]) for s in [0] + near], None, None)] + [(t, [(0, chunk[t, 0])], None, None) for t in beyond]
    )
    held = lax.optimization_barrier([chunk[0, s] for s in rest] + list(logits))
    for s, c in zip(rest, held):
        chunk[0, s] = c
    logits = held[len(rest):]
    for s in rest:
        for t in beyond:
            chunk[t, s] = lax.ppermute(chunk[0, s], "ctx", ring(n_ctx, t))
    done = call(
        [(0, [(s, chunk[0, s]) for s in rest], logits[0], wanted[0])]
        + [(t, [(s, chunk[t, s]) for s in near], logits[t], None) for t in beyond]
    )
    logits = [done[0]] + list(done[2:])
    stats = [done[1]]

    late = [(t, s) for t in beyond for s in rest]
    soon = [k for k in chunk if k not in late]
    far_soon = lax.ppermute(jnp.stack([chunk[k] for k in soon]), "dp", ring(n_dp, 1))
    done = call([(t, [(s, chunk[t, s]) for s in rest], logits[t], wanted[t]) for t in beyond])
    logits = [logits[0]] + list(done[0::2])
    stats = stats + list(done[1::2])

    others = [lax.ppermute(jnp.stack(stats), "ctx", ring(n_ctx, t)) for t in beyond]
    merged = []
    for b in range(n_ctx):
        seen = [stats[b]] + [o[(b - t) % n_ctx] for t, o in zip(beyond, others)]
        top = seen[0][0]
        for o in seen[1:]:
            top = jnp.maximum(top, o[0])
        total = sum(o[1] * jnp.exp(o[0] - top) for o in seen)
        picked = sum(o[2] for o in seen)
        merged.append(jnp.pad(jnp.stack([top, total, picked]), ((0, 5), (0, 0))))
    merged = jnp.concatenate(merged, axis=1)
    held = lax.optimization_barrier([merged] + [chunk[k] for k in late])
    merged = held[0]
    far_late = lax.ppermute(jnp.stack(held[1:]), "dp", ring(n_dp, 1))
    all_stats = [merged] + [lax.ppermute(merged, "vocab", ring(n_voc, s)) for s in range(1, n_voc)]

    goes_to = [(me_voc + s) % n_voc for s in range(n_voc)]
    leave = order[::-1]
    grads_own, grads_far, loss, kept, *send = grads_call(
        logits, target, info, scalars, all_stats, weights, goes_to[leave[0]], firsts, part
    )
    theirs = lax.ppermute(grads_far, "dp", ring(n_dp, 1))

    arrived, landed = [], []
    for i, s in enumerate(leave):
        if i:
            kept, *send = spread_call(grads_own, grads_far, weights, goes_to[s], part)
            held = lax.optimization_barrier(list(arrived) + list(send))
            arrived, send = held[:len(arrived)], held[len(arrived):]
            leaving = together(before, arrived).astype(BF16)
            leaving, *send = lax.optimization_barrier([leaving] + list(send))
            by = ring(n_voc, leave[i - 1])
            if i == 1:
                half = rows // 2
                landed = [lax.ppermute(leaving[:half], "vocab", by), lax.ppermute(leaving[half:], "vocab", by)]
            else:
                landed.append(lax.ppermute(leaving, "vocab", by))
            if i > 1:
                landed[i - 2], *send = lax.optimization_barrier([landed[i - 2]] + list(send))
        arrived = [lax.ppermute(c, "ctx", ring(n_ctx, -t)) for t, c in zip(beyond, send)]
        before = kept
    grad_head = head_call(chunk, [(soon, far_soon), (late, far_late)], [grads_own, theirs], meta)
    before, grad_head = lax.optimization_barrier((before, grad_head))
    landed = [jnp.concatenate(landed[:2])] + landed[2:]
    summed = together(before, arrived + landed)
    grad_hidden = summed.astype(BF16).reshape(1, sides, window, part).transpose(3, 0, 1, 2)

    far_loss = lax.ppermute(loss, "dp", ring(n_dp, 1))
    pair = lax.broadcasted_iota(jnp.int32, (n_dp,), 0)
    pair_loss = jnp.where(pair == me_dp, loss[0, :n_dp], far_loss[0, :n_dp])
    return (grad_hidden, grad_head, pair_loss)


def together(kept, arrived):
    for a in arrived:
        kept = kept + a.astype(F32)
    return kept


def solution(mesh):
    placed = (
        P("vocab", ("groups", "dp"), None, "ctx"),
        P(None, ("vocab", "ctx", "dp")),
        P("groups", None, None),
        P("groups"),
        P("groups", None),
        P("groups", None),
        P("groups"),
    )
    return jax.shard_map(
        shards,
        mesh=mesh,
        in_specs=placed,
        out_specs=(
            P("vocab", ("groups", "dp"), None, "ctx"),
            P("groups", ("vocab", "ctx", "dp")),
            P("groups"),
        ),
        check_vma=False,
    )
```

```python
import functools

import jax
import jax.numpy as jnp
from jax import lax
from jax.experimental import pallas as pl
from jax.experimental.pallas import tpu as pltpu
from jax.sharding import PartitionSpec as P

BETA = 0.1
F32, BF16 = jnp.float32, jnp.bfloat16
VMEM_BYTES = 16 * 1024 * 1024
IN_VMEM = pl.BlockSpec(memory_space=pltpu.VMEM)
IN_SMEM = pl.BlockSpec(memory_space=pltpu.SMEM)
IN_PLACE = pl.BlockSpec(memory_space=pl.ANY)
PAIRS_OUT = [(0, 1), (1, 0), (2, 3), (3, 2)]
PAIR_IN = [(1, 2), (2, 1)]
TO_ENDS = [(1, 0), (2, 3)]
FROM_ENDS = [(0, 1), (3, 2)]


def ring(count, shift):
    return [(i, (i + shift) % count) for i in range(count)]


def params():
    return pltpu.CompilerParams(vmem_limit_bytes=VMEM_BYTES)


def cost(flops, moved):
    return pl.CostEstimate(flops=int(flops), bytes_accessed=int(moved), transcendentals=0)


def shape_of(shape, kind):
    return jax.ShapeDtypeStruct(shape, kind)


def fetch(w_own, w_far, start, part, slots, i, sems):
    copies = []
    for j, w in enumerate((w_own, w_far)):
        copies.append(pltpu.make_async_copy(w.at[pl.ds(start, part), :], slots.at[i, j], sems.at[i, j]))
        copies[-1].start()
    return copies


def row_stats(own, far, wanted, first_own, first_far):
    top = jnp.max(jnp.maximum(own, far), axis=1, keepdims=True)
    total = jnp.sum(jnp.exp(own - top) + jnp.exp(far - top), axis=1, keepdims=True)
    column = lax.broadcasted_iota(jnp.int32, own.shape, 1)
    zero = jnp.zeros_like(own)
    picked = jnp.sum(
        jnp.where(column + first_own == wanted, own, zero) + jnp.where(column + first_far == wanted, far, zero),
        axis=1,
        keepdims=True,
    )
    lane = lax.broadcasted_iota(jnp.int32, (own.shape[0], 128), 1)
    return jnp.where(lane == 0, top, jnp.where(lane == 1, total, picked)).T[:8, :]


def logits_kernel(plan, columns, part, n_voc, meta, w_own, w_far, *refs):
    refs = list(refs)
    chunks = {(t, i): refs.pop(0) for t, parts, _, _ in plan for i in parts}
    accs = {t: refs.pop(0) for t, _, has_acc, _ in plan if has_acc}
    wanted = {t: refs.pop(0) for t, _, _, done in plan if done}
    slots, sems = refs[-2:]
    used = sorted({i for _, parts, _, _ in plan for i in parts})
    coming = [fetch(w_own, w_far, pl.multiple_of(meta[i] * part, part), part, slots, n, sems) for n, i in enumerate(used)]
    outs = {}
    stats = {}
    for t, _, _, done in plan:
        outs[t] = refs.pop(0)
        if done:
            stats[t] = refs.pop(0)
    for n, i in enumerate(used):
        for copy in coming[n]:
            copy.wait()
        for t, parts, has_acc, _ in plan:
            if i not in parts:
                continue
            x = chunks[t, i][...]
            for j in range(2):
                at = slice(j * columns, (j + 1) * columns)
                product = jnp.dot(x, slots[n, j], preferred_element_type=F32)
                if i != parts[0]:
                    product += outs[t][:, at]
                elif has_acc:
                    product += accs[t][:, at]
                outs[t][:, at] = product
    for t in stats:
        own, far = outs[t][:, :columns], outs[t][:, columns:]
        stats[t][...] = row_stats(own, far, wanted[t][...], meta[n_voc], meta[n_voc + 1])


def logits_call(plan, meta, weights, part, n_voc):
    columns = weights[0].shape[1]
    chunks = [c for _, parts, _, _ in plan for c in parts.values()]
    accs = [acc for _, _, acc, _ in plan if acc is not None]
    wanted = [w for _, _, _, w in plan if w is not None]
    rows = chunks[0].shape[0]
    out_shape = []
    for _, _, _, w in plan:
        out_shape.append(shape_of((rows, 2 * columns), F32))
        if w is not None:
            out_shape.append(shape_of((8, rows), F32))
    kernel_plan = [(t, sorted(parts), acc is not None, w is not None) for t, parts, acc, w in plan]
    chunks = [parts[i] for _, parts, _, _ in plan for i in sorted(parts)]
    n_used = len({i for _, parts, _, _ in plan for i in parts})
    operands = chunks + accs + wanted
    return pl.pallas_call(
        functools.partial(logits_kernel, kernel_plan, columns, part, n_voc),
        out_shape=out_shape,
        in_specs=[IN_SMEM, IN_PLACE, IN_PLACE] + [IN_VMEM] * len(operands),
        out_specs=[IN_VMEM] * len(out_shape),
        scratch_shapes=[pltpu.VMEM((n_used, 2, part, columns), BF16), pltpu.SemaphoreType.DMA((n_used, 2))],
        compiler_params=params(),
        cost_estimate=cost(4 * len(chunks) * rows * part * columns, n_used * 4 * part * columns),
    )(meta, *weights, *operands)


def spread(flipped_own, flipped_far, w_own, w_far, kept, send):
    rows = kept.shape[1]
    here = jnp.dot(w_own, flipped_own, preferred_element_type=F32)
    here += jnp.dot(w_far, flipped_far, preferred_element_type=F32)
    kept[...] = here[:, :rows]
    for t, out in enumerate(send, 1):
        out[...] = here[:, t * rows:(t + 1) * rows].astype(BF16)


def grads_kernel(n_blocks, n_stats, columns, part, window, meta, start, sums, refer, cotangent, w_own, w_far, *refs):
    refs = list(refs)
    logits = [refs.pop(0) for _ in range(n_blocks)]
    target = refs.pop(0)
    stats = [refs.pop(0) for _ in range(n_stats)]
    slots, sems = refs[-2:]
    grads_own, grads_far, flipped_own, flipped_far, loss, kept = refs[:6]
    send = refs[6:-2]
    coming = fetch(w_own, w_far, pl.multiple_of(meta[0] * part, part), part, slots, 0, sems)
    rows = logits[0].shape[0]
    pair, me_ctx = meta[3], meta[4]
    top = stats[0][0:1, :]
    for s in stats[1:]:
        top = jnp.maximum(top, s[0:1, :])
    total = jnp.zeros_like(top)
    picked = jnp.zeros_like(top)
    for s in stats:
        total += s[1:2, :] * jnp.exp(s[0:1, :] - top)
        picked += s[2:3, :]
    row = lax.broadcasted_iota(jnp.int32, (1, rows), 1)
    masks = []
    for t in range(n_blocks):
        block = lax.rem(me_ctx + (n_blocks - t), n_blocks)
        seen = lax.rem(row, window) + block * window >= start[pair]
        masks.append(jnp.where(seen, jnp.where(row < window, 1.0, -1.0), 0.0))
    signed_mask = jnp.concatenate(masks, axis=1)
    token_logp = picked - top - jnp.log(total)
    offset = (sums[pair, 0] - refer[pair, 0]) - (sums[pair, 1] - refer[pair, 1])
    zeros = jnp.zeros((1, 128), F32)
    margin = BETA * (jnp.sum(signed_mask * token_logp, axis=1, keepdims=True) + (zeros + offset))
    loss[...] = jnp.maximum(-margin, 0.0) + jnp.log1p(jnp.exp(-jnp.abs(margin)))
    factor = -BETA * (1.0 / (1.0 + jnp.exp(margin))) * cotangent[pair]
    weight = factor[:, 0:1] * signed_mask
    lines = lax.broadcasted_iota(jnp.int32, (128, top.shape[1]), 0)
    packed = jnp.where(lines == 0, top, jnp.where(lines == 1, weight, 1.0 / total)).T
    for t in range(n_blocks):
        at = slice(t * rows, (t + 1) * rows)
        top_t, weight_t, inverse_t = packed[at, 0:1], packed[at, 1:2], packed[at, 2:3]
        wanted = target[at, :]
        for j, (grads, flipped) in enumerate(((grads_own, flipped_own), (grads_far, flipped_far))):
            l = logits[t][:, j * columns:(j + 1) * columns]
            column = lax.broadcasted_iota(jnp.int32, l.shape, 1) + meta[1 + j]
            hit = jnp.where(column == wanted, 1.0, 0.0)
            g = weight_t * (hit - jnp.exp(l - top_t) * inverse_t)
            grads[t] = g.astype(BF16)
            flipped[:, at] = g.T.astype(BF16)
    for copy in coming:
        copy.wait()
    spread(flipped_own[...], flipped_far[...], slots[0, 0], slots[0, 1], kept, send)


def spread_kernel(part, meta, w_own, w_far, flipped_own, flipped_far, kept, *rest):
    send, slots, sems = rest[:-2], rest[-2], rest[-1]
    coming = fetch(w_own, w_far, pl.multiple_of(meta[0] * part, part), part, slots, 0, sems)
    for copy in coming:
        copy.wait()
    spread(flipped_own[...], flipped_far[...], slots[0, 0], slots[0, 1], kept, send)


def spread_shapes(n_blocks, rows, part):
    return [shape_of((part, rows), F32)] + [shape_of((part, rows), BF16)] * (n_blocks - 1)


def weight_slots(part, columns):
    return [pltpu.VMEM((1, 2, part, columns), BF16), pltpu.SemaphoreType.DMA((1, 2))]


def grads_call(logits, target, stats, small, weights, meta, part, window):
    n_blocks, rows, columns = len(logits), logits[0].shape[0], weights[0].shape[1]
    grads = shape_of((n_blocks, rows, columns), BF16)
    flipped = shape_of((columns, n_blocks * rows), BF16)
    out_shape = [grads, grads, flipped, flipped, shape_of((1, 128), F32)] + spread_shapes(n_blocks, rows, part)
    operands = list(logits) + [target] + list(stats)
    return pl.pallas_call(
        functools.partial(grads_kernel, n_blocks, len(stats), columns, part, window),
        out_shape=out_shape,
        in_specs=[IN_SMEM] * 5 + [IN_PLACE] * 2 + [IN_VMEM] * len(operands),
        out_specs=[IN_VMEM] * len(out_shape),
        scratch_shapes=weight_slots(part, columns),
        compiler_params=params(),
        cost_estimate=cost(4 * n_blocks * rows * part * columns, 8 * part * columns),
    )(meta, *small, *weights, *operands)


def spread_call(flipped_own, flipped_far, weights, k_id, part, rows):
    columns, n_rows = flipped_own.shape
    out_shape = spread_shapes(n_rows // rows, rows, part)
    return pl.pallas_call(
        functools.partial(spread_kernel, part),
        out_shape=out_shape,
        in_specs=[IN_SMEM] + [IN_PLACE] * 2 + [IN_VMEM] * 2,
        out_specs=[IN_VMEM] * len(out_shape),
        scratch_shapes=weight_slots(part, columns),
        compiler_params=params(),
        cost_estimate=cost(4 * n_rows * part * columns, 4 * part * columns),
    )(k_id.reshape(1).astype(jnp.int32), *weights, flipped_own, flipped_far)


def add_kernel(turned, kept, *refs):
    total = kept[...]
    for a in refs[:-1]:
        total += a[...].astype(F32)
    refs[-1][...] = (total.T if turned else total).astype(BF16)


def add_call(kept, arrived, turned=False):
    shape = kept.shape[::-1] if turned else kept.shape
    return pl.pallas_call(
        functools.partial(add_kernel, turned),
        out_shape=shape_of(shape, BF16),
        in_specs=[IN_VMEM] * (1 + len(arrived)),
        out_specs=IN_VMEM,
        compiler_params=params(),
        cost_estimate=cost(kept.size, 4 * kept.size),
    )(kept, *arrived)


def head_kernel(near_keys, far_keys, n_parts, part, meta, *refs):
    refs = list(refs)
    grads = [refs.pop(0), refs.pop(0)]
    near = {k: refs.pop(0) for k in near_keys}
    stacks = [refs.pop(0) for _ in far_keys]
    far = {k: stack.at[i] for stack, keys in zip(stacks, far_keys) for i, k in enumerate(keys)}
    out, slots, sems = refs
    n_blocks, rows, columns = grads[0].shape
    right = jnp.concatenate([g[...].reshape(n_blocks * rows, columns) for g in grads])
    copies = []
    for i in range(n_parts):
        left = jnp.concatenate([x[t, i][...] for x in (near, far) for t in range(n_blocks)])
        product = lax.dot_general(left, right, (((0,), (0,)), ((), ())), preferred_element_type=F32)
        if i >= 2:
            copies[i - 2].wait()
        slots[i % 2] = product.astype(BF16)
        start = pl.multiple_of(meta[i] * part, part)
        copies.append(pltpu.make_async_copy(slots.at[i % 2], out.at[pl.ds(start, part), :], sems.at[i % 2]))
        copies[-1].start()
    for copy in copies[-2:]:
        copy.wait()


def head_call(near, far, grads, meta):
    n_blocks, rows, columns = grads[0].shape
    n_parts = len(near) // n_blocks
    part = near[0, 0].shape[1]
    operands = list(grads) + list(near.values()) + [stack for _, stack in far]
    return pl.pallas_call(
        functools.partial(head_kernel, list(near), [keys for keys, _ in far], n_parts, part),
        out_shape=shape_of((n_parts * part, columns), BF16),
        in_specs=[IN_SMEM] + [IN_VMEM] * len(operands),
        out_specs=pl.BlockSpec(memory_space=pl.ANY),
        scratch_shapes=[pltpu.VMEM((2, part, columns), BF16), pltpu.SemaphoreType.DMA((2,))],
        compiler_params=params(),
        cost_estimate=cost(
            4 * n_blocks * rows * n_parts * part * columns,
            4 * n_blocks * n_parts * rows * part + 2 * n_parts * part * columns,
        ),
    )(meta, *operands)


def together(*groups):
    flat = lax.optimization_barrier([a for group in groups for a in group])
    out = []
    for group in groups:
        out.append(flat[:len(group)])
        flat = flat[len(group):]
    return out


def shards(hidden, head_weight, targets, response_start, other_sums, ref_logp, loss_cotangent):
    n_voc, n_ctx, n_dp = lax.axis_size("vocab"), lax.axis_size("ctx"), lax.axis_size("dp")
    me_voc, me_ctx, me_dp = lax.axis_index("vocab"), lax.axis_index("ctx"), lax.axis_index("dp")
    part, _, sides, window = hidden.shape
    rows = sides * window
    columns = head_weight.shape[1]
    line = n_voc == 4
    beyond = list(range(1, n_ctx))
    dp_swap = lambda a: lax.ppermute(a, "dp", ring(n_dp, 1))
    along = lambda a, by: lax.ppermute(a, "vocab", by)

    if line:
        table = [[0, 1, 2, 3], [1, 0, 2, 3], [2, 3, 1, 0], [3, 2, 1, 0]]
        part_of = [sum(jnp.where(me_voc == z, table[z][i], 0) for z in range(n_voc)) for i in range(n_voc)]
    else:
        part_of = [(me_voc - s) % n_voc for s in range(n_voc)]
    firsts = [
        ((me_voc * n_ctx + me_ctx) * n_dp + owner) * columns for owner in (me_dp, (me_dp + 1) % n_dp)
    ]
    meta = jnp.stack(part_of + firsts).astype(jnp.int32)

    weights = (head_weight, dp_swap(head_weight))

    own = hidden.transpose(1, 2, 3, 0).reshape(rows, part)
    chunk = {(0, 0): own}
    logits = [None] * n_ctx
    stats = [None] * n_ctx
    call = functools.partial(logits_call, meta=meta, weights=weights, part=part, n_voc=n_voc)
    cross = lambda a: [lax.ppermute(a, "ctx", ring(n_ctx, t)) for t in beyond]
    inner = last = None
    for step in range(n_voc):
        over = cross(chunk[0, step])
        came = []
        if line:
            if step == 0:
                came = [along(own, PAIRS_OUT), along(own, PAIR_IN)]
            elif step == 1:
                came = [along(inner, TO_ENDS), along(chunk[0, 1], PAIR_IN)]
            elif step == 2:
                came = [along(last, TO_ENDS)]
        elif step + 1 < n_voc:
            came = [along(own, ring(n_voc, step + 1))]
        if step:
            plan = [(0, {i: chunk[0, i] for i in ([0, 1] if step == 1 else [step])}, logits[0], None)]
            plan += [(t, {step - 1: chunk[t, step - 1]}, logits[t], None) for t in beyond]
            if step == n_voc - 1:
                plan[0] = plan[0][:3] + (wanted[0],)
            done = list(call(plan))
            if step == n_voc - 1:
                stats[0] = done.pop(1)
            logits = list(done)
        else:
            held, raw = together(came[:1], [targets])
            pair = lax.broadcasted_iota(jnp.int32, targets.shape, 0)
            mine = jnp.sum(jnp.where(pair == me_dp, raw[0], 0), axis=0)
            blocks = [mine[:, b * window:(b + 1) * window].reshape(rows) for b in range(n_ctx)]
            wanted = []
            for t in range(n_ctx):
                at = (me_ctx - t) % n_ctx
                wanted.append(sum(jnp.where(at == b, blocks[b], 0) for b in range(n_ctx))[:, None])
            target = jnp.concatenate(wanted)
        ready = [a for a in logits if a is not None]
        over, came, ready = together(over, came, ready)
        if ready:
            logits = ready
        for t, a in zip(beyond, over):
            chunk[t, step] = a
        if not line:
            if came:
                chunk[0, step + 1] = came[0]
        elif step == 0:
            chunk[0, 1], inner = came
        elif step == 1:
            chunk[0, 2] = inner + came[0]
            last = came[1]
        elif step == 2:
            chunk[0, 3] = last + came[0]

    final = n_voc - 1
    done = call([(t, {final: chunk[t, final]}, logits[t], wanted[t]) for t in beyond])
    logits = [logits[0]] + list(done[0::2])
    stats = [stats[0]] + list(done[1::2])

    late = [(t, final) for t in beyond]
    soon = [k for k in chunk if k not in late]
    far_soon = dp_swap(jnp.stack([chunk[k] for k in soon]))

    others = cross(jnp.stack(stats))
    merged = []
    for b in range(n_ctx):
        seen = [stats[b]] + [o[(b - t) % n_ctx] for t, o in zip(beyond, others)]
        top = seen[0][0]
        for o in seen[1:]:
            top = jnp.maximum(top, o[0])
        total = sum(o[1] * jnp.exp(o[0] - top) for o in seen)
        picked = sum(o[2] for o in seen)
        merged.append(jnp.pad(jnp.stack([top, total, picked]), ((0, 5), (0, 0))))
    merged = jnp.concatenate(merged, axis=1)
    all_stats = [merged] + [along(merged, ring(n_voc, s)) for s in range(1, n_voc)]

    meta_grads = jnp.stack([part_of[final]] + firsts + [me_dp, me_ctx]).astype(jnp.int32)
    small = (response_start, other_sums, ref_logp, loss_cotangent)
    grads_own, grads_far, flipped_own, flipped_far, loss, kept, *send = grads_call(
        logits, target, all_stats, small, weights, meta_grads, part, window
    )
    theirs = dp_swap(grads_far)
    far_late = dp_swap(jnp.stack(together([chunk[k] for k in late], [kept])[0]))
    back = lambda cs: [lax.ppermute(c, "ctx", ring(n_ctx, -t)) for t, c in zip(beyond, cs)]
    landed = []
    for step in range(n_voc):
        slot = final - step
        over = back(send)
        came = []
        if line:
            if step == 1:
                sum_3 = (kept_before, arrived)
                came = [along(add_call(*sum_3), FROM_ENDS)]
            elif step == 2:
                sum_2 = (kept_before, arrived)
                came = [along(add_call(*sum_2), FROM_ENDS), along(add_call(sum_3[0], sum_3[1] + landed), PAIR_IN)]
            elif step == 3:
                came = [
                    along(add_call(kept_before, arrived + landed[1:]), PAIRS_OUT),
                    along(add_call(sum_2[0], sum_2[1] + landed[:1]), PAIR_IN),
                ]
        elif step:
            came = [along(add_call(kept_before, arrived), ring(n_voc, -(slot + 1)))]
        kept_before = kept
        if step < n_voc - 1:
            kept, *send = spread_call(flipped_own, flipped_far, weights, part_of[slot - 1], part, rows)
            arrived, came, send = together(over, came, send)
        else:
            grad_head = head_call(chunk, [(soon, far_soon), (late, far_late)], [grads_own, theirs], meta)
            arrived, came, (grad_head,) = together(over, came, [grad_head])
        landed = came if line else landed + came
    summed = add_call(kept_before, arrived + landed, turned=True)
    grad_hidden = summed.reshape(1, sides, window, part).transpose(3, 0, 1, 2)

    far_loss = dp_swap(loss)
    pair = lax.broadcasted_iota(jnp.int32, (n_dp,), 0)
    pair_loss = jnp.where(pair == me_dp, loss[0, :n_dp], far_loss[0, :n_dp])
    return (grad_hidden, grad_head, pair_loss)


def solution(mesh):
    placed = (
        P("vocab", ("groups", "dp"), None, "ctx"),
        P(None, ("vocab", "ctx", "dp")),
        P("groups", None, None),
        P("groups"),
        P("groups", None),
        P("groups", None),
        P("groups"),
    )
    return jax.shard_map(
        shards,
        mesh=mesh,
        in_specs=placed,
        out_specs=(
            P("vocab", ("groups", "dp"), None, "ctx"),
            P("groups", ("vocab", "ctx", "dp")),
            P("groups"),
        ),
        check_vma=False,
    )
```

```python
import functools

import jax
import jax.numpy as jnp
from jax import lax
from jax.experimental import pallas as pl
from jax.experimental.pallas import tpu as pltpu
from jax.sharding import PartitionSpec as P

BETA = 0.1
F32, BF16 = jnp.float32, jnp.bfloat16
VMEM_BYTES = 16 * 1024 * 1024
IN_VMEM = pl.BlockSpec(memory_space=pltpu.VMEM)
IN_SMEM = pl.BlockSpec(memory_space=pltpu.SMEM)
IN_PLACE = pl.BlockSpec(memory_space=pl.ANY)
PAIRS_OUT = [(0, 1), (1, 0), (2, 3), (3, 2)]
PAIR_IN = [(1, 2), (2, 1)]
TO_ENDS = [(1, 0), (2, 3)]
FROM_ENDS = [(0, 1), (3, 2)]
SWAP_HALVES = [(0, 2), (2, 0), (1, 3), (3, 1)]


def ring(count, shift):
    return [(i, (i + shift) % count) for i in range(count)]


def params():
    return pltpu.CompilerParams(vmem_limit_bytes=VMEM_BYTES)


def cost(flops, moved):
    return pl.CostEstimate(flops=int(flops), bytes_accessed=int(moved), transcendentals=0)


def shape_of(shape, kind):
    return jax.ShapeDtypeStruct(shape, kind)


def hold_kernel(w, out, sem):
    copy = pltpu.make_async_copy(w, out, sem)
    copy.start()
    copy.wait()


def hold(w):
    return pl.pallas_call(
        hold_kernel,
        out_shape=shape_of(w.shape, w.dtype),
        in_specs=[IN_PLACE],
        out_specs=IN_VMEM,
        scratch_shapes=[pltpu.SemaphoreType.DMA],
        compiler_params=params(),
        cost_estimate=cost(1, 4 * w.size),
    )(w)


def row_stats(own, far, wanted, first_own, first_far):
    top = jnp.max(jnp.maximum(own, far), axis=1, keepdims=True)
    total = jnp.sum(jnp.exp(own - top) + jnp.exp(far - top), axis=1, keepdims=True)
    column = lax.broadcasted_iota(jnp.int32, own.shape, 1)
    zero = jnp.zeros_like(own)
    picked = jnp.sum(
        jnp.where(column + first_own == wanted, own, zero) + jnp.where(column + first_far == wanted, far, zero),
        axis=1,
        keepdims=True,
    )
    lane = lax.broadcasted_iota(jnp.int32, (own.shape[0], 128), 1)
    return jnp.where(lane == 0, top, jnp.where(lane == 1, total, picked)).T[:8, :]


def logits_kernel(plan, columns, part, n_voc, meta, w_own, w_far, *refs):
    refs = list(refs)
    chunks = {(t, i): refs.pop(0) for t, parts, _, _ in plan for i in parts}
    accs = {t: refs.pop(0) for t, _, has_acc, _ in plan if has_acc}
    wanted = {t: refs.pop(0) for t, _, _, done in plan if done}
    used = sorted({i for _, parts, _, _ in plan for i in parts})
    outs = {}
    stats = {}
    for t, _, _, done in plan:
        outs[t] = refs.pop(0)
        if done:
            stats[t] = refs.pop(0)
    for i in used:
        at_part = pl.ds(pl.multiple_of(meta[i] * part, part), part)
        for t, parts, has_acc, _ in plan:
            if i not in parts:
                continue
            x = chunks[t, i][...]
            for j, w in enumerate((w_own, w_far)):
                at = slice(j * columns, (j + 1) * columns)
                product = jnp.dot(x, w[at_part, :], preferred_element_type=F32)
                if i != parts[0]:
                    product += outs[t][:, at]
                elif has_acc:
                    product += accs[t][:, at]
                outs[t][:, at] = product
    for t in stats:
        own, far = outs[t][:, :columns], outs[t][:, columns:]
        stats[t][...] = row_stats(own, far, wanted[t][...], meta[n_voc], meta[n_voc + 1])


def logits_call(plan, meta, weights, part, n_voc):
    columns = weights[0].shape[1]
    chunks = [c for _, parts, _, _ in plan for c in parts.values()]
    accs = [acc for _, _, acc, _ in plan if acc is not None]
    wanted = [w for _, _, _, w in plan if w is not None]
    rows = chunks[0].shape[0]
    out_shape = []
    for _, _, _, w in plan:
        out_shape.append(shape_of((rows, 2 * columns), F32))
        if w is not None:
            out_shape.append(shape_of((8, rows), F32))
    kernel_plan = [(t, sorted(parts), acc is not None, w is not None) for t, parts, acc, w in plan]
    chunks = [parts[i] for _, parts, _, _ in plan for i in sorted(parts)]
    operands = list(weights) + chunks + accs + wanted
    return pl.pallas_call(
        functools.partial(logits_kernel, kernel_plan, columns, part, n_voc),
        out_shape=out_shape,
        in_specs=[IN_SMEM] + [IN_VMEM] * len(operands),
        out_specs=[IN_VMEM] * len(out_shape),
        compiler_params=params(),
        cost_estimate=cost(4 * len(chunks) * rows * part * columns, len(chunks) * 4 * part * columns),
    )(meta, *operands)


def spread(flipped_own, flipped_far, w_own, w_far, kept, send):
    rows = kept.shape[1]
    here = jnp.dot(w_own, flipped_own, preferred_element_type=F32)
    here += jnp.dot(w_far, flipped_far, preferred_element_type=F32)
    kept[...] = here[:, :rows]
    for t, out in enumerate(send, 1):
        out[...] = here[:, t * rows:(t + 1) * rows].astype(BF16)


def grads_kernel(n_blocks, n_stats, columns, part, window, meta, start, sums, refer, cotangent, w_own, w_far, *refs):
    refs = list(refs)
    logits = [refs.pop(0) for _ in range(n_blocks)]
    target = refs.pop(0)
    stats = [refs.pop(0) for _ in range(n_stats)]
    grads_own, grads_far, flipped_own, flipped_far, loss, kept = refs[:6]
    send = refs[6:]
    rows = logits[0].shape[0]
    pair, me_ctx = meta[3], meta[4]
    top = stats[0][0:1, :]
    for s in stats[1:]:
        top = jnp.maximum(top, s[0:1, :])
    total = jnp.zeros_like(top)
    picked = jnp.zeros_like(top)
    for s in stats:
        total += s[1:2, :] * jnp.exp(s[0:1, :] - top)
        picked += s[2:3, :]
    row = lax.broadcasted_iota(jnp.int32, (1, rows), 1)
    masks = []
    for t in range(n_blocks):
        block = lax.rem(me_ctx + (n_blocks - t), n_blocks)
        seen = lax.rem(row, window) + block * window >= start[pair]
        masks.append(jnp.where(seen, jnp.where(row < window, 1.0, -1.0), 0.0))
    signed_mask = jnp.concatenate(masks, axis=1)
    token_logp = picked - top - jnp.log(total)
    offset = (sums[pair, 0] - refer[pair, 0]) - (sums[pair, 1] - refer[pair, 1])
    zeros = jnp.zeros((1, 128), F32)
    margin = BETA * (jnp.sum(signed_mask * token_logp, axis=1, keepdims=True) + (zeros + offset))
    loss[...] = jnp.maximum(-margin, 0.0) + jnp.log1p(jnp.exp(-jnp.abs(margin)))
    factor = -BETA * (1.0 / (1.0 + jnp.exp(margin))) * cotangent[pair]
    weight = factor[:, 0:1] * signed_mask
    lines = lax.broadcasted_iota(jnp.int32, (128, top.shape[1]), 0)
    packed = jnp.where(lines == 0, top, jnp.where(lines == 1, weight, 1.0 / total)).T
    for t in range(n_blocks):
        at = slice(t * rows, (t + 1) * rows)
        top_t, weight_t, inverse_t = packed[at, 0:1], packed[at, 1:2], packed[at, 2:3]
        wanted = target[at, :]
        for j, (grads, flipped) in enumerate(((grads_own, flipped_own), (grads_far, flipped_far))):
            l = logits[t][:, j * columns:(j + 1) * columns]
            column = lax.broadcasted_iota(jnp.int32, l.shape, 1) + meta[1 + j]
            hit = jnp.where(column == wanted, 1.0, 0.0)
            g = weight_t * (hit - jnp.exp(l - top_t) * inverse_t)
            grads[t] = g.astype(BF16)
            flipped[:, at] = g.T.astype(BF16)
    at_part = pl.ds(pl.multiple_of(meta[0] * part, part), part)
    spread(flipped_own[...], flipped_far[...], w_own[at_part, :], w_far[at_part, :], kept, send)


def spread_kernel(part, n_parts, meta, w_own, w_far, flipped_own, flipped_far, *outs):
    each = len(outs) // n_parts
    for i in range(n_parts):
        kept, *send = outs[i * each:(i + 1) * each]
        at_part = pl.ds(pl.multiple_of(meta[i] * part, part), part)
        spread(flipped_own[...], flipped_far[...], w_own[at_part, :], w_far[at_part, :], kept, send)


def spread_shapes(n_blocks, rows, part):
    return [shape_of((part, rows), F32)] + [shape_of((part, rows), BF16)] * (n_blocks - 1)


def grads_call(logits, target, stats, small, weights, meta, part, window):
    n_blocks, rows, columns = len(logits), logits[0].shape[0], weights[0].shape[1]
    grads = shape_of((n_blocks, rows, columns), BF16)
    flipped = shape_of((columns, n_blocks * rows), BF16)
    out_shape = [grads, grads, flipped, flipped, shape_of((1, 128), F32)] + spread_shapes(n_blocks, rows, part)
    operands = list(logits) + [target] + list(stats)
    return pl.pallas_call(
        functools.partial(grads_kernel, n_blocks, len(stats), columns, part, window),
        out_shape=out_shape,
        in_specs=[IN_SMEM] * 5 + [IN_VMEM] * (2 + len(operands)),
        out_specs=[IN_VMEM] * len(out_shape),
        compiler_params=params(),
        cost_estimate=cost(4 * n_blocks * rows * part * columns, 8 * part * columns),
    )(meta, *small, *weights, *operands)


def spread_call(flipped_own, flipped_far, weights, k_ids, part, rows):
    columns, n_rows = flipped_own.shape
    n_parts = len(k_ids)
    out_shape = spread_shapes(n_rows // rows, rows, part) * n_parts
    outs = pl.pallas_call(
        functools.partial(spread_kernel, part, n_parts),
        out_shape=out_shape,
        in_specs=[IN_SMEM] + [IN_VMEM] * 4,
        out_specs=[IN_VMEM] * len(out_shape),
        compiler_params=params(),
        cost_estimate=cost(4 * n_parts * n_rows * part * columns, 4 * n_parts * part * columns),
    )(jnp.stack(k_ids).astype(jnp.int32), *weights, flipped_own, flipped_far)
    each = len(outs) // n_parts
    return [(outs[i * each], list(outs[i * each + 1:(i + 1) * each])) for i in range(n_parts)]


def add_kernel(turned, kept, *refs):
    total = kept[...]
    for a in refs[:-1]:
        total += a[...].astype(F32)
    refs[-1][...] = (total.T if turned else total).astype(BF16)


def add_call(kept, arrived, turned=False):
    shape = kept.shape[::-1] if turned else kept.shape
    return pl.pallas_call(
        functools.partial(add_kernel, turned),
        out_shape=shape_of(shape, BF16),
        in_specs=[IN_VMEM] * (1 + len(arrived)),
        out_specs=IN_VMEM,
        compiler_params=params(),
        cost_estimate=cost(kept.size, 4 * kept.size),
    )(kept, *arrived)


def head_kernel(slots_here, near_keys, far_keys, part, has_out, meta, *refs):
    refs = list(refs)
    grads = [refs.pop(0), refs.pop(0)]
    near = {k: refs.pop(0) for k in near_keys}
    stacks = [refs.pop(0) for _ in far_keys]
    far = {k: stack.at[i] for stack, keys in zip(stacks, far_keys) for i, k in enumerate(keys)}
    out, ready, sems = refs[has_out:]
    n_blocks, rows, columns = grads[0].shape
    right = jnp.concatenate([g[...].reshape(n_blocks * rows, columns) for g in grads])
    copies = []
    for n, i in enumerate(slots_here):
        left = jnp.concatenate([x[t, i][...] for x in (near, far) for t in range(n_blocks)])
        product = lax.dot_general(left, right, (((0,), (0,)), ((), ())), preferred_element_type=F32)
        if n >= 2:
            copies[n - 2].wait()
        ready[n % 2] = product.astype(BF16)
        start = pl.multiple_of(meta[i] * part, part)
        copies.append(pltpu.make_async_copy(ready.at[n % 2], out.at[pl.ds(start, part), :], sems.at[n % 2]))
        copies[-1].start()
    for copy in copies[-2:]:
        copy.wait()


def head_call(slots_here, near, far, grads, meta, out=None):
    n_blocks, rows, columns = grads[0].shape
    n_parts = len(near) // n_blocks
    part = near[0, 0].shape[1]
    near = {k: c for k, c in near.items() if k[1] in slots_here}
    far = [(keys, stack) for keys, stack in far if any(k[1] in slots_here for k in keys)]
    operands = list(grads) + list(near.values()) + [stack for _, stack in far]
    here = [] if out is None else [out]
    return pl.pallas_call(
        functools.partial(head_kernel, slots_here, list(near), [keys for keys, _ in far], part, len(here)),
        out_shape=shape_of((n_parts * part, columns), BF16),
        in_specs=[IN_SMEM] + [IN_VMEM] * len(operands) + [IN_PLACE] * len(here),
        out_specs=IN_PLACE,
        scratch_shapes=[pltpu.VMEM((2, part, columns), BF16), pltpu.SemaphoreType.DMA((2,))],
        input_output_aliases={1 + len(operands): 0} if here else {},
        compiler_params=params(),
        cost_estimate=cost(
            4 * n_blocks * rows * len(slots_here) * part * columns,
            4 * n_blocks * len(slots_here) * rows * part + 2 * len(slots_here) * part * columns,
        ),
    )(meta, *operands, *here)


def together(*groups):
    flat = lax.optimization_barrier([a for group in groups for a in group])
    out = []
    for group in groups:
        out.append(flat[:len(group)])
        flat = flat[len(group):]
    return out


def shards(hidden, head_weight, targets, response_start, other_sums, ref_logp, loss_cotangent):
    n_voc, n_ctx, n_dp = lax.axis_size("vocab"), lax.axis_size("ctx"), lax.axis_size("dp")
    me_voc, me_ctx, me_dp = lax.axis_index("vocab"), lax.axis_index("ctx"), lax.axis_index("dp")
    part, _, sides, window = hidden.shape
    rows = sides * window
    columns = head_weight.shape[1]
    line = n_voc == 4
    beyond = list(range(1, n_ctx))
    dp_swap = lambda a: lax.ppermute(a, "dp", ring(n_dp, 1))
    along = lambda a, by: lax.ppermute(a, "vocab", by)

    if line:
        table = [[0, 1, 2, 3], [1, 0, 2, 3], [2, 3, 1, 0], [3, 2, 1, 0]]
        part_of = [sum(jnp.where(me_voc == z, table[z][i], 0) for z in range(n_voc)) for i in range(n_voc)]
    else:
        part_of = [(me_voc - s) % n_voc for s in range(n_voc)]
    firsts = [
        ((me_voc * n_ctx + me_ctx) * n_dp + owner) * columns for owner in (me_dp, (me_dp + 1) % n_dp)
    ]
    meta = jnp.stack(part_of + firsts).astype(jnp.int32)

    weights = (hold(head_weight), dp_swap(head_weight))

    pair = lax.broadcasted_iota(jnp.int32, targets.shape, 0)

    def by_block(all_targets):
        mine = jnp.sum(jnp.where(pair == me_dp, all_targets, 0), axis=0)
        blocks = [mine[:, b * window:(b + 1) * window].reshape(rows) for b in range(n_ctx)]
        wanted = []
        for t in range(n_ctx):
            at = (me_ctx - t) % n_ctx
            wanted.append(sum(jnp.where(at == b, blocks[b], 0) for b in range(n_ctx))[:, None])
        return wanted

    own = hidden.transpose(1, 2, 3, 0).reshape(rows, part)
    final = n_voc - 1
    call = functools.partial(logits_call, meta=meta, weights=weights, part=part, n_voc=n_voc)
    cross = lambda a: [lax.ppermute(a, "ctx", ring(n_ctx, t)) for t in beyond]
    chunk = {}

    def arrive(i, near, over):
        chunk[0, i] = near
        for t, a in zip(beyond, over):
            chunk[t, i] = a

    def more_logits(i, logits):
        if logits is None:
            return call([(0, {j: chunk[0, j] for j in (0, 1)}, None, None)] + [(t, {0: chunk[t, 0]}, None, None) for t in beyond])
        return call(
            [(0, {i: chunk[0, i]}, logits[0], None)] + [(t, {i - 1: chunk[t, i - 1]}, logits[t], None) for t in beyond]
        )

    arrive(0, own, cross(own))
    if line:
        first = along(own, PAIRS_OUT)
        inner = along(own, PAIR_IN)
        over = cross(first)
        outer, inner_last = along(inner, TO_ENDS), along(first, PAIR_IN)
        arrive(1, first, over)
        over, (inner, outer, inner_last), logits = together(over, [inner, outer, inner_last], more_logits(1, None))
        arrive(1, first, over)
        arrive(2, inner + outer, cross(inner + outer))
        outer = along(inner_last, TO_ENDS)
        (inner_last, outer), logits = together([inner_last, outer], more_logits(2, logits))
        last = inner_last + outer
    else:
        near = [own] + [along(own, ring(n_voc, i)) for i in range(1, n_voc)]
        logits = None
        for i in range(1, final):
            arrive(i, near[i], cross(near[i]))
            (near[i + 1],), logits = together([near[i + 1]], more_logits(i, logits))
        last = near[final]
    arrive(final, last, cross(last))
    (raw_targets,), _ = together([targets], logits)
    wanted = by_block(raw_targets)
    target = jnp.concatenate(wanted)

    done = call(
        [(0, {final: chunk[0, final]}, logits[0], wanted[0])]
        + [(t, {final - 1: chunk[t, final - 1]}, logits[t], None) for t in beyond]
    )
    logits, stats = [done[0]] + list(done[2:]), [done[1]]
    done = call([(t, {final: chunk[t, final]}, logits[t], wanted[t]) for t in beyond])
    logits = [logits[0]] + list(done[0::2])
    stats = stats + list(done[1::2])

    late = [(t, final) for t in beyond]
    soon = [k for k in chunk if k not in late]
    far_soon = dp_swap(jnp.stack(together([chunk[k] for k in soon], [stats[0]])[0]))

    def merge(seen):
        merged = []
        for b in range(n_ctx):
            these = [s[(b - t) % n_ctx] for t, s in seen]
            top = these[0][0]
            for s in these[1:]:
                top = jnp.maximum(top, s[0])
            total = sum(s[1] * jnp.exp(s[0] - top) for s in these)
            picked = sum(s[2] for s in these)
            merged.append(jnp.pad(jnp.stack([top, total, picked]), ((0, 5), (0, 0))))
        return jnp.concatenate(merged, axis=1)

    stats = jnp.stack(stats)
    if line and n_ctx == 2:
        corner = [(2 * a + c, 2 * b + (1 - c)) for a, b in PAIRS_OUT for c in range(2)]
        diagonal = lax.ppermute(stats, ("vocab", "ctx"), corner)
        merged = merge([(0, stats), (1, cross(stats)[0]), (0, along(stats, PAIRS_OUT)), (1, diagonal)])
        all_stats = [merged, along(merged, SWAP_HALVES)]
    else:
        merged = merge([(0, stats)] + list(zip(beyond, cross(stats))))
        all_stats = [merged] + [along(merged, ring(n_voc, s)) for s in range(1, n_voc)]

    meta_grads = jnp.stack([part_of[final]] + firsts + [me_dp, me_ctx]).astype(jnp.int32)
    small = (response_start, other_sums, ref_logp, loss_cotangent)
    grads_own, grads_far, flipped_own, flipped_far, loss, kept, *send = grads_call(
        logits, target, all_stats, small, weights, meta_grads, part, window
    )
    theirs = dp_swap(grads_far)
    far_late = dp_swap(jnp.stack(together([chunk[k] for k in late], [kept])[0]))
    back = lambda cs: [lax.ppermute(c, "ctx", ring(n_ctx, -t)) for t, c in zip(beyond, cs)]
    shares = {final: (kept, list(send))}
    leave = list(range(final))[::-1]
    for i, share in zip(leave, spread_call(flipped_own, flipped_far, weights, [part_of[i] for i in leave], part, rows)):
        shares[i] = share

    over = {}
    for i in range(n_voc)[::-1]:
        send = shares[i][1]
        if i + 2 in over:
            over[i + 2], send = together(over[i + 2], send)
        over[i] = back(send)
    near_over = lambda i, *more: add_call(shares[i][0], over[i] + list(more))
    head = functools.partial(head_call, near=chunk, far=[(soon, far_soon), (late, far_late)], grads=[grads_own, theirs], meta=meta)
    early, rest = list(range(n_voc // 2)), list(range(n_voc // 2, n_voc))
    grad_head = head(early)
    if line:
        up_3 = along(near_over(3), FROM_ENDS)
        up_2 = along(near_over(2), FROM_ENDS)
        up_3 = along(near_over(3, up_3), PAIR_IN)
        (up_3,), (grad_head,) = together([up_3], [grad_head])
        landed = [along(near_over(1, up_3), PAIRS_OUT), along(near_over(2, up_2), PAIR_IN)]
    else:
        landed = [along(near_over(i), ring(n_voc, -i)) for i in range(1, n_voc)]
    grad_head = head(rest, out=grad_head)
    (kept,), (grad_head,) = together([shares[0][0]], [grad_head])
    summed = add_call(kept, over[0] + landed, turned=True)
    grad_hidden = summed.reshape(1, sides, window, part).transpose(3, 0, 1, 2)

    far_loss = dp_swap(loss)
    owner = lax.broadcasted_iota(jnp.int32, (n_dp,), 0)
    pair_loss = jnp.where(owner == me_dp, loss[0, :n_dp], far_loss[0, :n_dp])
    return (grad_hidden, grad_head, pair_loss)


def solution(mesh):
    placed = (
        P("vocab", ("groups", "dp"), None, "ctx"),
        P(None, ("vocab", "ctx", "dp")),
        P("groups", None, None),
        P("groups"),
        P("groups", None),
        P("groups", None),
        P("groups"),
    )
    return jax.shard_map(
        shards,
        mesh=mesh,
        in_specs=placed,
        out_specs=(
            P("vocab", ("groups", "dp"), None, "ctx"),
            P("groups", ("vocab", "ctx", "dp")),
            P("groups"),
        ),
        check_vma=False,
    )
```

```python
import functools

import jax
import jax.numpy as jnp
from jax import lax
from jax.experimental import pallas as pl
from jax.experimental.pallas import tpu as pltpu
from jax.sharding import PartitionSpec as P

BETA = 0.1
F32, BF16 = jnp.float32, jnp.bfloat16
VMEM_BYTES = 40 * 1024 * 1024
WORK_BYTES = 32 * 1024 * 1024
IN_VMEM = pl.BlockSpec(memory_space=pltpu.VMEM)
IN_SMEM = pl.BlockSpec(memory_space=pltpu.SMEM)
IN_PLACE = pl.BlockSpec(memory_space=pl.ANY)
PAIRS_OUT = [(0, 1), (1, 0), (2, 3), (3, 2)]
PAIR_IN = [(1, 2), (2, 1)]
TO_ENDS = [(1, 0), (2, 3)]
FROM_ENDS = [(0, 1), (3, 2)]
SWAP_HALVES = [(0, 2), (2, 0), (1, 3), (3, 1)]


def ring(count, shift):
    return [(i, (i + shift) % count) for i in range(count)]


def params():
    return pltpu.CompilerParams(vmem_limit_bytes=VMEM_BYTES)


def cost(flops, moved):
    return pl.CostEstimate(flops=int(flops), bytes_accessed=int(moved), transcendentals=0)


def shape_of(shape, kind):
    return jax.ShapeDtypeStruct(shape, kind)


def work_shape(w):
    times = max(2, -(-WORK_BYTES // (w.size * w.dtype.itemsize)))
    return shape_of((times * w.shape[0], w.shape[1]), w.dtype)


def hold_kernel(w, out, sem):
    copy = pltpu.make_async_copy(w, out.at[pl.ds(0, w.shape[0]), :], sem)
    copy.start()
    copy.wait()


def hold(w):
    return pl.pallas_call(
        hold_kernel,
        out_shape=work_shape(w),
        in_specs=[IN_PLACE],
        out_specs=IN_PLACE,
        scratch_shapes=[pltpu.SemaphoreType.DMA],
        compiler_params=params(),
        cost_estimate=cost(1, 4 * w.size),
    )(w)


def fetch(work, width, start, part, slots, i, sems, far=None):
    own = work.at[pl.ds(start, part), :]
    far = work.at[pl.ds(width + start, part), :] if far is None else far.at[pl.ds(start, part), :]
    copies = []
    for j, w in enumerate((own, far)):
        copies.append(pltpu.make_async_copy(w, slots.at[i, j], sems.at[i, j]))
        copies[-1].start()
    return copies


def row_stats(own, far, wanted, first_own, first_far):
    top = jnp.max(jnp.maximum(own, far), axis=1, keepdims=True)
    total = jnp.sum(jnp.exp(own - top) + jnp.exp(far - top), axis=1, keepdims=True)
    column = lax.broadcasted_iota(jnp.int32, own.shape, 1)
    zero = jnp.zeros_like(own)
    picked = jnp.sum(
        jnp.where(column + first_own == wanted, own, zero) + jnp.where(column + first_far == wanted, far, zero),
        axis=1,
        keepdims=True,
    )
    lane = lax.broadcasted_iota(jnp.int32, (own.shape[0], 128), 1)
    return jnp.where(lane == 0, top, jnp.where(lane == 1, total, picked)).T[:8, :]


def logits_kernel(plan, columns, part, n_voc, fresh, meta, work, *refs):
    refs = list(refs)
    width = part * n_voc
    far = refs.pop(0) if fresh else None
    chunks = {(t, i): refs.pop(0) for t, parts, _, _ in plan for i in parts}
    accs = {t: refs.pop(0) for t, _, has_acc, _ in plan if has_acc}
    wanted = {t: refs.pop(0) for t, _, _, done in plan if done}
    used = sorted({i for _, parts, _, _ in plan for i in parts})
    slots, sems = refs[-2:]
    coming = [
        fetch(work, width, pl.multiple_of(meta[i] * part, part), part, slots, n, sems, far) for n, i in enumerate(used)
    ]
    if fresh:
        kept = pltpu.make_async_copy(far, refs[-3].at[pl.ds(width, width), :], sems.at[len(used), 0])
        kept.start()
    outs = {}
    stats = {}
    for t, _, _, done in plan:
        outs[t] = refs.pop(0)
        if done:
            stats[t] = refs.pop(0)
    for n, i in enumerate(used):
        for copy in coming[n]:
            copy.wait()
        for t, parts, has_acc, _ in plan:
            if i not in parts:
                continue
            x = chunks[t, i][...]
            for j in range(2):
                at = slice(j * columns, (j + 1) * columns)
                product = jnp.dot(x, slots[n, j], preferred_element_type=F32)
                if i != parts[0]:
                    product += outs[t][:, at]
                elif has_acc:
                    product += accs[t][:, at]
                outs[t][:, at] = product
    for t in stats:
        own, beside = outs[t][:, :columns], outs[t][:, columns:]
        stats[t][...] = row_stats(own, beside, wanted[t][...], meta[n_voc], meta[n_voc + 1])
    if fresh:
        kept.wait()


def logits_call(plan, work, meta, part, n_voc, far=None):
    columns = work.shape[1]
    accs = [acc for _, _, acc, _ in plan if acc is not None]
    wanted = [w for _, _, _, w in plan if w is not None]
    chunks = [parts[i] for _, parts, _, _ in plan for i in sorted(parts)]
    rows = chunks[0].shape[0]
    out_shape = []
    for _, _, _, w in plan:
        out_shape.append(shape_of((rows, 2 * columns), F32))
        if w is not None:
            out_shape.append(shape_of((8, rows), F32))
    out_specs = [IN_VMEM] * len(out_shape)
    kernel_plan = [(t, sorted(parts), acc is not None, w is not None) for t, parts, acc, w in plan]
    n_used = len({i for _, parts, _, _ in plan for i in parts})
    fresh = far is not None
    in_place = [work] + ([far] if fresh else [])
    if fresh:
        out_shape.append(shape_of(work.shape, work.dtype))
        out_specs.append(IN_PLACE)
    operands = chunks + accs + wanted
    return pl.pallas_call(
        functools.partial(logits_kernel, kernel_plan, columns, part, n_voc, fresh),
        out_shape=out_shape,
        in_specs=[IN_SMEM] + [IN_PLACE] * len(in_place) + [IN_VMEM] * len(operands),
        out_specs=out_specs,
        scratch_shapes=[pltpu.VMEM((n_used, 2, part, columns), BF16), pltpu.SemaphoreType.DMA((n_used + fresh, 2))],
        input_output_aliases={1: len(out_shape) - 1} if fresh else {},
        compiler_params=params(),
        cost_estimate=cost(4 * len(chunks) * rows * part * columns, n_used * 4 * part * columns),
    )(meta, *in_place, *operands)


def spread(flipped_own, flipped_far, w_own, w_far, kept, send):
    rows = kept.shape[1]
    here = jnp.dot(w_own, flipped_own, preferred_element_type=F32)
    here += jnp.dot(w_far, flipped_far, preferred_element_type=F32)
    kept[...] = here[:, :rows]
    for t, out in enumerate(send, 1):
        out[...] = here[:, t * rows:(t + 1) * rows].astype(BF16)


def grads_kernel(n_blocks, n_stats, columns, part, width, window, meta, start, sums, refer, cotangent, work, *refs):
    refs = list(refs)
    logits = [refs.pop(0) for _ in range(n_blocks)]
    target = refs.pop(0)
    stats = [refs.pop(0) for _ in range(n_stats)]
    slots, sems = refs[-2:]
    grads_own, grads_far, flipped_own, flipped_far, loss, kept = refs[:6]
    send = refs[6:-2]
    coming = fetch(work, width, pl.multiple_of(meta[0] * part, part), part, slots, 0, sems)
    rows = logits[0].shape[0]
    pair, me_ctx = meta[3], meta[4]
    top = stats[0][0:1, :]
    for s in stats[1:]:
        top = jnp.maximum(top, s[0:1, :])
    total = jnp.zeros_like(top)
    picked = jnp.zeros_like(top)
    for s in stats:
        total += s[1:2, :] * jnp.exp(s[0:1, :] - top)
        picked += s[2:3, :]
    row = lax.broadcasted_iota(jnp.int32, (1, rows), 1)
    masks = []
    for t in range(n_blocks):
        block = lax.rem(me_ctx + (n_blocks - t), n_blocks)
        seen = lax.rem(row, window) + block * window >= start[pair]
        masks.append(jnp.where(seen, jnp.where(row < window, 1.0, -1.0), 0.0))
    signed_mask = jnp.concatenate(masks, axis=1)
    token_logp = picked - top - jnp.log(total)
    offset = (sums[pair, 0] - refer[pair, 0]) - (sums[pair, 1] - refer[pair, 1])
    zeros = jnp.zeros((1, 128), F32)
    margin = BETA * (jnp.sum(signed_mask * token_logp, axis=1, keepdims=True) + (zeros + offset))
    loss[...] = jnp.maximum(-margin, 0.0) + jnp.log1p(jnp.exp(-jnp.abs(margin)))
    factor = -BETA * (1.0 / (1.0 + jnp.exp(margin))) * cotangent[pair]
    weight = factor[:, 0:1] * signed_mask
    lines = lax.broadcasted_iota(jnp.int32, (128, top.shape[1]), 0)
    packed = jnp.where(lines == 0, top, jnp.where(lines == 1, weight, 1.0 / total)).T
    for t in range(n_blocks):
        at = slice(t * rows, (t + 1) * rows)
        top_t, weight_t, inverse_t = packed[at, 0:1], packed[at, 1:2], packed[at, 2:3]
        wanted = target[at, :]
        for j, (grads, flipped) in enumerate(((grads_own, flipped_own), (grads_far, flipped_far))):
            l = logits[t][:, j * columns:(j + 1) * columns]
            column = lax.broadcasted_iota(jnp.int32, l.shape, 1) + meta[1 + j]
            hit = jnp.where(column == wanted, 1.0, 0.0)
            g = weight_t * (hit - jnp.exp(l - top_t) * inverse_t)
            grads[t] = g.astype(BF16)
            flipped[:, at] = g.T.astype(BF16)
    for copy in coming:
        copy.wait()
    spread(flipped_own[...], flipped_far[...], slots[0, 0], slots[0, 1], kept, send)


def spread_kernel(part, width, n_parts, meta, work, flipped_own, flipped_far, *refs):
    outs, slots, sems = refs[:-2], refs[-2], refs[-1]
    each = len(outs) // n_parts
    coming = [
        fetch(work, width, pl.multiple_of(meta[i] * part, part), part, slots, i, sems) for i in range(n_parts)
    ]
    for i in range(n_parts):
        for copy in coming[i]:
            copy.wait()
        kept, *send = outs[i * each:(i + 1) * each]
        spread(flipped_own[...], flipped_far[...], slots[i, 0], slots[i, 1], kept, send)


def spread_shapes(n_blocks, rows, part):
    return [shape_of((part, rows), F32)] + [shape_of((part, rows), BF16)] * (n_blocks - 1)


def weight_slots(n_parts, part, columns):
    return [pltpu.VMEM((n_parts, 2, part, columns), BF16), pltpu.SemaphoreType.DMA((n_parts, 2))]


def grads_call(logits, target, stats, small, work, meta, part, width, window):
    n_blocks, rows, columns = len(logits), logits[0].shape[0], work.shape[1]
    grads = shape_of((n_blocks, rows, columns), BF16)
    flipped = shape_of((columns, n_blocks * rows), BF16)
    out_shape = [grads, grads, flipped, flipped, shape_of((1, 128), F32)] + spread_shapes(n_blocks, rows, part)
    operands = list(logits) + [target] + list(stats)
    return pl.pallas_call(
        functools.partial(grads_kernel, n_blocks, len(stats), columns, part, width, window),
        out_shape=out_shape,
        in_specs=[IN_SMEM] * 5 + [IN_PLACE] + [IN_VMEM] * len(operands),
        out_specs=[IN_VMEM] * len(out_shape),
        scratch_shapes=weight_slots(1, part, columns),
        compiler_params=params(),
        cost_estimate=cost(4 * n_blocks * rows * part * columns, 8 * part * columns),
    )(meta, *small, work, *operands)


def spread_call(flipped_own, flipped_far, work, k_ids, part, width, rows):
    columns, n_rows = flipped_own.shape
    n_parts = len(k_ids)
    out_shape = spread_shapes(n_rows // rows, rows, part) * n_parts
    outs = pl.pallas_call(
        functools.partial(spread_kernel, part, width, n_parts),
        out_shape=out_shape,
        in_specs=[IN_SMEM] + [IN_PLACE] + [IN_VMEM] * 2,
        out_specs=[IN_VMEM] * len(out_shape),
        scratch_shapes=weight_slots(n_parts, part, columns),
        compiler_params=params(),
        cost_estimate=cost(4 * n_parts * n_rows * part * columns, 4 * n_parts * part * columns),
    )(jnp.stack(k_ids).astype(jnp.int32), work, flipped_own, flipped_far)
    each = len(outs) // n_parts
    return [(outs[i * each], list(outs[i * each + 1:(i + 1) * each])) for i in range(n_parts)]


def add_kernel(turned, kept, *refs):
    total = kept[...]
    for a in refs[:-1]:
        total += a[...].astype(F32)
    refs[-1][...] = (total.T if turned else total).astype(BF16)


def add_call(kept, arrived, turned=False):
    shape = kept.shape[::-1] if turned else kept.shape
    return pl.pallas_call(
        functools.partial(add_kernel, turned),
        out_shape=shape_of(shape, BF16),
        in_specs=[IN_VMEM] * (1 + len(arrived)),
        out_specs=IN_VMEM,
        compiler_params=params(),
        cost_estimate=cost(kept.size, 4 * kept.size),
    )(kept, *arrived)


def head_kernel(slots_here, near_keys, far_keys, part, has_out, meta, *refs):
    refs = list(refs)
    grads = [refs.pop(0), refs.pop(0)]
    near = {k: refs.pop(0) for k in near_keys}
    stacks = [refs.pop(0) for _ in far_keys]
    far = {k: stack.at[i] for stack, keys in zip(stacks, far_keys) for i, k in enumerate(keys)}
    out, ready, sems = refs[has_out:]
    n_blocks, rows, columns = grads[0].shape
    right = jnp.concatenate([g[...].reshape(n_blocks * rows, columns) for g in grads])
    copies = []
    for n, i in enumerate(slots_here):
        left = jnp.concatenate([x[t, i][...] for x in (near, far) for t in range(n_blocks)])
        product = lax.dot_general(left, right, (((0,), (0,)), ((), ())), preferred_element_type=F32)
        if n >= 2:
            copies[n - 2].wait()
        ready[n % 2] = product.astype(BF16)
        start = pl.multiple_of(meta[i] * part, part)
        copies.append(pltpu.make_async_copy(ready.at[n % 2], out.at[pl.ds(start, part), :], sems.at[n % 2]))
        copies[-1].start()
    for copy in copies[-2:]:
        copy.wait()


def head_call(slots_here, near, far, grads, meta, out=None):
    n_blocks, rows, columns = grads[0].shape
    n_parts = len(near) // n_blocks
    part = near[0, 0].shape[1]
    near = {k: c for k, c in near.items() if k[1] in slots_here}
    far = [(keys, stack) for keys, stack in far if any(k[1] in slots_here for k in keys)]
    operands = list(grads) + list(near.values()) + [stack for _, stack in far]
    here = [] if out is None else [out]
    return pl.pallas_call(
        functools.partial(head_kernel, slots_here, list(near), [keys for keys, _ in far], part, len(here)),
        out_shape=shape_of((n_parts * part, columns), BF16),
        in_specs=[IN_SMEM] + [IN_VMEM] * len(operands) + [IN_PLACE] * len(here),
        out_specs=IN_PLACE,
        scratch_shapes=[pltpu.VMEM((2, part, columns), BF16), pltpu.SemaphoreType.DMA((2,))],
        input_output_aliases={1 + len(operands): 0} if here else {},
        compiler_params=pltpu.CompilerParams(vmem_limit_bytes=16 * 1024 * 1024),
        cost_estimate=cost(
            4 * n_blocks * rows * len(slots_here) * part * columns,
            4 * n_blocks * len(slots_here) * rows * part + 2 * len(slots_here) * part * columns,
        ),
    )(meta, *operands, *here)


def together(*groups):
    flat = lax.optimization_barrier([a for group in groups for a in group])
    out = []
    for group in groups:
        out.append(flat[:len(group)])
        flat = flat[len(group):]
    return out


def shards(hidden, head_weight, targets, response_start, other_sums, ref_logp, loss_cotangent):
    n_voc, n_ctx, n_dp = lax.axis_size("vocab"), lax.axis_size("ctx"), lax.axis_size("dp")
    me_voc, me_ctx, me_dp = lax.axis_index("vocab"), lax.axis_index("ctx"), lax.axis_index("dp")
    part, _, sides, window = hidden.shape
    rows = sides * window
    columns = head_weight.shape[1]
    line = n_voc == 4
    beyond = list(range(1, n_ctx))
    dp_swap = lambda a: lax.ppermute(a, "dp", ring(n_dp, 1))
    along = lambda a, by: lax.ppermute(a, "vocab", by)

    if line:
        table = [[0, 1, 2, 3], [1, 0, 2, 3], [2, 3, 1, 0], [3, 2, 1, 0]]
        part_of = [sum(jnp.where(me_voc == z, table[z][i], 0) for z in range(n_voc)) for i in range(n_voc)]
    else:
        part_of = [(me_voc - s) % n_voc for s in range(n_voc)]
    firsts = [
        ((me_voc * n_ctx + me_ctx) * n_dp + owner) * columns for owner in (me_dp, (me_dp + 1) % n_dp)
    ]
    meta = jnp.stack(part_of + firsts).astype(jnp.int32)

    far_weights = dp_swap(head_weight)
    work = hold(head_weight)
    width = head_weight.shape[0]

    pair = lax.broadcasted_iota(jnp.int32, targets.shape, 0)

    def by_block(all_targets):
        mine = jnp.sum(jnp.where(pair == me_dp, all_targets, 0), axis=0)
        blocks = [mine[:, b * window:(b + 1) * window].reshape(rows) for b in range(n_ctx)]
        wanted = []
        for t in range(n_ctx):
            at = (me_ctx - t) % n_ctx
            wanted.append(sum(jnp.where(at == b, blocks[b], 0) for b in range(n_ctx))[:, None])
        return wanted

    own = hidden.transpose(1, 2, 3, 0).reshape(rows, part)
    final = n_voc - 1
    call = functools.partial(logits_call, meta=meta, part=part, n_voc=n_voc)
    cross = lambda a: [lax.ppermute(a, "ctx", ring(n_ctx, t)) for t in beyond]
    chunk = {}

    def arrive(i, near, over):
        chunk[0, i] = near
        for t, a in zip(beyond, over):
            chunk[t, i] = a

    def first_logits(work):
        plan = [(0, {j: chunk[0, j] for j in (0, 1)}, None, None)]
        plan += [(t, {0: chunk[t, 0]}, None, None) for t in beyond]
        *logits, work = call(plan, work, far=far_weights)
        return logits, work

    def more_logits(i, logits):
        plan = [(0, {i: chunk[0, i]}, logits[0], None)]
        plan += [(t, {i - 1: chunk[t, i - 1]}, logits[t], None) for t in beyond]
        return call(plan, work)

    arrive(0, own, cross(own))
    if line:
        first = along(own, PAIRS_OUT)
        inner = along(own, PAIR_IN)
        (first, inner), (work,) = together([first, inner], [work])
        over = cross(first)
        outer, inner_last = along(inner, TO_ENDS), along(first, PAIR_IN)
        arrive(1, first, over)
        logits, work = first_logits(work)
        over, (inner, outer, inner_last), logits = together(over, [inner, outer, inner_last], logits)
        arrive(1, first, over)
        arrive(2, inner + outer, cross(inner + outer))
        outer = along(inner_last, TO_ENDS)
        (inner_last, outer), logits = together([inner_last, outer], more_logits(2, logits))
        last = inner_last + outer
    else:
        near = [own] + [along(own, ring(n_voc, i)) for i in range(1, n_voc)]
        logits = None
        for i in range(1, final):
            arrive(i, near[i], cross(near[i]))
            if logits is None:
                logits, work = first_logits(work)
            else:
                logits = more_logits(i, logits)
            (near[i + 1],), logits = together([near[i + 1]], logits)
        last = near[final]
    arrive(final, last, cross(last))
    (raw_targets,), _ = together([targets], logits)
    wanted = by_block(raw_targets)
    target = jnp.concatenate(wanted)

    done = call(
        [(0, {final: chunk[0, final]}, logits[0], wanted[0])]
        + [(t, {final - 1: chunk[t, final - 1]}, logits[t], None) for t in beyond],
        work,
    )
    logits, stats = [done[0]] + list(done[2:]), [done[1]]
    done = call([(t, {final: chunk[t, final]}, logits[t], wanted[t]) for t in beyond], work)
    logits = [logits[0]] + list(done[0::2])
    stats = stats + list(done[1::2])

    late = [(t, final) for t in beyond]
    soon = [k for k in chunk if k not in late]
    far_soon = dp_swap(jnp.stack(together([chunk[k] for k in soon], [stats[0]])[0]))

    def merge(seen):
        merged = []
        for b in range(n_ctx):
            these = [s[(b - t) % n_ctx] for t, s in seen]
            top = these[0][0]
            for s in these[1:]:
                top = jnp.maximum(top, s[0])
            total = sum(s[1] * jnp.exp(s[0] - top) for s in these)
            picked = sum(s[2] for s in these)
            merged.append(jnp.pad(jnp.stack([top, total, picked]), ((0, 5), (0, 0))))
        return jnp.concatenate(merged, axis=1)

    stats = jnp.stack(stats)
    if line and n_ctx == 2:
        corner = [(2 * a + c, 2 * b + (1 - c)) for a, b in PAIRS_OUT for c in range(2)]
        diagonal = lax.ppermute(stats, ("vocab", "ctx"), corner)
        merged = merge([(0, stats), (1, cross(stats)[0]), (0, along(stats, PAIRS_OUT)), (1, diagonal)])
        all_stats = [merged, along(merged, SWAP_HALVES)]
    else:
        merged = merge([(0, stats)] + list(zip(beyond, cross(stats))))
        all_stats = [merged] + [along(merged, ring(n_voc, s)) for s in range(1, n_voc)]

    meta_grads = jnp.stack([part_of[final]] + firsts + [me_dp, me_ctx]).astype(jnp.int32)
    small = (response_start, other_sums, ref_logp, loss_cotangent)
    grads_own, grads_far, flipped_own, flipped_far, loss, kept, *send = grads_call(
        logits, target, all_stats, small, work, meta_grads, part, width, window
    )
    theirs = dp_swap(grads_far)
    far_late = dp_swap(jnp.stack(together([chunk[k] for k in late], [kept])[0]))
    back = lambda cs: [lax.ppermute(c, "ctx", ring(n_ctx, -t)) for t, c in zip(beyond, cs)]
    shares = {final: (kept, list(send))}
    leave = list(range(final))[::-1]
    for i, share in zip(leave, spread_call(flipped_own, flipped_far, work, [part_of[i] for i in leave], part, width, rows)):
        shares[i] = share

    over = {}
    near_over = lambda i, *more: add_call(shares[i][0], over[i] + list(more))
    head = functools.partial(head_call, near=chunk, far=[(soon, far_soon), (late, far_late)], meta=meta)
    early, rest = list(range(n_voc // 2)), list(range(n_voc // 2, n_voc))
    landed, grad_head = [], None
    for i in range(n_voc)[::-1]:
        over[i] = back(shares[i][1])
        came, beside = [], []
        if not line:
            came = [along(near_over(i + 1), ring(n_voc, -(i + 1)))] if i < final else []
        elif i == 2:
            came = [along(near_over(3), FROM_ENDS)]
        elif i == 1:
            came = [along(near_over(3, landed[0]), PAIR_IN), along(near_over(2), FROM_ENDS)]
        elif i == 0:
            came = [along(near_over(1, landed[0]), PAIRS_OUT), along(near_over(2, landed[1]), PAIR_IN)]
        if i == 0:
            beside = [head(rest, grads=[grads_own, theirs], out=grad_head)]
        elif i == 1:
            beside = [head(early, grads=[grads_own, theirs])]
        elif i == final:
            beside = [a for j in leave for a in [shares[j][0]] + shares[j][1]]
        elif i == final - 1:
            beside = [theirs, far_late]
        over[i], came, beside = together(over[i], came, beside)
        landed = came if line else landed + came
        if i <= 1:
            grad_head, = beside
        elif i == final:
            for j in leave:
                shares[j] = (beside[0], beside[1:n_ctx])
                beside = beside[n_ctx:]
        elif i == final - 1:
            theirs, far_late = beside
            head = functools.partial(head_call, near=chunk, far=[(soon, far_soon), (late, far_late)], meta=meta)
    kept = shares[0][0]
    summed = add_call(kept, over[0] + landed, turned=True)
    grad_hidden = summed.reshape(1, sides, window, part).transpose(3, 0, 1, 2)

    far_loss = dp_swap(loss)
    owner = lax.broadcasted_iota(jnp.int32, (n_dp,), 0)
    pair_loss = jnp.where(owner == me_dp, loss[0, :n_dp], far_loss[0, :n_dp])
    return (grad_hidden, grad_head, pair_loss)


def solution(mesh):
    placed = (
        P("vocab", ("groups", "dp"), None, "ctx"),
        P(None, ("vocab", "ctx", "dp")),
        P("groups", None, None),
        P("groups"),
        P("groups", None),
        P("groups", None),
        P("groups"),
    )
    return jax.shard_map(
        shards,
        mesh=mesh,
        in_specs=placed,
        out_specs=(
            P("vocab", ("groups", "dp"), None, "ctx"),
            P("groups", ("vocab", "ctx", "dp")),
            P("groups"),
        ),
        check_vma=False,
    )
```

```python
import functools

import jax
import jax.numpy as jnp
from jax import lax
from jax.experimental import pallas as pl
from jax.experimental.pallas import tpu as pltpu
from jax.sharding import PartitionSpec as P

BETA = 0.1
F32, BF16 = jnp.float32, jnp.bfloat16
VMEM_BYTES = 16 * 1024 * 1024
WORK_BYTES = 52 * 1024 * 1024
IN_VMEM = pl.BlockSpec(memory_space=pltpu.VMEM)
IN_SMEM = pl.BlockSpec(memory_space=pltpu.SMEM)
IN_PLACE = pl.BlockSpec(memory_space=pl.ANY)
PAIRS_OUT = [(0, 1), (1, 0), (2, 3), (3, 2)]
PAIR_IN = [(1, 2), (2, 1)]
TO_ENDS = [(1, 0), (2, 3)]
FROM_ENDS = [(0, 1), (3, 2)]
SWAP_HALVES = [(0, 2), (2, 0), (1, 3), (3, 1)]


def ring(count, shift):
    return [(i, (i + shift) % count) for i in range(count)]


def params():
    return pltpu.CompilerParams(vmem_limit_bytes=VMEM_BYTES)


def cost(flops, moved):
    return pl.CostEstimate(flops=int(flops), bytes_accessed=int(moved), transcendentals=0)


def shape_of(shape, kind):
    return jax.ShapeDtypeStruct(shape, kind)


def work_shape(w):
    times = max(2, -(-WORK_BYTES // (w.size * w.dtype.itemsize)))
    return shape_of((times * w.shape[0], w.shape[1]), w.dtype)


def hold_kernel(w, out, sem):
    copy = pltpu.make_async_copy(w, out.at[pl.ds(0, w.shape[0]), :], sem)
    copy.start()
    copy.wait()


def hold(w):
    return pl.pallas_call(
        hold_kernel,
        out_shape=work_shape(w),
        in_specs=[IN_PLACE],
        out_specs=IN_PLACE,
        scratch_shapes=[pltpu.SemaphoreType.DMA],
        compiler_params=params(),
        cost_estimate=cost(1, 4 * w.size),
    )(w)


def fetch(work, width, start, part, slots, i, sems, own_only=False):
    copies = []
    for j in range(1 if own_only else 2):
        source = work.at[pl.ds(j * width + start, part), :]
        copies.append(pltpu.make_async_copy(source, slots.at[i, j], sems.at[i, j]))
        copies[-1].start()
    return copies


def row_stats(own, far, wanted, first_own, first_far):
    top = jnp.max(jnp.maximum(own, far), axis=1, keepdims=True)
    total = jnp.sum(jnp.exp(own - top) + jnp.exp(far - top), axis=1, keepdims=True)
    column = lax.broadcasted_iota(jnp.int32, own.shape, 1)
    zero = jnp.zeros_like(own)
    picked = jnp.sum(
        jnp.where(column + first_own == wanted, own, zero) + jnp.where(column + first_far == wanted, far, zero),
        axis=1,
        keepdims=True,
    )
    lane = lax.broadcasted_iota(jnp.int32, (own.shape[0], 128), 1)
    return jnp.where(lane == 0, top, jnp.where(lane == 1, total, picked)).T[:8, :]


def logits_kernel(plan, columns, part, n_voc, fresh, meta, work, *refs):
    refs = list(refs)
    width = part * n_voc
    far = refs.pop(0) if fresh else None
    chunks = {(t, i): refs.pop(0) for t, parts, _, _ in plan for i in parts}
    accs = {t: refs.pop(0) for t, _, has_acc, _ in plan if has_acc}
    wanted = {t: refs.pop(0) for t, _, _, done in plan if done}
    used = sorted({i for _, parts, _, _ in plan for i in parts})
    starts = [pl.multiple_of(meta[i] * part, part) for i in used]
    if fresh:
        held, far_sems = refs[-2:]
        refs = refs[:-2]
        into = pltpu.make_async_copy(far, held, far_sems.at[0])
        into.start()
    slots, sems = refs[-2:]
    coming = [fetch(work, width, start, part, slots, n, sems, fresh) for n, start in enumerate(starts)]
    if fresh:
        into.wait()
        kept = pltpu.make_async_copy(held, refs[-3].at[pl.ds(width, width), :], far_sems.at[1])
        kept.start()
    outs = {}
    stats = {}
    for t, _, _, done in plan:
        outs[t] = refs.pop(0)
        if done:
            stats[t] = refs.pop(0)
    for n, i in enumerate(used):
        for copy in coming[n]:
            copy.wait()
        for t, parts, has_acc, _ in plan:
            if i not in parts:
                continue
            x = chunks[t, i][...]
            for j in range(2):
                at = slice(j * columns, (j + 1) * columns)
                w = held[pl.ds(starts[n], part), :] if fresh and j else slots[n, j]
                product = jnp.dot(x, w, preferred_element_type=F32)
                if i != parts[0]:
                    product += outs[t][:, at]
                elif has_acc:
                    product += accs[t][:, at]
                outs[t][:, at] = product
    for t in stats:
        own, beside = outs[t][:, :columns], outs[t][:, columns:]
        stats[t][...] = row_stats(own, beside, wanted[t][...], meta[n_voc], meta[n_voc + 1])
    if fresh:
        kept.wait()


def logits_call(plan, work, meta, part, n_voc, far=None):
    columns = work.shape[1]
    accs = [acc for _, _, acc, _ in plan if acc is not None]
    wanted = [w for _, _, _, w in plan if w is not None]
    chunks = [parts[i] for _, parts, _, _ in plan for i in sorted(parts)]
    rows = chunks[0].shape[0]
    out_shape = []
    for _, _, _, w in plan:
        out_shape.append(shape_of((rows, 2 * columns), F32))
        if w is not None:
            out_shape.append(shape_of((8, rows), F32))
    out_specs = [IN_VMEM] * len(out_shape)
    kernel_plan = [(t, sorted(parts), acc is not None, w is not None) for t, parts, acc, w in plan]
    n_used = len({i for _, parts, _, _ in plan for i in parts})
    fresh = far is not None
    in_place = [work] + ([far] if fresh else [])
    if fresh:
        out_shape.append(shape_of(work.shape, work.dtype))
        out_specs.append(IN_PLACE)
    operands = chunks + accs + wanted
    return pl.pallas_call(
        functools.partial(logits_kernel, kernel_plan, columns, part, n_voc, fresh),
        out_shape=out_shape,
        in_specs=[IN_SMEM] + [IN_PLACE] * len(in_place) + [IN_VMEM] * len(operands),
        out_specs=out_specs,
        scratch_shapes=[pltpu.VMEM((n_used, 2 - fresh, part, columns), BF16), pltpu.SemaphoreType.DMA((n_used, 2))]
        + ([pltpu.VMEM((part * n_voc, columns), BF16), pltpu.SemaphoreType.DMA((2,))] if fresh else []),
        input_output_aliases={1: len(out_shape) - 1} if fresh else {},
        compiler_params=params(),
        cost_estimate=cost(4 * len(chunks) * rows * part * columns, n_used * 4 * part * columns),
    )(meta, *in_place, *operands)


def spread(flipped_own, flipped_far, w_own, w_far, kept, send):
    rows = kept.shape[1]
    here = jnp.dot(w_own, flipped_own, preferred_element_type=F32)
    here += jnp.dot(w_far, flipped_far, preferred_element_type=F32)
    kept[...] = here[:, :rows]
    for t, out in enumerate(send, 1):
        out[...] = here[:, t * rows:(t + 1) * rows].astype(BF16)


def grads_kernel(n_blocks, n_stats, columns, part, width, window, meta, start, sums, refer, cotangent, work, *refs):
    refs = list(refs)
    logits = [refs.pop(0) for _ in range(n_blocks)]
    target = refs.pop(0)
    stats = [refs.pop(0) for _ in range(n_stats)]
    slots, sems = refs[-2:]
    grads_own, grads_far, flipped_own, flipped_far, loss, kept = refs[:6]
    send = refs[6:-2]
    coming = fetch(work, width, pl.multiple_of(meta[0] * part, part), part, slots, 0, sems)
    rows = logits[0].shape[0]
    pair, me_ctx = meta[3], meta[4]
    top = stats[0][0:1, :]
    for s in stats[1:]:
        top = jnp.maximum(top, s[0:1, :])
    total = jnp.zeros_like(top)
    picked = jnp.zeros_like(top)
    for s in stats:
        total += s[1:2, :] * jnp.exp(s[0:1, :] - top)
        picked += s[2:3, :]
    row = lax.broadcasted_iota(jnp.int32, (1, rows), 1)
    masks = []
    for t in range(n_blocks):
        block = lax.rem(me_ctx + (n_blocks - t), n_blocks)
        seen = lax.rem(row, window) + block * window >= start[pair]
        masks.append(jnp.where(seen, jnp.where(row < window, 1.0, -1.0), 0.0))
    signed_mask = jnp.concatenate(masks, axis=1)
    token_logp = picked - top - jnp.log(total)
    offset = (sums[pair, 0] - refer[pair, 0]) - (sums[pair, 1] - refer[pair, 1])
    zeros = jnp.zeros((1, 128), F32)
    margin = BETA * (jnp.sum(signed_mask * token_logp, axis=1, keepdims=True) + (zeros + offset))
    loss[...] = jnp.maximum(-margin, 0.0) + jnp.log1p(jnp.exp(-jnp.abs(margin)))
    factor = -BETA * (1.0 / (1.0 + jnp.exp(margin))) * cotangent[pair]
    weight = factor[:, 0:1] * signed_mask
    lines = lax.broadcasted_iota(jnp.int32, (128, top.shape[1]), 0)
    packed = jnp.where(lines == 0, top, jnp.where(lines == 1, weight, 1.0 / total)).T
    for t in range(n_blocks):
        at = slice(t * rows, (t + 1) * rows)
        top_t, weight_t, inverse_t = packed[at, 0:1], packed[at, 1:2], packed[at, 2:3]
        wanted = target[at, :]
        for j, (grads, flipped) in enumerate(((grads_own, flipped_own), (grads_far, flipped_far))):
            l = logits[t][:, j * columns:(j + 1) * columns]
            column = lax.broadcasted_iota(jnp.int32, l.shape, 1) + meta[1 + j]
            hit = jnp.where(column == wanted, 1.0, 0.0)
            g = weight_t * (hit - jnp.exp(l - top_t) * inverse_t)
            grads[t] = g.astype(BF16)
            flipped[:, at] = g.T.astype(BF16)
    for copy in coming:
        copy.wait()
    spread(flipped_own[...], flipped_far[...], slots[0, 0], slots[0, 1], kept, send)


def spread_kernel(part, width, n_parts, meta, work, flipped_own, flipped_far, *refs):
    outs, slots, sems = refs[:-2], refs[-2], refs[-1]
    each = len(outs) // n_parts
    coming = [
        fetch(work, width, pl.multiple_of(meta[i] * part, part), part, slots, i, sems) for i in range(n_parts)
    ]
    for i in range(n_parts):
        for copy in coming[i]:
            copy.wait()
        kept, *send = outs[i * each:(i + 1) * each]
        spread(flipped_own[...], flipped_far[...], slots[i, 0], slots[i, 1], kept, send)


def spread_shapes(n_blocks, rows, part):
    return [shape_of((part, rows), F32)] + [shape_of((part, rows), BF16)] * (n_blocks - 1)


def weight_slots(n_parts, part, columns):
    return [pltpu.VMEM((n_parts, 2, part, columns), BF16), pltpu.SemaphoreType.DMA((n_parts, 2))]


def grads_call(logits, target, stats, small, work, meta, part, width, window):
    n_blocks, rows, columns = len(logits), logits[0].shape[0], work.shape[1]
    grads = shape_of((n_blocks, rows, columns), BF16)
    flipped = shape_of((columns, n_blocks * rows), BF16)
    out_shape = [grads, grads, flipped, flipped, shape_of((1, 128), F32)] + spread_shapes(n_blocks, rows, part)
    operands = list(logits) + [target] + list(stats)
    return pl.pallas_call(
        functools.partial(grads_kernel, n_blocks, len(stats), columns, part, width, window),
        out_shape=out_shape,
        in_specs=[IN_SMEM] * 5 + [IN_PLACE] + [IN_VMEM] * len(operands),
        out_specs=[IN_VMEM] * len(out_shape),
        scratch_shapes=weight_slots(1, part, columns),
        compiler_params=params(),
        cost_estimate=cost(4 * n_blocks * rows * part * columns, 8 * part * columns),
    )(meta, *small, work, *operands)


def spread_call(flipped_own, flipped_far, work, k_ids, part, width, rows):
    columns, n_rows = flipped_own.shape
    n_parts = len(k_ids)
    out_shape = spread_shapes(n_rows // rows, rows, part) * n_parts
    outs = pl.pallas_call(
        functools.partial(spread_kernel, part, width, n_parts),
        out_shape=out_shape,
        in_specs=[IN_SMEM] + [IN_PLACE] + [IN_VMEM] * 2,
        out_specs=[IN_VMEM] * len(out_shape),
        scratch_shapes=weight_slots(n_parts, part, columns),
        compiler_params=params(),
        cost_estimate=cost(4 * n_parts * n_rows * part * columns, 4 * n_parts * part * columns),
    )(jnp.stack(k_ids).astype(jnp.int32), work, flipped_own, flipped_far)
    each = len(outs) // n_parts
    return [(outs[i * each], list(outs[i * each + 1:(i + 1) * each])) for i in range(n_parts)]


def add_kernel(turned, kept, *refs):
    total = kept[...]
    for a in refs[:-1]:
        total += a[...].astype(F32)
    refs[-1][...] = (total.T if turned else total).astype(BF16)


def add_call(kept, arrived, turned=False):
    shape = kept.shape[::-1] if turned else kept.shape
    return pl.pallas_call(
        functools.partial(add_kernel, turned),
        out_shape=shape_of(shape, BF16),
        in_specs=[IN_VMEM] * (1 + len(arrived)),
        out_specs=IN_VMEM,
        compiler_params=params(),
        cost_estimate=cost(kept.size, 4 * kept.size),
    )(kept, *arrived)


def head_kernel(slots_here, near_keys, far_keys, part, has_out, meta, *refs):
    refs = list(refs)
    grads = [refs.pop(0), refs.pop(0)]
    near = {k: refs.pop(0) for k in near_keys}
    stacks = [refs.pop(0) for _ in far_keys]
    far = {k: stack.at[i] for stack, keys in zip(stacks, far_keys) for i, k in enumerate(keys)}
    out, ready, sems = refs[has_out:]
    n_blocks, rows, columns = grads[0].shape
    right = jnp.concatenate([g[...].reshape(n_blocks * rows, columns) for g in grads])
    copies = []
    for n, i in enumerate(slots_here):
        left = jnp.concatenate([x[t, i][...] for x in (near, far) for t in range(n_blocks)])
        product = lax.dot_general(left, right, (((0,), (0,)), ((), ())), preferred_element_type=F32)
        if n >= 2:
            copies[n - 2].wait()
        ready[n % 2] = product.astype(BF16)
        start = pl.multiple_of(meta[i] * part, part)
        copies.append(pltpu.make_async_copy(ready.at[n % 2], out.at[pl.ds(start, part), :], sems.at[n % 2]))
        copies[-1].start()
    for copy in copies[-2:]:
        copy.wait()


def head_call(slots_here, near, far, grads, meta, out=None):
    n_blocks, rows, columns = grads[0].shape
    n_parts = len(near) // n_blocks
    part = near[0, 0].shape[1]
    near = {k: c for k, c in near.items() if k[1] in slots_here}
    far = [(keys, stack) for keys, stack in far if any(k[1] in slots_here for k in keys)]
    operands = list(grads) + list(near.values()) + [stack for _, stack in far]
    here = [] if out is None else [out]
    return pl.pallas_call(
        functools.partial(head_kernel, slots_here, list(near), [keys for keys, _ in far], part, len(here)),
        out_shape=shape_of((n_parts * part, columns), BF16),
        in_specs=[IN_SMEM] + [IN_VMEM] * len(operands) + [IN_PLACE] * len(here),
        out_specs=IN_PLACE,
        scratch_shapes=[pltpu.VMEM((2, part, columns), BF16), pltpu.SemaphoreType.DMA((2,))],
        input_output_aliases={1 + len(operands): 0} if here else {},
        compiler_params=pltpu.CompilerParams(vmem_limit_bytes=16 * 1024 * 1024),
        cost_estimate=cost(
            4 * n_blocks * rows * len(slots_here) * part * columns,
            4 * n_blocks * len(slots_here) * rows * part + 2 * len(slots_here) * part * columns,
        ),
    )(meta, *operands, *here)


def together(*groups):
    flat = lax.optimization_barrier([a for group in groups for a in group])
    out = []
    for group in groups:
        out.append(flat[:len(group)])
        flat = flat[len(group):]
    return out


def shards(hidden, head_weight, targets, response_start, other_sums, ref_logp, loss_cotangent):
    n_voc, n_ctx, n_dp = lax.axis_size("vocab"), lax.axis_size("ctx"), lax.axis_size("dp")
    me_voc, me_ctx, me_dp = lax.axis_index("vocab"), lax.axis_index("ctx"), lax.axis_index("dp")
    part, _, sides, window = hidden.shape
    rows = sides * window
    columns = head_weight.shape[1]
    line = n_voc == 4
    beyond = list(range(1, n_ctx))
    dp_swap = lambda a: lax.ppermute(a, "dp", ring(n_dp, 1))
    along = lambda a, by: lax.ppermute(a, "vocab", by)

    if line:
        table = [[0, 1, 2, 3], [1, 0, 2, 3], [2, 3, 1, 0], [3, 2, 1, 0]]
        part_of = [sum(jnp.where(me_voc == z, table[z][i], 0) for z in range(n_voc)) for i in range(n_voc)]
    else:
        part_of = [(me_voc - s) % n_voc for s in range(n_voc)]
    firsts = [
        ((me_voc * n_ctx + me_ctx) * n_dp + owner) * columns for owner in (me_dp, (me_dp + 1) % n_dp)
    ]
    meta = jnp.stack(part_of + firsts).astype(jnp.int32)

    far_weights = dp_swap(head_weight)
    work = hold(head_weight)
    width = head_weight.shape[0]

    pair = lax.broadcasted_iota(jnp.int32, targets.shape, 0)

    def by_block(all_targets):
        mine = jnp.sum(jnp.where(pair == me_dp, all_targets, 0), axis=0)
        blocks = [mine[:, b * window:(b + 1) * window].reshape(rows) for b in range(n_ctx)]
        wanted = []
        for t in range(n_ctx):
            at = (me_ctx - t) % n_ctx
            wanted.append(sum(jnp.where(at == b, blocks[b], 0) for b in range(n_ctx))[:, None])
        return wanted

    own = hidden.transpose(1, 2, 3, 0).reshape(rows, part)
    final = n_voc - 1
    call = functools.partial(logits_call, meta=meta, part=part, n_voc=n_voc)
    cross = lambda a: [lax.ppermute(a, "ctx", ring(n_ctx, t)) for t in beyond]
    chunk = {}

    def arrive(i, near, over):
        chunk[0, i] = near
        for t, a in zip(beyond, over):
            chunk[t, i] = a

    def first_logits(work):
        plan = [(0, {j: chunk[0, j] for j in (0, 1)}, None, None)]
        plan += [(t, {0: chunk[t, 0]}, None, None) for t in beyond]
        *logits, work = call(plan, work, far=far_weights)
        return logits, work

    def more_logits(i, logits):
        plan = [(0, {i: chunk[0, i]}, logits[0], None)]
        plan += [(t, {i - 1: chunk[t, i - 1]}, logits[t], None) for t in beyond]
        return call(plan, work)

    arrive(0, own, cross(own))
    if line:
        first = along(own, PAIRS_OUT)
        inner = along(own, PAIR_IN)
        (first, inner), (work,) = together([first, inner], [work])
        over = cross(first)
        outer, inner_last = along(inner, TO_ENDS), along(first, PAIR_IN)
        arrive(1, first, over)
        logits, work = first_logits(work)
        over, (inner, outer, inner_last), logits = together(over, [inner, outer, inner_last], logits)
        arrive(1, first, over)
        arrive(2, inner + outer, cross(inner + outer))
        outer = along(inner_last, TO_ENDS)
        (inner_last, outer), logits = together([inner_last, outer], more_logits(2, logits))
        last = inner_last + outer
    else:
        near = [own] + [along(own, ring(n_voc, i)) for i in range(1, n_voc)]
        logits = None
        for i in range(1, final):
            arrive(i, near[i], cross(near[i]))
            if logits is None:
                logits, work = first_logits(work)
            else:
                logits = more_logits(i, logits)
            (near[i + 1],), logits = together([near[i + 1]], logits)
        last = near[final]
    arrive(final, last, cross(last))
    (raw_targets,), _ = together([targets], logits)
    wanted = by_block(raw_targets)
    target = jnp.concatenate(wanted)

    done = call(
        [(0, {final: chunk[0, final]}, logits[0], wanted[0])]
        + [(t, {final - 1: chunk[t, final - 1]}, logits[t], None) for t in beyond],
        work,
    )
    logits, stats = [done[0]] + list(done[2:]), [done[1]]
    done = call([(t, {final: chunk[t, final]}, logits[t], wanted[t]) for t in beyond], work)
    logits = [logits[0]] + list(done[0::2])
    stats = stats + list(done[1::2])

    late = [(t, final) for t in beyond]
    soon = [k for k in chunk if k not in late]
    far_soon = dp_swap(jnp.stack(together([chunk[k] for k in soon], [stats[0]])[0]))

    def merge(seen):
        merged = []
        for b in range(n_ctx):
            these = [s[(b - t) % n_ctx] for t, s in seen]
            top = these[0][0]
            for s in these[1:]:
                top = jnp.maximum(top, s[0])
            total = sum(s[1] * jnp.exp(s[0] - top) for s in these)
            picked = sum(s[2] for s in these)
            merged.append(jnp.pad(jnp.stack([top, total, picked]), ((0, 5), (0, 0))))
        return jnp.concatenate(merged, axis=1)

    stats = jnp.stack(stats)
    if line and n_ctx == 2:
        corner = [(2 * a + c, 2 * b + (1 - c)) for a, b in PAIRS_OUT for c in range(2)]
        diagonal = lax.ppermute(stats, ("vocab", "ctx"), corner)
        merged = merge([(0, stats), (1, cross(stats)[0]), (0, along(stats, PAIRS_OUT)), (1, diagonal)])
        all_stats = [merged, along(merged, SWAP_HALVES)]
    else:
        merged = merge([(0, stats)] + list(zip(beyond, cross(stats))))
        all_stats = [merged] + [along(merged, ring(n_voc, s)) for s in range(1, n_voc)]

    meta_grads = jnp.stack([part_of[final]] + firsts + [me_dp, me_ctx]).astype(jnp.int32)
    small = (response_start, other_sums, ref_logp, loss_cotangent)
    grads_own, grads_far, flipped_own, flipped_far, loss, kept, *send = grads_call(
        logits, target, all_stats, small, work, meta_grads, part, width, window
    )
    theirs = dp_swap(grads_far)
    far_late = dp_swap(jnp.stack(together([chunk[k] for k in late], [kept])[0]))
    back = lambda cs: [lax.ppermute(c, "ctx", ring(n_ctx, -t)) for t, c in zip(beyond, cs)]
    shares = {final: (kept, list(send))}
    leave = list(range(final))[::-1]

    def more_shares(slots):
        done = spread_call(flipped_own, flipped_far, work, [part_of[i] for i in slots], part, width, rows)
        shares.update(zip(slots, done))
        return [a for i in slots for a in [shares[i][0]] + shares[i][1]]

    def set_shares(slots, flat):
        for i in slots:
            shares[i] = (flat[0], list(flat[1:n_ctx]))
            flat = flat[n_ctx:]

    over = {}
    near_over = lambda i, *more: add_call(shares[i][0], over[i] + list(more))
    head = functools.partial(head_call, near=chunk, far=[(soon, far_soon), (late, far_late)], meta=meta)
    early, rest = list(range(n_voc // 2)), list(range(n_voc // 2, n_voc))
    landed, grad_head = [], None
    for i in range(n_voc)[::-1]:
        over[i] = back(shares[i][1])
        came, beside = [], []
        if not line:
            came = [along(near_over(i + 1), ring(n_voc, -(i + 1)))] if i < final else []
        elif i == 2:
            came = [along(near_over(3), FROM_ENDS)]
        elif i == 1:
            came = [along(near_over(3, landed[0]), PAIR_IN), along(near_over(2), FROM_ENDS)]
        elif i == 0:
            came = [along(near_over(1, landed[0]), PAIRS_OUT), along(near_over(2, landed[1]), PAIR_IN)]
        if i == 0:
            beside = [head(rest, grads=[grads_own, theirs], out=grad_head)]
        elif i == 1:
            beside = [head(early, grads=[grads_own, theirs])]
        elif i == final:
            beside = more_shares(leave[:2])
        elif i == final - 1:
            beside = [theirs, far_late] + more_shares(leave[2:])
        sends = shares[i - 1][1] if i and i - 1 in shares else []
        over[i], came, beside, sends = together(over[i], came, beside, sends)
        landed = came if line else landed + came
        if i <= 1:
            grad_head, = beside
        elif i == final:
            set_shares(leave[:2], beside)
        elif i == final - 1:
            theirs, far_late = beside[:2]
            set_shares(leave[2:], beside[2:])
            head = functools.partial(head_call, near=chunk, far=[(soon, far_soon), (late, far_late)], meta=meta)
        if sends:
            shares[i - 1] = (shares[i - 1][0], list(sends))
    kept = shares[0][0]
    summed = add_call(kept, over[0] + landed, turned=True)
    grad_hidden = summed.reshape(1, sides, window, part).transpose(3, 0, 1, 2)

    far_loss = dp_swap(loss)
    owner = lax.broadcasted_iota(jnp.int32, (n_dp,), 0)
    pair_loss = jnp.where(owner == me_dp, loss[0, :n_dp], far_loss[0, :n_dp])
    return (grad_hidden, grad_head, pair_loss)


def solution(mesh):
    placed = (
        P("vocab", ("groups", "dp"), None, "ctx"),
        P(None, ("vocab", "ctx", "dp")),
        P("groups", None, None),
        P("groups"),
        P("groups", None),
        P("groups", None),
        P("groups"),
    )
    return jax.shard_map(
        shards,
        mesh=mesh,
        in_specs=placed,
        out_specs=(
            P("vocab", ("groups", "dp"), None, "ctx"),
            P("groups", ("vocab", "ctx", "dp")),
            P("groups"),
        ),
        check_vma=False,
    )
```

```python
import functools

import jax
import jax.numpy as jnp
from jax import lax
from jax.experimental import pallas as pl
from jax.experimental.pallas import tpu as pltpu
from jax.sharding import PartitionSpec as P

BETA = 0.1
F32, BF16 = jnp.float32, jnp.bfloat16
VMEM_BYTES = 16 * 1024 * 1024
WORK_BYTES = 52 * 1024 * 1024
IN_VMEM = pl.BlockSpec(memory_space=pltpu.VMEM)
IN_SMEM = pl.BlockSpec(memory_space=pltpu.SMEM)
IN_PLACE = pl.BlockSpec(memory_space=pl.ANY)
PAIRS_OUT = [(0, 1), (1, 0), (2, 3), (3, 2)]
PAIR_IN = [(1, 2), (2, 1)]
TO_ENDS = [(1, 0), (2, 3)]
FROM_ENDS = [(0, 1), (3, 2)]
SWAP_HALVES = [(0, 2), (2, 0), (1, 3), (3, 1)]


def ring(count, shift):
    return [(i, (i + shift) % count) for i in range(count)]


def params():
    return pltpu.CompilerParams(vmem_limit_bytes=VMEM_BYTES)


def cost(flops, moved):
    return pl.CostEstimate(flops=int(flops), bytes_accessed=int(moved), transcendentals=0)


def shape_of(shape, kind):
    return jax.ShapeDtypeStruct(shape, kind)


def work_shape(w):
    times = max(2, -(-WORK_BYTES // (w.size * w.dtype.itemsize)))
    return shape_of((times * w.shape[0], w.shape[1]), w.dtype)


def hold_kernel(w, out, sem):
    copy = pltpu.make_async_copy(w, out.at[pl.ds(0, w.shape[0]), :], sem)
    copy.start()
    copy.wait()


def hold(w):
    return pl.pallas_call(
        hold_kernel,
        out_shape=work_shape(w),
        in_specs=[IN_PLACE],
        out_specs=IN_PLACE,
        scratch_shapes=[pltpu.SemaphoreType.DMA],
        compiler_params=params(),
        cost_estimate=cost(1, 4 * w.size),
    )(w)


def fetch(work, width, start, part, slots, i, sems, own_only=False):
    copies = []
    for j in range(1 if own_only else 2):
        source = work.at[pl.ds(j * width + start, part), :]
        copies.append(pltpu.make_async_copy(source, slots.at[i, j], sems.at[i, j]))
        copies[-1].start()
    return copies


def row_stats(own, far, wanted, first_own, first_far):
    top = jnp.max(jnp.maximum(own, far), axis=1, keepdims=True)
    total = jnp.sum(jnp.exp(own - top) + jnp.exp(far - top), axis=1, keepdims=True)
    column = lax.broadcasted_iota(jnp.int32, own.shape, 1)
    zero = jnp.zeros_like(own)
    picked = jnp.sum(
        jnp.where(column + first_own == wanted, own, zero) + jnp.where(column + first_far == wanted, far, zero),
        axis=1,
        keepdims=True,
    )
    lane = lax.broadcasted_iota(jnp.int32, (own.shape[0], 128), 1)
    return jnp.where(lane == 0, top, jnp.where(lane == 1, total, picked)).T[:8, :]


def logits_kernel(plan, columns, part, n_voc, fresh, n_earlier, meta, work, *refs):
    refs = list(refs)
    width = part * n_voc
    far = refs.pop(0) if fresh else None
    chunks = {(t, i): refs.pop(0) for t, parts, _, _ in plan for i in parts}
    accs = {t: refs.pop(0) for t, _, has_acc, _ in plan if has_acc}
    wanted = {t: refs.pop(0) for t, _, _, done in plan if done}
    earlier = [refs.pop(0) for _ in range(n_earlier)]
    used = sorted({i for _, parts, _, _ in plan for i in parts})
    starts = [pl.multiple_of(meta[i] * part, part) for i in used]
    if fresh:
        held, far_sems = refs[-2:]
        refs = refs[:-2]
        into = pltpu.make_async_copy(far, held, far_sems.at[0])
        into.start()
    slots, sems = refs[-2:]
    coming = [fetch(work, width, start, part, slots, n, sems, fresh) for n, start in enumerate(starts)]
    if fresh:
        into.wait()
        kept = pltpu.make_async_copy(held, refs[-3].at[pl.ds(width, width), :], far_sems.at[1])
        kept.start()
    outs = {t: refs.pop(0) for t, _, _, _ in plan}
    for n, i in enumerate(used):
        for copy in coming[n]:
            copy.wait()
        for t, parts, has_acc, _ in plan:
            if i not in parts:
                continue
            x = chunks[t, i][...]
            for j in range(2):
                at = slice(j * columns, (j + 1) * columns)
                w = held[pl.ds(starts[n], part), :] if fresh and j else slots[n, j]
                product = jnp.dot(x, w, preferred_element_type=F32)
                if i != parts[0]:
                    product += outs[t][:, at]
                elif has_acc:
                    product += accs[t][:, at]
                outs[t][:, at] = product
    if wanted:
        stats = refs[0]
        for n, a in enumerate(earlier):
            stats[n] = a[0]
        for n, t in enumerate(wanted, n_earlier):
            own, beside = outs[t][:, :columns], outs[t][:, columns:]
            stats[n] = row_stats(own, beside, wanted[t][...], meta[n_voc], meta[n_voc + 1])
    if fresh:
        kept.wait()


def logits_call(plan, work, meta, part, n_voc, far=None, earlier=()):
    columns = work.shape[1]
    accs = [acc for _, _, acc, _ in plan if acc is not None]
    wanted = [w for _, _, _, w in plan if w is not None]
    chunks = [parts[i] for _, parts, _, _ in plan for i in sorted(parts)]
    rows = chunks[0].shape[0]
    out_shape = [shape_of((rows, 2 * columns), F32)] * len(plan)
    if wanted:
        out_shape.append(shape_of((len(earlier) + len(wanted), 8, rows), F32))
    out_specs = [IN_VMEM] * len(out_shape)
    kernel_plan = [(t, sorted(parts), acc is not None, w is not None) for t, parts, acc, w in plan]
    n_used = len({i for _, parts, _, _ in plan for i in parts})
    fresh = far is not None
    in_place = [work] + ([far] if fresh else [])
    if fresh:
        out_shape.append(shape_of(work.shape, work.dtype))
        out_specs.append(IN_PLACE)
    operands = chunks + accs + wanted + list(earlier)
    return pl.pallas_call(
        functools.partial(logits_kernel, kernel_plan, columns, part, n_voc, fresh, len(earlier)),
        out_shape=out_shape,
        in_specs=[IN_SMEM] + [IN_PLACE] * len(in_place) + [IN_VMEM] * len(operands),
        out_specs=out_specs,
        scratch_shapes=[pltpu.VMEM((n_used, 2 - fresh, part, columns), BF16), pltpu.SemaphoreType.DMA((n_used, 2))]
        + ([pltpu.VMEM((part * n_voc, columns), BF16), pltpu.SemaphoreType.DMA((2,))] if fresh else []),
        input_output_aliases={1: len(out_shape) - 1} if fresh else {},
        compiler_params=params(),
        cost_estimate=cost(4 * len(chunks) * rows * part * columns, n_used * 4 * part * columns),
    )(meta, *in_place, *operands)


def spread(flipped_own, flipped_far, w_own, w_far, kept, send):
    rows = kept.shape[1]
    here = jnp.dot(w_own, flipped_own, preferred_element_type=F32)
    here += jnp.dot(w_far, flipped_far, preferred_element_type=F32)
    kept[...] = here[:, :rows]
    for t, out in enumerate(send, 1):
        out[...] = here[:, t * rows:(t + 1) * rows].astype(BF16)


def grads_kernel(n_blocks, n_stats, columns, part, width, window, meta, small, work, *refs):
    refs = list(refs)
    logits = [refs.pop(0) for _ in range(n_blocks)]
    target = refs.pop(0)
    stats = [refs.pop(0) for _ in range(n_stats)]
    slots, sems = refs[-2:]
    grads_own, grads_far, flipped_own, flipped_far, loss, kept = refs[:6]
    send = refs[6:-2]
    coming = fetch(work, width, pl.multiple_of(meta[0] * part, part), part, slots, 0, sems)
    rows = logits[0].shape[0]
    me_ctx, start = meta[3], meta[4]
    top = stats[0][0:1, :]
    for s in stats[1:]:
        top = jnp.maximum(top, s[0:1, :])
    total = jnp.zeros_like(top)
    picked = jnp.zeros_like(top)
    for s in stats:
        total += s[1:2, :] * jnp.exp(s[0:1, :] - top)
        picked += s[2:3, :]
    row = lax.broadcasted_iota(jnp.int32, (1, rows), 1)
    masks = []
    for t in range(n_blocks):
        block = lax.rem(me_ctx + (n_blocks - t), n_blocks)
        seen = lax.rem(row, window) + block * window >= start
        masks.append(jnp.where(seen, jnp.where(row < window, 1.0, -1.0), 0.0))
    signed_mask = jnp.concatenate(masks, axis=1)
    token_logp = picked - top - jnp.log(total)
    zeros = jnp.zeros((1, 128), F32)
    margin = BETA * (jnp.sum(signed_mask * token_logp, axis=1, keepdims=True) + (zeros + small[0]))
    loss[...] = jnp.maximum(-margin, 0.0) + jnp.log1p(jnp.exp(-jnp.abs(margin)))
    factor = -BETA * (1.0 / (1.0 + jnp.exp(margin))) * small[1]
    weight = factor[:, 0:1] * signed_mask
    lines = lax.broadcasted_iota(jnp.int32, (128, top.shape[1]), 0)
    packed = jnp.where(lines == 0, top, jnp.where(lines == 1, weight, 1.0 / total)).T
    for t in range(n_blocks):
        at = slice(t * rows, (t + 1) * rows)
        top_t, weight_t, inverse_t = packed[at, 0:1], packed[at, 1:2], packed[at, 2:3]
        wanted = target[at, :]
        for j, (grads, flipped) in enumerate(((grads_own, flipped_own), (grads_far, flipped_far))):
            l = logits[t][:, j * columns:(j + 1) * columns]
            column = lax.broadcasted_iota(jnp.int32, l.shape, 1) + meta[1 + j]
            hit = jnp.where(column == wanted, 1.0, 0.0)
            g = weight_t * (hit - jnp.exp(l - top_t) * inverse_t)
            grads[t] = g.astype(BF16)
            flipped[:, at] = g.T.astype(BF16)
    for copy in coming:
        copy.wait()
    spread(flipped_own[...], flipped_far[...], slots[0, 0], slots[0, 1], kept, send)


def spread_kernel(part, width, n_parts, meta, work, flipped_own, flipped_far, *refs):
    outs, slots, sems = refs[:-2], refs[-2], refs[-1]
    each = len(outs) // n_parts
    coming = [
        fetch(work, width, pl.multiple_of(meta[i] * part, part), part, slots, i, sems) for i in range(n_parts)
    ]
    for i in range(n_parts):
        for copy in coming[i]:
            copy.wait()
        kept, *send = outs[i * each:(i + 1) * each]
        spread(flipped_own[...], flipped_far[...], slots[i, 0], slots[i, 1], kept, send)


def spread_shapes(n_blocks, rows, part):
    return [shape_of((part, rows), F32)] + [shape_of((part, rows), BF16)] * (n_blocks - 1)


def weight_slots(n_parts, part, columns):
    return [pltpu.VMEM((n_parts, 2, part, columns), BF16), pltpu.SemaphoreType.DMA((n_parts, 2))]


def grads_call(logits, target, stats, small, work, meta, part, width, window):
    n_blocks, rows, columns = len(logits), logits[0].shape[0], work.shape[1]
    grads = shape_of((n_blocks, rows, columns), BF16)
    flipped = shape_of((columns, n_blocks * rows), BF16)
    out_shape = [grads, grads, flipped, flipped, shape_of((1, 128), F32)] + spread_shapes(n_blocks, rows, part)
    operands = list(logits) + [target] + list(stats)
    return pl.pallas_call(
        functools.partial(grads_kernel, n_blocks, len(stats), columns, part, width, window),
        out_shape=out_shape,
        in_specs=[IN_SMEM] * 2 + [IN_PLACE] + [IN_VMEM] * len(operands),
        out_specs=[IN_VMEM] * len(out_shape),
        scratch_shapes=weight_slots(1, part, columns),
        compiler_params=params(),
        cost_estimate=cost(4 * n_blocks * rows * part * columns, 8 * part * columns),
    )(meta, small, work, *operands)


def spread_call(flipped_own, flipped_far, work, k_ids, part, width, rows):
    columns, n_rows = flipped_own.shape
    n_parts = len(k_ids)
    out_shape = spread_shapes(n_rows // rows, rows, part) * n_parts
    outs = pl.pallas_call(
        functools.partial(spread_kernel, part, width, n_parts),
        out_shape=out_shape,
        in_specs=[IN_SMEM] + [IN_PLACE] + [IN_VMEM] * 2,
        out_specs=[IN_VMEM] * len(out_shape),
        scratch_shapes=weight_slots(n_parts, part, columns),
        compiler_params=params(),
        cost_estimate=cost(4 * n_parts * n_rows * part * columns, 4 * n_parts * part * columns),
    )(jnp.stack(k_ids).astype(jnp.int32), work, flipped_own, flipped_far)
    each = len(outs) // n_parts
    return [(outs[i * each], list(outs[i * each + 1:(i + 1) * each])) for i in range(n_parts)]


def either_kernel(a, b, out):
    out[...] = a[...] + b[...]


def either(a, b):
    return pl.pallas_call(
        either_kernel,
        out_shape=shape_of(a.shape, a.dtype),
        in_specs=[IN_VMEM] * 2,
        out_specs=IN_VMEM,
        compiler_params=params(),
        cost_estimate=cost(a.size, 6 * a.size),
    )(a, b)


def stack_kernel(*refs):
    *arrays, out, sems = refs
    copies = [pltpu.make_async_copy(a, out.at[i], sems.at[i]) for i, a in enumerate(arrays)]
    for copy in copies:
        copy.start()
    for copy in copies:
        copy.wait()


def stack_call(arrays):
    return pl.pallas_call(
        stack_kernel,
        out_shape=shape_of((len(arrays),) + arrays[0].shape, arrays[0].dtype),
        in_specs=[IN_PLACE] * len(arrays),
        out_specs=IN_PLACE,
        scratch_shapes=[pltpu.SemaphoreType.DMA((len(arrays),))],
        compiler_params=params(),
        cost_estimate=cost(1, 4 * len(arrays) * arrays[0].size),
    )(*arrays)


def merge_kernel(turns, *refs):
    *seen, out = refs
    n_blocks, _, rows = seen[0].shape
    out[...] = jnp.zeros_like(out)
    for b in range(n_blocks):
        these = [s[(b - t) % n_blocks] for t, s in zip(turns, seen)]
        top = these[0][0:1, :]
        for s in these[1:]:
            top = jnp.maximum(top, s[0:1, :])
        at = slice(b * rows, (b + 1) * rows)
        out[0:1, at] = top
        out[1:2, at] = sum(s[1:2, :] * jnp.exp(s[0:1, :] - top) for s in these)
        out[2:3, at] = sum(s[2:3, :] for s in these)


def merge_call(turns, seen):
    n_blocks, lines, rows = seen[0].shape
    return pl.pallas_call(
        functools.partial(merge_kernel, turns),
        out_shape=shape_of((lines, n_blocks * rows), F32),
        in_specs=[IN_VMEM] * len(seen),
        out_specs=IN_VMEM,
        compiler_params=params(),
        cost_estimate=cost(1, 4 * len(seen) * n_blocks * lines * rows),
    )(*seen)


def add_kernel(turned, kept, *refs):
    total = kept[...]
    for a in refs[:-1]:
        total += a[...].astype(F32)
    refs[-1][...] = (total.T if turned else total).astype(BF16)


def add_call(kept, arrived, turned=False):
    shape = kept.shape[::-1] if turned else kept.shape
    return pl.pallas_call(
        functools.partial(add_kernel, turned),
        out_shape=shape_of(shape, BF16),
        in_specs=[IN_VMEM] * (1 + len(arrived)),
        out_specs=IN_VMEM,
        compiler_params=params(),
        cost_estimate=cost(kept.size, 4 * kept.size),
    )(kept, *arrived)


def head_kernel(slots_here, near_keys, far_keys, part, has_out, meta, *refs):
    refs = list(refs)
    grads = [refs.pop(0), refs.pop(0)]
    near = {k: refs.pop(0) for k in near_keys}
    stacks = [refs.pop(0) for _ in far_keys]
    far = {k: stack.at[i] for stack, keys in zip(stacks, far_keys) for i, k in enumerate(keys)}
    out, ready, sems = refs[has_out:]
    n_blocks, rows, columns = grads[0].shape
    right = jnp.concatenate([g[...].reshape(n_blocks * rows, columns) for g in grads])
    copies = []
    for n, i in enumerate(slots_here):
        left = jnp.concatenate([x[t, i][...] for x in (near, far) for t in range(n_blocks)])
        product = lax.dot_general(left, right, (((0,), (0,)), ((), ())), preferred_element_type=F32)
        if n >= 2:
            copies[n - 2].wait()
        ready[n % 2] = product.astype(BF16)
        start = pl.multiple_of(meta[i] * part, part)
        copies.append(pltpu.make_async_copy(ready.at[n % 2], out.at[pl.ds(start, part), :], sems.at[n % 2]))
        copies[-1].start()
    for copy in copies[-2:]:
        copy.wait()


def head_call(slots_here, near, far, grads, meta, out=None):
    n_blocks, rows, columns = grads[0].shape
    n_parts = len(near) // n_blocks
    part = near[0, 0].shape[1]
    near = {k: c for k, c in near.items() if k[1] in slots_here}
    far = [(keys, stack) for keys, stack in far if any(k[1] in slots_here for k in keys)]
    operands = list(grads) + list(near.values()) + [stack for _, stack in far]
    here = [] if out is None else [out]
    return pl.pallas_call(
        functools.partial(head_kernel, slots_here, list(near), [keys for keys, _ in far], part, len(here)),
        out_shape=shape_of((n_parts * part, columns), BF16),
        in_specs=[IN_SMEM] + [IN_VMEM] * len(operands) + [IN_PLACE] * len(here),
        out_specs=IN_PLACE,
        scratch_shapes=[pltpu.VMEM((2, part, columns), BF16), pltpu.SemaphoreType.DMA((2,))],
        input_output_aliases={1 + len(operands): 0} if here else {},
        compiler_params=pltpu.CompilerParams(vmem_limit_bytes=16 * 1024 * 1024),
        cost_estimate=cost(
            4 * n_blocks * rows * len(slots_here) * part * columns,
            4 * n_blocks * len(slots_here) * rows * part + 2 * len(slots_here) * part * columns,
        ),
    )(meta, *operands, *here)


def together(*groups):
    flat = lax.optimization_barrier([a for group in groups for a in group])
    out = []
    for group in groups:
        out.append(flat[:len(group)])
        flat = flat[len(group):]
    return out


def shards(hidden, head_weight, targets, response_start, other_sums, ref_logp, loss_cotangent):
    n_voc, n_ctx, n_dp = lax.axis_size("vocab"), lax.axis_size("ctx"), lax.axis_size("dp")
    me_voc, me_ctx, me_dp = lax.axis_index("vocab"), lax.axis_index("ctx"), lax.axis_index("dp")
    part, _, sides, window = hidden.shape
    rows = sides * window
    columns = head_weight.shape[1]
    line = n_voc == 4
    beyond = list(range(1, n_ctx))
    dp_swap = lambda a: lax.ppermute(a, "dp", ring(n_dp, 1))
    along = lambda a, by: lax.ppermute(a, "vocab", by)

    if line:
        table = [[0, 1, 2, 3], [1, 0, 2, 3], [2, 3, 1, 0], [3, 2, 1, 0]]
        part_of = [sum(jnp.where(me_voc == z, table[z][i], 0) for z in range(n_voc)) for i in range(n_voc)]
    else:
        part_of = [(me_voc - s) % n_voc for s in range(n_voc)]
    firsts = [
        ((me_voc * n_ctx + me_ctx) * n_dp + owner) * columns for owner in (me_dp, (me_dp + 1) % n_dp)
    ]
    meta = jnp.stack(part_of + firsts).astype(jnp.int32)

    far_weights = dp_swap(head_weight)
    work = hold(head_weight)
    width = head_weight.shape[0]

    def mine(a):
        pair = lax.broadcasted_iota(jnp.int32, a.shape, 0)
        return jnp.sum(jnp.where(pair == me_dp, a, jnp.zeros_like(a)), axis=0)

    blocks = [mine(targets)[:, b * window:(b + 1) * window].reshape(rows) for b in range(n_ctx)]
    wanted = []
    for t in range(n_ctx):
        at = (me_ctx - t) % n_ctx
        wanted.append(sum(jnp.where(at == b, blocks[b], 0) for b in range(n_ctx))[:, None])
    target = jnp.concatenate(wanted)
    ratio = mine(other_sums) - mine(ref_logp)
    small = jnp.stack([ratio[0] - ratio[1], mine(loss_cotangent)])
    meta_grads = jnp.stack([part_of[n_voc - 1]] + firsts + [me_ctx, mine(response_start)]).astype(jnp.int32)

    own = hidden.transpose(1, 2, 3, 0).reshape(rows, part)
    final = n_voc - 1
    call = lambda *args, **more: logits_call(*args, meta=meta, part=part, n_voc=n_voc, **more)
    cross = lambda a: [lax.ppermute(a, "ctx", ring(n_ctx, t)) for t in beyond]
    chunk = {}

    def arrive(i, near, over):
        chunk[0, i] = near
        for t, a in zip(beyond, over):
            chunk[t, i] = a

    def first_logits(work):
        plan = [(0, {j: chunk[0, j] for j in (0, 1)}, None, None)]
        plan += [(t, {0: chunk[t, 0]}, None, None) for t in beyond]
        *logits, work = call(plan, work, far=far_weights)
        return logits, work

    def more_logits(i, logits):
        plan = [(0, {i: chunk[0, i]}, logits[0], None)]
        plan += [(t, {i - 1: chunk[t, i - 1]}, logits[t], None) for t in beyond]
        return call(plan, work)

    arrive(0, own, cross(own))
    if line:
        first = along(own, PAIRS_OUT)
        inner = along(own, PAIR_IN)
        (first, inner), (work, target, small, meta_grads, meta), wanted = together(
            [first, inner], [work, target, small, meta_grads, meta], wanted
        )
        over = cross(first)
        outer, inner_last = along(inner, TO_ENDS), along(first, PAIR_IN)
        arrive(1, first, over)
        logits, work = first_logits(work)
        over, (inner, outer, inner_last), logits = together(over, [inner, outer, inner_last], logits)
        arrive(1, first, over)
        inner = either(inner, outer)
        arrive(2, inner, cross(inner))
        outer = along(inner_last, TO_ENDS)
        (inner_last, outer), logits = together([inner_last, outer], more_logits(2, logits))
        last = either(inner_last, outer)
    else:
        near = [own] + [along(own, ring(n_voc, i)) for i in range(1, n_voc)]
        logits = None
        for i in range(1, final):
            arrive(i, near[i], cross(near[i]))
            if logits is None:
                logits, work = first_logits(work)
            else:
                logits = more_logits(i, logits)
            (near[i + 1],), logits = together([near[i + 1]], logits)
        last = near[final]
    arrive(final, last, cross(last))
    done = call(
        [(0, {final: chunk[0, final]}, logits[0], wanted[0])]
        + [(t, {final - 1: chunk[t, final - 1]}, logits[t], None) for t in beyond],
        work,
    )
    last, done = together([chunk[t, final] for t in beyond], list(done))
    arrive(final, chunk[0, final], last)
    *logits, stats = done

    far_chunks = dp_swap(stack_call(list(chunk.values())))

    *others, stats = call(
        [(t, {final: chunk[t, final]}, logits[t], wanted[t]) for t in beyond], work, earlier=[stats]
    )
    logits = [logits[0]] + others

    if line and n_ctx == 2:
        corner = [(2 * a + c, 2 * b + (1 - c)) for a, b in PAIRS_OUT for c in range(2)]
        diagonal = lax.ppermute(stats, ("vocab", "ctx"), corner)
        merged = merge_call([0, 1, 0, 1], [stats, cross(stats)[0], along(stats, PAIRS_OUT), diagonal])
        all_stats = [merged, along(merged, SWAP_HALVES)]
    else:
        merged = merge_call([0] + beyond, [stats] + cross(stats))
        all_stats = [merged] + [along(merged, ring(n_voc, s)) for s in range(1, n_voc)]

    grads_own, grads_far, flipped_own, flipped_far, loss, kept, *send = grads_call(
        logits, target, all_stats, small, work, meta_grads, part, width, window
    )
    theirs = dp_swap(grads_far)

    back = lambda cs: [lax.ppermute(c, "ctx", ring(n_ctx, -t)) for t, c in zip(beyond, cs)]
    shares = {final: (kept, list(send))}

    def more_shares(slots):
        done = spread_call(flipped_own, flipped_far, work, [part_of[i] for i in slots], part, width, rows)
        shares.update(zip(slots, done))
        return [a for i in slots for a in [shares[i][0]] + shares[i][1]]

    def set_shares(slots, flat):
        for i in slots:
            shares[i] = (flat[0], list(flat[1:n_ctx]))
            flat = flat[n_ctx:]

    over = {}
    near_over = lambda i, *more: add_call(shares[i][0], over[i] + list(more))
    landed, grad_head = [], None
    for i in range(n_voc)[::-1]:
        over[i] = back(shares[i][1])
        came, beside = [], []
        if not line:
            came = [along(near_over(i + 1), ring(n_voc, -(i + 1)))] if i < final else []
        elif i == 2:
            came = [along(near_over(3), FROM_ENDS)]
        elif i == 1:
            came = [along(near_over(3, landed[0]), PAIR_IN), along(near_over(2), FROM_ENDS)]
        elif i == 0:
            came = [along(near_over(1, landed[0]), PAIRS_OUT), along(near_over(2, landed[1]), PAIR_IN)]
        if i:
            beside = more_shares([i - 1])
        else:
            grad_head = head_call(list(range(n_voc)), chunk, [(list(chunk), far_chunks)], [grads_own, theirs], meta)
            beside = [grad_head]
        swapped = [theirs] if i == final - 1 else []
        over[i], came, beside, swapped = together(over[i], came, beside, swapped)
        landed = came if line else landed + came
        if i:
            set_shares([i - 1], beside)
        else:
            grad_head, = beside
        if swapped:
            theirs, = swapped
    kept = shares[0][0]
    summed = add_call(kept, over[0] + landed, turned=True)
    grad_hidden = summed.reshape(1, sides, window, part).transpose(3, 0, 1, 2)

    far_loss = dp_swap(loss)
    owner = lax.broadcasted_iota(jnp.int32, (n_dp,), 0)
    pair_loss = jnp.where(owner == me_dp, loss[0, :n_dp], far_loss[0, :n_dp])
    return (grad_hidden, grad_head, pair_loss)


def solution(mesh):
    placed = (
        P("vocab", ("groups", "dp"), None, "ctx"),
        P(None, ("vocab", "ctx", "dp")),
        P("groups", None, None),
        P("groups"),
        P("groups", None),
        P("groups", None),
        P("groups"),
    )
    return jax.shard_map(
        shards,
        mesh=mesh,
        in_specs=placed,
        out_specs=(
            P("vocab", ("groups", "dp"), None, "ctx"),
            P("groups", ("vocab", "ctx", "dp")),
            P("groups"),
        ),
        check_vma=False,
    )
```

```python
import functools

import jax
import jax.numpy as jnp
from jax import lax
from jax.experimental import pallas as pl
from jax.experimental.pallas import tpu as pltpu
from jax.sharding import PartitionSpec as P

BETA = 0.1
F32, BF16 = jnp.float32, jnp.bfloat16
VMEM_BYTES = 16 * 1024 * 1024
WORK_BYTES = 52 * 1024 * 1024
IN_VMEM = pl.BlockSpec(memory_space=pltpu.VMEM)
IN_SMEM = pl.BlockSpec(memory_space=pltpu.SMEM)
IN_PLACE = pl.BlockSpec(memory_space=pl.ANY)
PAIRS_OUT = [(0, 1), (1, 0), (2, 3), (3, 2)]
PAIR_IN = [(1, 2), (2, 1)]
TO_ENDS = [(1, 0), (2, 3)]
FROM_ENDS = [(0, 1), (3, 2)]
SWAP_HALVES = [(0, 2), (2, 0), (1, 3), (3, 1)]


def ring(count, shift):
    return [(i, (i + shift) % count) for i in range(count)]


def params():
    return pltpu.CompilerParams(vmem_limit_bytes=VMEM_BYTES)


def cost(flops, moved):
    return pl.CostEstimate(flops=int(flops), bytes_accessed=int(moved), transcendentals=0)


def shape_of(shape, kind):
    return jax.ShapeDtypeStruct(shape, kind)


def work_shape(w):
    times = max(2, -(-WORK_BYTES // (w.size * w.dtype.itemsize)))
    return shape_of((times * w.shape[0], w.shape[1]), w.dtype)


def hold_kernel(w, out, sem):
    copy = pltpu.make_async_copy(w, out.at[pl.ds(0, w.shape[0]), :], sem)
    copy.start()
    copy.wait()


def hold(w):
    return pl.pallas_call(
        hold_kernel,
        out_shape=work_shape(w),
        in_specs=[IN_PLACE],
        out_specs=IN_PLACE,
        scratch_shapes=[pltpu.SemaphoreType.DMA],
        compiler_params=params(),
        cost_estimate=cost(1, 4 * w.size),
    )(w)


def fetch(work, width, start, part, slots, i, sems, own_only=False):
    copies = []
    for j in range(1 if own_only else 2):
        source = work.at[pl.ds(j * width + start, part), :]
        copies.append(pltpu.make_async_copy(source, slots.at[i, j], sems.at[i, j]))
        copies[-1].start()
    return copies


def row_stats(own, far, wanted, first_own, first_far):
    top = jnp.max(jnp.maximum(own, far), axis=1, keepdims=True)
    total = jnp.sum(jnp.exp(own - top) + jnp.exp(far - top), axis=1, keepdims=True)
    column = lax.broadcasted_iota(jnp.int32, own.shape, 1)
    zero = jnp.zeros_like(own)
    picked = jnp.sum(
        jnp.where(column + first_own == wanted, own, zero) + jnp.where(column + first_far == wanted, far, zero),
        axis=1,
        keepdims=True,
    )
    lane = lax.broadcasted_iota(jnp.int32, (own.shape[0], 128), 1)
    return jnp.where(lane == 0, top, jnp.where(lane == 1, total, picked)).T[:8, :]


def logits_kernel(plan, columns, part, n_voc, fresh, n_earlier, meta, work, *refs):
    refs = list(refs)
    width = part * n_voc
    far = refs.pop(0) if fresh else None
    chunks = {(t, i): refs.pop(0) for t, parts, _, _ in plan for i in parts}
    accs = {t: refs.pop(0) for t, _, has_acc, _ in plan if has_acc}
    wanted = {t: refs.pop(0) for t, _, _, done in plan if done}
    earlier = [refs.pop(0) for _ in range(n_earlier)]
    used = sorted({i for _, parts, _, _ in plan for i in parts})
    starts = [pl.multiple_of(meta[i] * part, part) for i in used]
    if fresh:
        held, far_sems = refs[-2:]
        refs = refs[:-2]
        into = pltpu.make_async_copy(far, held, far_sems.at[0])
        into.start()
    slots, sems = refs[-2:]
    coming = [fetch(work, width, start, part, slots, n, sems, fresh) for n, start in enumerate(starts)]
    if fresh:
        into.wait()
        kept = pltpu.make_async_copy(held, refs[-3].at[pl.ds(width, width), :], far_sems.at[1])
        kept.start()
    outs = {t: refs.pop(0) for t, _, _, _ in plan}
    for n, i in enumerate(used):
        for copy in coming[n]:
            copy.wait()
        for t, parts, has_acc, _ in plan:
            if i not in parts:
                continue
            x = chunks[t, i][...]
            for j in range(2):
                at = slice(j * columns, (j + 1) * columns)
                w = held[pl.ds(starts[n], part), :] if fresh and j else slots[n, j]
                product = jnp.dot(x, w, preferred_element_type=F32)
                if i != parts[0]:
                    product += outs[t][:, at]
                elif has_acc:
                    product += accs[t][:, at]
                outs[t][:, at] = product
    if wanted:
        stats = refs[0]
        for n, a in enumerate(earlier):
            stats[n] = a[0]
        for n, t in enumerate(wanted, n_earlier):
            own, beside = outs[t][:, :columns], outs[t][:, columns:]
            stats[n] = row_stats(own, beside, wanted[t][...], meta[n_voc], meta[n_voc + 1])
    if fresh:
        kept.wait()


def logits_call(plan, work, meta, part, n_voc, far=None, earlier=()):
    columns = work.shape[1]
    accs = [acc for _, _, acc, _ in plan if acc is not None]
    wanted = [w for _, _, _, w in plan if w is not None]
    chunks = [parts[i] for _, parts, _, _ in plan for i in sorted(parts)]
    rows = chunks[0].shape[0]
    out_shape = [shape_of((rows, 2 * columns), F32)] * len(plan)
    if wanted:
        out_shape.append(shape_of((len(earlier) + len(wanted), 8, rows), F32))
    out_specs = [IN_VMEM] * len(out_shape)
    kernel_plan = [(t, sorted(parts), acc is not None, w is not None) for t, parts, acc, w in plan]
    n_used = len({i for _, parts, _, _ in plan for i in parts})
    fresh = far is not None
    in_place = [work] + ([far] if fresh else [])
    if fresh:
        out_shape.append(shape_of(work.shape, work.dtype))
        out_specs.append(IN_PLACE)
    operands = chunks + accs + wanted + list(earlier)
    return pl.pallas_call(
        functools.partial(logits_kernel, kernel_plan, columns, part, n_voc, fresh, len(earlier)),
        out_shape=out_shape,
        in_specs=[IN_SMEM] + [IN_PLACE] * len(in_place) + [IN_VMEM] * len(operands),
        out_specs=out_specs,
        scratch_shapes=[pltpu.VMEM((n_used, 2 - fresh, part, columns), BF16), pltpu.SemaphoreType.DMA((n_used, 2))]
        + ([pltpu.VMEM((part * n_voc, columns), BF16), pltpu.SemaphoreType.DMA((2,))] if fresh else []),
        input_output_aliases={1: len(out_shape) - 1} if fresh else {},
        compiler_params=params(),
        cost_estimate=cost(4 * len(chunks) * rows * part * columns, n_used * 4 * part * columns),
    )(meta, *in_place, *operands)


def spread(flipped_own, flipped_far, w_own, w_far, kept, send):
    rows = kept.shape[1]
    here = jnp.dot(w_own, flipped_own, preferred_element_type=F32)
    here += jnp.dot(w_far, flipped_far, preferred_element_type=F32)
    kept[...] = here[:, :rows]
    for t, out in enumerate(send, 1):
        out[...] = here[:, t * rows:(t + 1) * rows].astype(BF16)


def grads_kernel(n_blocks, n_stats, columns, part, width, window, meta, small, work, *refs):
    refs = list(refs)
    logits = [refs.pop(0) for _ in range(n_blocks)]
    target = [refs.pop(0) for _ in range(n_blocks)]
    stats = [refs.pop(0) for _ in range(n_stats)]
    slots, sems = refs[-2:]
    grads_own, grads_far, flipped_own, flipped_far, loss, kept = refs[:6]
    send = refs[6:-2]
    coming = fetch(work, width, pl.multiple_of(meta[0] * part, part), part, slots, 0, sems)
    rows = logits[0].shape[0]
    me_ctx, start = meta[3], meta[4]
    top = stats[0][0:1, :]
    for s in stats[1:]:
        top = jnp.maximum(top, s[0:1, :])
    total = jnp.zeros_like(top)
    picked = jnp.zeros_like(top)
    for s in stats:
        total += s[1:2, :] * jnp.exp(s[0:1, :] - top)
        picked += s[2:3, :]
    row = lax.broadcasted_iota(jnp.int32, (1, rows), 1)
    masks = []
    for t in range(n_blocks):
        block = lax.rem(me_ctx + (n_blocks - t), n_blocks)
        seen = lax.rem(row, window) + block * window >= start
        masks.append(jnp.where(seen, jnp.where(row < window, 1.0, -1.0), 0.0))
    signed_mask = jnp.concatenate(masks, axis=1)
    token_logp = picked - top - jnp.log(total)
    zeros = jnp.zeros((1, 128), F32)
    margin = BETA * (jnp.sum(signed_mask * token_logp, axis=1, keepdims=True) + (zeros + small[0]))
    loss[...] = jnp.maximum(-margin, 0.0) + jnp.log1p(jnp.exp(-jnp.abs(margin)))
    factor = -BETA * (1.0 / (1.0 + jnp.exp(margin))) * small[1]
    weight = factor[:, 0:1] * signed_mask
    lines = lax.broadcasted_iota(jnp.int32, (128, top.shape[1]), 0)
    packed = jnp.where(lines == 0, top, jnp.where(lines == 1, weight, 1.0 / total)).T
    for t in range(n_blocks):
        at = slice(t * rows, (t + 1) * rows)
        top_t, weight_t, inverse_t = packed[at, 0:1], packed[at, 1:2], packed[at, 2:3]
        wanted = target[t][...]
        for j, (grads, flipped) in enumerate(((grads_own, flipped_own), (grads_far, flipped_far))):
            l = logits[t][:, j * columns:(j + 1) * columns]
            column = lax.broadcasted_iota(jnp.int32, l.shape, 1) + meta[1 + j]
            hit = jnp.where(column == wanted, 1.0, 0.0)
            g = weight_t * (hit - jnp.exp(l - top_t) * inverse_t)
            grads[t] = g.astype(BF16)
            flipped[:, at] = g.T.astype(BF16)
    for copy in coming:
        copy.wait()
    spread(flipped_own[...], flipped_far[...], slots[0, 0], slots[0, 1], kept, send)


def spread_kernel(part, width, n_parts, meta, work, flipped_own, flipped_far, *refs):
    outs, slots, sems = refs[:-2], refs[-2], refs[-1]
    each = len(outs) // n_parts
    coming = [
        fetch(work, width, pl.multiple_of(meta[i] * part, part), part, slots, i, sems) for i in range(n_parts)
    ]
    for i in range(n_parts):
        for copy in coming[i]:
            copy.wait()
        kept, *send = outs[i * each:(i + 1) * each]
        spread(flipped_own[...], flipped_far[...], slots[i, 0], slots[i, 1], kept, send)


def spread_shapes(n_blocks, rows, part):
    return [shape_of((part, rows), F32)] + [shape_of((part, rows), BF16)] * (n_blocks - 1)


def weight_slots(n_parts, part, columns):
    return [pltpu.VMEM((n_parts, 2, part, columns), BF16), pltpu.SemaphoreType.DMA((n_parts, 2))]


def grads_call(logits, target, stats, small, work, meta, part, width, window):
    n_blocks, rows, columns = len(logits), logits[0].shape[0], work.shape[1]
    grads = shape_of((n_blocks, rows, columns), BF16)
    flipped = shape_of((columns, n_blocks * rows), BF16)
    out_shape = [grads, grads, flipped, flipped, shape_of((1, 128), F32)] + spread_shapes(n_blocks, rows, part)
    operands = list(logits) + list(target) + list(stats)
    return pl.pallas_call(
        functools.partial(grads_kernel, n_blocks, len(stats), columns, part, width, window),
        out_shape=out_shape,
        in_specs=[IN_SMEM] * 2 + [IN_PLACE] + [IN_VMEM] * len(operands),
        out_specs=[IN_VMEM] * len(out_shape),
        scratch_shapes=weight_slots(1, part, columns),
        compiler_params=params(),
        cost_estimate=cost(4 * n_blocks * rows * part * columns, 8 * part * columns),
    )(meta, small, work, *operands)


def spread_call(flipped_own, flipped_far, work, k_ids, part, width, rows):
    columns, n_rows = flipped_own.shape
    n_parts = len(k_ids)
    out_shape = spread_shapes(n_rows // rows, rows, part) * n_parts
    outs = pl.pallas_call(
        functools.partial(spread_kernel, part, width, n_parts),
        out_shape=out_shape,
        in_specs=[IN_SMEM] + [IN_PLACE] + [IN_VMEM] * 2,
        out_specs=[IN_VMEM] * len(out_shape),
        scratch_shapes=weight_slots(n_parts, part, columns),
        compiler_params=params(),
        cost_estimate=cost(4 * n_parts * n_rows * part * columns, 4 * n_parts * part * columns),
    )(jnp.stack(k_ids).astype(jnp.int32), work, flipped_own, flipped_far)
    each = len(outs) // n_parts
    return [(outs[i * each], list(outs[i * each + 1:(i + 1) * each])) for i in range(n_parts)]


def either_kernel(a, b, out):
    out[...] = a[...] + b[...]


def either(a, b):
    return pl.pallas_call(
        either_kernel,
        out_shape=shape_of(a.shape, a.dtype),
        in_specs=[IN_VMEM] * 2,
        out_specs=IN_VMEM,
        compiler_params=params(),
        cost_estimate=cost(a.size, 6 * a.size),
    )(a, b)


def stack_kernel(*refs):
    *arrays, out, sems = refs
    copies = [pltpu.make_async_copy(a, out.at[i], sems.at[i]) for i, a in enumerate(arrays)]
    for copy in copies:
        copy.start()
    for copy in copies:
        copy.wait()


def stack_call(arrays):
    return pl.pallas_call(
        stack_kernel,
        out_shape=shape_of((len(arrays),) + arrays[0].shape, arrays[0].dtype),
        in_specs=[IN_PLACE] * len(arrays),
        out_specs=IN_PLACE,
        scratch_shapes=[pltpu.SemaphoreType.DMA((len(arrays),))],
        compiler_params=params(),
        cost_estimate=cost(1, 4 * len(arrays) * arrays[0].size),
    )(*arrays)


def merge_kernel(turns, *refs):
    *seen, out = refs
    n_blocks, _, rows = seen[0].shape
    out[...] = jnp.zeros_like(out)
    for b in range(n_blocks):
        these = [s[(b - t) % n_blocks] for t, s in zip(turns, seen)]
        top = these[0][0:1, :]
        for s in these[1:]:
            top = jnp.maximum(top, s[0:1, :])
        at = slice(b * rows, (b + 1) * rows)
        out[0:1, at] = top
        out[1:2, at] = sum(s[1:2, :] * jnp.exp(s[0:1, :] - top) for s in these)
        out[2:3, at] = sum(s[2:3, :] for s in these)


def merge_call(turns, seen):
    n_blocks, lines, rows = seen[0].shape
    return pl.pallas_call(
        functools.partial(merge_kernel, turns),
        out_shape=shape_of((lines, n_blocks * rows), F32),
        in_specs=[IN_VMEM] * len(seen),
        out_specs=IN_VMEM,
        compiler_params=params(),
        cost_estimate=cost(1, 4 * len(seen) * n_blocks * lines * rows),
    )(*seen)


def add_kernel(turned, kept, *refs):
    total = kept[...]
    for a in refs[:-1]:
        total += a[...].astype(F32)
    refs[-1][...] = (total.T if turned else total).astype(BF16)


def add_call(kept, arrived, turned=False):
    shape = kept.shape[::-1] if turned else kept.shape
    return pl.pallas_call(
        functools.partial(add_kernel, turned),
        out_shape=shape_of(shape, BF16),
        in_specs=[IN_VMEM] * (1 + len(arrived)),
        out_specs=IN_VMEM,
        compiler_params=params(),
        cost_estimate=cost(kept.size, 4 * kept.size),
    )(kept, *arrived)


def head_kernel(slots_here, near_keys, far_keys, part, has_out, meta, *refs):
    refs = list(refs)
    grads = [refs.pop(0), refs.pop(0)]
    near = {k: refs.pop(0) for k in near_keys}
    stacks = [refs.pop(0) for _ in far_keys]
    far = {k: stack.at[i] for stack, keys in zip(stacks, far_keys) for i, k in enumerate(keys)}
    out, ready, sems = refs[has_out:]
    n_blocks, rows, columns = grads[0].shape
    right = jnp.concatenate([g[...].reshape(n_blocks * rows, columns) for g in grads])
    copies = []
    for n, i in enumerate(slots_here):
        left = jnp.concatenate([x[t, i][...] for x in (near, far) for t in range(n_blocks)])
        product = lax.dot_general(left, right, (((0,), (0,)), ((), ())), preferred_element_type=F32)
        if n >= 2:
            copies[n - 2].wait()
        ready[n % 2] = product.astype(BF16)
        start = pl.multiple_of(meta[i] * part, part)
        copies.append(pltpu.make_async_copy(ready.at[n % 2], out.at[pl.ds(start, part), :], sems.at[n % 2]))
        copies[-1].start()
    for copy in copies[-2:]:
        copy.wait()


def head_call(slots_here, near, far, grads, meta, out=None):
    n_blocks, rows, columns = grads[0].shape
    n_parts = len(near) // n_blocks
    part = near[0, 0].shape[1]
    near = {k: c for k, c in near.items() if k[1] in slots_here}
    far = [(keys, stack) for keys, stack in far if any(k[1] in slots_here for k in keys)]
    operands = list(grads) + list(near.values()) + [stack for _, stack in far]
    here = [] if out is None else [out]
    return pl.pallas_call(
        functools.partial(head_kernel, slots_here, list(near), [keys for keys, _ in far], part, len(here)),
        out_shape=shape_of((n_parts * part, columns), BF16),
        in_specs=[IN_SMEM] + [IN_VMEM] * len(operands) + [IN_PLACE] * len(here),
        out_specs=IN_PLACE,
        scratch_shapes=[pltpu.VMEM((2, part, columns), BF16), pltpu.SemaphoreType.DMA((2,))],
        input_output_aliases={1 + len(operands): 0} if here else {},
        compiler_params=pltpu.CompilerParams(vmem_limit_bytes=16 * 1024 * 1024),
        cost_estimate=cost(
            4 * n_blocks * rows * len(slots_here) * part * columns,
            4 * n_blocks * len(slots_here) * rows * part + 2 * len(slots_here) * part * columns,
        ),
    )(meta, *operands, *here)


def together(*groups):
    flat = lax.optimization_barrier([a for group in groups for a in group])
    out = []
    for group in groups:
        out.append(flat[:len(group)])
        flat = flat[len(group):]
    return out


def shards(hidden, head_weight, targets, response_start, other_sums, ref_logp, loss_cotangent):
    n_voc, n_ctx, n_dp = lax.axis_size("vocab"), lax.axis_size("ctx"), lax.axis_size("dp")
    me_voc, me_ctx, me_dp = lax.axis_index("vocab"), lax.axis_index("ctx"), lax.axis_index("dp")
    part, _, sides, window = hidden.shape
    rows = sides * window
    columns = head_weight.shape[1]
    line = n_voc == 4
    beyond = list(range(1, n_ctx))
    dp_swap = lambda a: lax.ppermute(a, "dp", ring(n_dp, 1))
    along = lambda a, by: lax.ppermute(a, "vocab", by)

    if line:
        table = [[0, 1, 2, 3], [1, 0, 2, 3], [2, 3, 1, 0], [3, 2, 1, 0]]
        part_of = [sum(jnp.where(me_voc == z, table[z][i], 0) for z in range(n_voc)) for i in range(n_voc)]
    else:
        part_of = [(me_voc - s) % n_voc for s in range(n_voc)]
    firsts = [
        ((me_voc * n_ctx + me_ctx) * n_dp + owner) * columns for owner in (me_dp, (me_dp + 1) % n_dp)
    ]
    meta = jnp.stack(part_of + firsts).astype(jnp.int32)

    far_weights = dp_swap(head_weight)
    work = hold(head_weight)
    width = head_weight.shape[0]

    def mine(a):
        pair = lax.broadcasted_iota(jnp.int32, a.shape, 0)
        return jnp.sum(jnp.where(pair == me_dp, a, jnp.zeros_like(a)), axis=0)

    blocks = [mine(targets)[:, b * window:(b + 1) * window].reshape(rows) for b in range(n_ctx)]
    wanted = []
    for t in range(n_ctx):
        at = (me_ctx - t) % n_ctx
        wanted.append(sum(jnp.where(at == b, blocks[b], 0) for b in range(n_ctx))[:, None])

    own = hidden.transpose(1, 2, 3, 0).reshape(rows, part)
    final = n_voc - 1
    call = lambda *args, **more: logits_call(*args, meta=meta, part=part, n_voc=n_voc, **more)
    cross = lambda a: [lax.ppermute(a, "ctx", ring(n_ctx, t)) for t in beyond]
    chunk = {}

    def arrive(i, near, over):
        chunk[0, i] = near
        for t, a in zip(beyond, over):
            chunk[t, i] = a

    def first_logits(work):
        *logits, work = call([(0, {j: chunk[0, j] for j in (0, 1)}, None, None)], work, far=far_weights)
        return logits, work

    def more_logits(i, logits):
        return call([(0, {i: chunk[0, i]}, logits[0], None)], work)

    scalars = [response_start, other_sums, ref_logp, loss_cotangent]

    def prepare(begin, others, refer, cotangent):
        ratio = mine(others) - mine(refer)
        small = jnp.stack([ratio[0] - ratio[1], mine(cotangent)])
        return [small, jnp.stack([part_of[final]] + firsts + [me_ctx, mine(begin)]).astype(jnp.int32)]

    arrive(0, own, cross(own))
    if line:
        first = along(own, PAIRS_OUT)
        inner = along(own, PAIR_IN)
        (first, inner), (work, meta), over = together([first, inner], [work, meta], [chunk[t, 0] for t in beyond])
        arrive(0, own, over)
        over = cross(first)
        outer, inner_last = along(inner, TO_ENDS), along(first, PAIR_IN)
        arrive(1, first, over)
        logits, work = first_logits(work)
        logits, raw = together(logits, scalars)
        over, (inner, outer, inner_last), logits, wanted, (small, meta_grads) = together(
            over, [inner, outer, inner_last], logits, wanted, prepare(*raw)
        )
        arrive(1, first, over)
        inner = either(inner, outer)
        arrive(2, inner, cross(inner))
        outer = along(inner_last, TO_ENDS)
        (inner_last, outer), logits = together([inner_last, outer], more_logits(2, logits))
        last = either(inner_last, outer)
    else:
        near = [own] + [along(own, ring(n_voc, i)) for i in range(1, n_voc)]
        logits = None
        for i in range(1, final):
            arrive(i, near[i], cross(near[i]))
            if logits is None:
                logits, work = first_logits(work)
            else:
                logits = more_logits(i, logits)
            (near[i + 1],), logits = together([near[i + 1]], logits)
        last = near[final]
        small, meta_grads = prepare(*scalars)
    arrive(final, last, cross(last))
    late = [(t, final) for t in beyond]
    soon = [k for k in chunk if k not in late]
    done = call([(0, {final: chunk[0, final]}, logits[0], wanted[0])], work)
    last, (near_logits, stats), (stacked,) = together(
        [chunk[k] for k in late], list(done), [stack_call([chunk[k] for k in soon])]
    )
    arrive(final, chunk[0, final], last)
    *logits, stats = call(
        [(t, {i: chunk[t, i] for i in range(n_voc)}, None, wanted[t]) for t in beyond], work, earlier=[stats]
    )
    logits = [near_logits] + logits
    far_soon = dp_swap(stacked)

    if line and n_ctx == 2:
        corner = [(2 * a + c, 2 * b + (1 - c)) for a, b in PAIRS_OUT for c in range(2)]
        diagonal = lax.ppermute(stats, ("vocab", "ctx"), corner)
        merged = merge_call([0, 1, 0, 1], [stats, cross(stats)[0], along(stats, PAIRS_OUT), diagonal])
        all_stats = [merged, along(merged, SWAP_HALVES)]
    else:
        merged = merge_call([0] + beyond, [stats] + cross(stats))
        all_stats = [merged] + [along(merged, ring(n_voc, s)) for s in range(1, n_voc)]

    grads_own, grads_far, flipped_own, flipped_far, loss, kept, *send = grads_call(
        logits, wanted, all_stats, small, work, meta_grads, part, width, window
    )
    theirs, far_loss = dp_swap(grads_far), dp_swap(loss)
    far_late = dp_swap(jnp.stack(together([chunk[k] for k in late], [kept])[0]))

    back = lambda cs: [lax.ppermute(c, "ctx", ring(n_ctx, -t)) for t, c in zip(beyond, cs)]
    shares = {final: (kept, list(send))}

    def more_shares(slots):
        done = spread_call(flipped_own, flipped_far, work, [part_of[i] for i in slots], part, width, rows)
        shares.update(zip(slots, done))
        return [a for i in slots for a in [shares[i][0]] + shares[i][1]]

    def set_shares(slots, flat):
        for i in slots:
            shares[i] = (flat[0], list(flat[1:n_ctx]))
            flat = flat[n_ctx:]

    over = {}
    near_over = lambda i, *more: add_call(shares[i][0], over[i] + list(more))
    landed, grad_head = [], None
    for i in range(n_voc)[::-1]:
        over[i] = back(shares[i][1])
        came, beside = [], []
        if not line:
            came = [along(near_over(i + 1), ring(n_voc, -(i + 1)))] if i < final else []
        elif i == 2:
            came = [along(near_over(3), FROM_ENDS)]
        elif i == 1:
            came = [along(near_over(3, landed[0]), PAIR_IN), along(near_over(2), FROM_ENDS)]
        elif i == 0:
            outer = near_over(1, landed[0])
            (outer,), landed = together([outer], landed)
            came = [along(outer, PAIRS_OUT), along(near_over(2, landed[1]), PAIR_IN)]
        if i:
            beside = more_shares([i - 1])
        else:
            grad_head = head_call(list(range(n_voc)), chunk, [(soon, far_soon), (late, far_late)], [grads_own, theirs], meta)
            beside = [grad_head]
        swapped = [theirs, far_loss, far_late] if i == final - 1 else []
        over[i], came, beside, swapped = together(over[i], came, beside, swapped)
        landed = came if line else landed + came
        if i:
            set_shares([i - 1], beside)
        else:
            grad_head, = beside
        if swapped:
            theirs, far_loss, far_late = swapped
    kept = shares[0][0]
    summed = add_call(kept, over[0] + landed, turned=True)
    grad_hidden = summed.reshape(1, sides, window, part).transpose(3, 0, 1, 2)

    owner = lax.broadcasted_iota(jnp.int32, (n_dp,), 0)
    pair_loss = jnp.where(owner == me_dp, loss[0, :n_dp], far_loss[0, :n_dp])
    return (grad_hidden, grad_head, pair_loss)


def solution(mesh):
    placed = (
        P("vocab", ("groups", "dp"), None, "ctx"),
        P(None, ("vocab", "ctx", "dp")),
        P("groups", None, None),
        P("groups"),
        P("groups", None),
        P("groups", None),
        P("groups"),
    )
    return jax.shard_map(
        shards,
        mesh=mesh,
        in_specs=placed,
        out_specs=(
            P("vocab", ("groups", "dp"), None, "ctx"),
            P("groups", ("vocab", "ctx", "dp")),
            P("groups"),
        ),
        check_vma=False,
    )
```

```python
import functools

import jax
import jax.numpy as jnp
from jax import lax
from jax.experimental import pallas as pl
from jax.experimental.pallas import tpu as pltpu
from jax.sharding import PartitionSpec as P

BETA = 0.1
F32, BF16 = jnp.float32, jnp.bfloat16
VMEM_BYTES = 16 * 1024 * 1024
WORK_BYTES = 52 * 1024 * 1024
IN_VMEM = pl.BlockSpec(memory_space=pltpu.VMEM)
IN_SMEM = pl.BlockSpec(memory_space=pltpu.SMEM)
IN_PLACE = pl.BlockSpec(memory_space=pl.ANY)
PAIRS_OUT = [(0, 1), (1, 0), (2, 3), (3, 2)]
PAIR_IN = [(1, 2), (2, 1)]
TO_ENDS = [(1, 0), (2, 3)]
FROM_ENDS = [(0, 1), (3, 2)]
SWAP_HALVES = [(0, 2), (2, 0), (1, 3), (3, 1)]


def ring(count, shift):
    return [(i, (i + shift) % count) for i in range(count)]


def params():
    return pltpu.CompilerParams(vmem_limit_bytes=VMEM_BYTES)


def cost(flops, moved):
    return pl.CostEstimate(flops=int(flops), bytes_accessed=int(moved), transcendentals=0)


def shape_of(shape, kind):
    return jax.ShapeDtypeStruct(shape, kind)


def work_shape(w):
    times = max(2, -(-WORK_BYTES // (w.size * w.dtype.itemsize)))
    return shape_of((times * w.shape[0], w.shape[1]), w.dtype)


def hold_kernel(w, out, sem):
    copy = pltpu.make_async_copy(w, out.at[pl.ds(0, w.shape[0]), :], sem)
    copy.start()
    copy.wait()


def hold(w):
    return pl.pallas_call(
        hold_kernel,
        out_shape=work_shape(w),
        in_specs=[IN_PLACE],
        out_specs=IN_PLACE,
        scratch_shapes=[pltpu.SemaphoreType.DMA],
        compiler_params=params(),
        cost_estimate=cost(1, 4 * w.size),
    )(w)


def fetch(work, width, start, part, slots, i, sems, own_only=False):
    copies = []
    for j in range(1 if own_only else 2):
        source = work.at[pl.ds(j * width + start, part), :]
        copies.append(pltpu.make_async_copy(source, slots.at[i, j], sems.at[i, j]))
        copies[-1].start()
    return copies


def row_stats(own, far, wanted, first_own, first_far):
    top = jnp.max(jnp.maximum(own, far), axis=1, keepdims=True)
    total = jnp.sum(jnp.exp(own - top) + jnp.exp(far - top), axis=1, keepdims=True)
    column = lax.broadcasted_iota(jnp.int32, own.shape, 1)
    zero = jnp.zeros_like(own)
    picked = jnp.sum(
        jnp.where(column + first_own == wanted, own, zero) + jnp.where(column + first_far == wanted, far, zero),
        axis=1,
        keepdims=True,
    )
    lane = lax.broadcasted_iota(jnp.int32, (own.shape[0], 128), 1)
    return jnp.where(lane == 0, top, jnp.where(lane == 1, total, picked)).T[:8, :]


def logits_kernel(plan, columns, part, n_voc, fresh, n_earlier, meta, work, *refs):
    refs = list(refs)
    width = part * n_voc
    far = refs.pop(0) if fresh else None
    chunks = {(t, i): refs.pop(0) for t, parts, _, _ in plan for i in parts}
    accs = {t: refs.pop(0) for t, _, has_acc, _ in plan if has_acc}
    wanted = {t: refs.pop(0) for t, _, _, done in plan if done}
    earlier = [refs.pop(0) for _ in range(n_earlier)]
    used = sorted({i for _, parts, _, _ in plan for i in parts})
    starts = [pl.multiple_of(meta[i] * part, part) for i in used]
    if fresh:
        held, far_sems = refs[-2:]
        refs = refs[:-2]
        into = pltpu.make_async_copy(far, held, far_sems.at[0])
        into.start()
    slots, sems = refs[-2:]
    coming = [fetch(work, width, start, part, slots, n, sems, fresh) for n, start in enumerate(starts)]
    if fresh:
        into.wait()
        kept = pltpu.make_async_copy(held, refs[-3].at[pl.ds(width, width), :], far_sems.at[1])
        kept.start()
    outs = {t: refs.pop(0) for t, _, _, _ in plan}
    for n, i in enumerate(used):
        for copy in coming[n]:
            copy.wait()
        for t, parts, has_acc, _ in plan:
            if i not in parts:
                continue
            x = chunks[t, i][...]
            for j in range(2):
                at = slice(j * columns, (j + 1) * columns)
                w = held[pl.ds(starts[n], part), :] if fresh and j else slots[n, j]
                product = jnp.dot(x, w, preferred_element_type=F32)
                if i != parts[0]:
                    product += outs[t][:, at]
                elif has_acc:
                    product += accs[t][:, at]
                outs[t][:, at] = product
    if wanted:
        stats = refs[0]
        for n, a in enumerate(earlier):
            stats[n] = a[0]
        for n, t in enumerate(wanted, n_earlier):
            own, beside = outs[t][:, :columns], outs[t][:, columns:]
            stats[n] = row_stats(own, beside, wanted[t][...], meta[n_voc], meta[n_voc + 1])
    if fresh:
        kept.wait()


def logits_call(plan, work, meta, part, n_voc, far=None, earlier=()):
    columns = work.shape[1]
    accs = [acc for _, _, acc, _ in plan if acc is not None]
    wanted = [w for _, _, _, w in plan if w is not None]
    chunks = [parts[i] for _, parts, _, _ in plan for i in sorted(parts)]
    rows = chunks[0].shape[0]
    out_shape = [shape_of((rows, 2 * columns), F32)] * len(plan)
    if wanted:
        out_shape.append(shape_of((len(earlier) + len(wanted), 8, rows), F32))
    out_specs = [IN_VMEM] * len(out_shape)
    kernel_plan = [(t, sorted(parts), acc is not None, w is not None) for t, parts, acc, w in plan]
    n_used = len({i for _, parts, _, _ in plan for i in parts})
    fresh = far is not None
    in_place = [work] + ([far] if fresh else [])
    if fresh:
        out_shape.append(shape_of(work.shape, work.dtype))
        out_specs.append(IN_PLACE)
    operands = chunks + accs + wanted + list(earlier)
    return pl.pallas_call(
        functools.partial(logits_kernel, kernel_plan, columns, part, n_voc, fresh, len(earlier)),
        out_shape=out_shape,
        in_specs=[IN_SMEM] + [IN_PLACE] * len(in_place) + [IN_VMEM] * len(operands),
        out_specs=out_specs,
        scratch_shapes=[pltpu.VMEM((n_used, 2 - fresh, part, columns), BF16), pltpu.SemaphoreType.DMA((n_used, 2))]
        + ([pltpu.VMEM((part * n_voc, columns), BF16), pltpu.SemaphoreType.DMA((2,))] if fresh else []),
        input_output_aliases={1: len(out_shape) - 1} if fresh else {},
        compiler_params=params(),
        cost_estimate=cost(4 * len(chunks) * rows * part * columns, n_used * 4 * part * columns),
    )(meta, *in_place, *operands)


def spread(flipped_own, flipped_far, w_own, w_far, kept, send):
    rows = kept.shape[1]
    here = jnp.dot(w_own, flipped_own, preferred_element_type=F32)
    here += jnp.dot(w_far, flipped_far, preferred_element_type=F32)
    kept[...] = here[:, :rows]
    for t, out in enumerate(send, 1):
        out[...] = here[:, t * rows:(t + 1) * rows].astype(BF16)


def grads_kernel(n_blocks, n_stats, columns, part, width, window, meta, small, work, *refs):
    refs = list(refs)
    logits = [refs.pop(0) for _ in range(n_blocks)]
    target = [refs.pop(0) for _ in range(n_blocks)]
    stats = [refs.pop(0) for _ in range(n_stats)]
    slots, sems = refs[-2:]
    grads_own, grads_far, flipped_own, flipped_far, loss, kept = refs[:6]
    send = refs[6:-2]
    coming = fetch(work, width, pl.multiple_of(meta[0] * part, part), part, slots, 0, sems)
    rows = logits[0].shape[0]
    me_ctx, start = meta[3], meta[4]
    top = stats[0][0:1, :]
    for s in stats[1:]:
        top = jnp.maximum(top, s[0:1, :])
    total = jnp.zeros_like(top)
    picked = jnp.zeros_like(top)
    for s in stats:
        total += s[1:2, :] * jnp.exp(s[0:1, :] - top)
        picked += s[2:3, :]
    row = lax.broadcasted_iota(jnp.int32, (1, rows), 1)
    masks = []
    for t in range(n_blocks):
        block = lax.rem(me_ctx + (n_blocks - t), n_blocks)
        seen = lax.rem(row, window) + block * window >= start
        masks.append(jnp.where(seen, jnp.where(row < window, 1.0, -1.0), 0.0))
    signed_mask = jnp.concatenate(masks, axis=1)
    token_logp = picked - top - jnp.log(total)
    zeros = jnp.zeros((1, 128), F32)
    margin = BETA * (jnp.sum(signed_mask * token_logp, axis=1, keepdims=True) + (zeros + small[0]))
    loss[...] = jnp.maximum(-margin, 0.0) + jnp.log1p(jnp.exp(-jnp.abs(margin)))
    factor = -BETA * (1.0 / (1.0 + jnp.exp(margin))) * small[1]
    weight = factor[:, 0:1] * signed_mask
    lines = lax.broadcasted_iota(jnp.int32, (128, top.shape[1]), 0)
    packed = jnp.where(lines == 0, top, jnp.where(lines == 1, weight, 1.0 / total)).T
    for t in range(n_blocks):
        at = slice(t * rows, (t + 1) * rows)
        top_t, weight_t, inverse_t = packed[at, 0:1], packed[at, 1:2], packed[at, 2:3]
        wanted = target[t][...]
        for j, (grads, flipped) in enumerate(((grads_own, flipped_own), (grads_far, flipped_far))):
            l = logits[t][:, j * columns:(j + 1) * columns]
            column = lax.broadcasted_iota(jnp.int32, l.shape, 1) + meta[1 + j]
            hit = jnp.where(column == wanted, 1.0, 0.0)
            g = weight_t * (hit - jnp.exp(l - top_t) * inverse_t)
            grads[t] = g.astype(BF16)
            flipped[:, at] = g.T.astype(BF16)
    for copy in coming:
        copy.wait()
    spread(flipped_own[...], flipped_far[...], slots[0, 0], slots[0, 1], kept, send)


def spread_kernel(part, width, n_parts, meta, work, flipped_own, flipped_far, *refs):
    outs, slots, sems = refs[:-2], refs[-2], refs[-1]
    each = len(outs) // n_parts
    coming = [
        fetch(work, width, pl.multiple_of(meta[i] * part, part), part, slots, i, sems) for i in range(n_parts)
    ]
    for i in range(n_parts):
        for copy in coming[i]:
            copy.wait()
        kept, *send = outs[i * each:(i + 1) * each]
        spread(flipped_own[...], flipped_far[...], slots[i, 0], slots[i, 1], kept, send)


def spread_shapes(n_blocks, rows, part):
    return [shape_of((part, rows), F32)] + [shape_of((part, rows), BF16)] * (n_blocks - 1)


def weight_slots(n_parts, part, columns):
    return [pltpu.VMEM((n_parts, 2, part, columns), BF16), pltpu.SemaphoreType.DMA((n_parts, 2))]


def grads_call(logits, target, stats, small, work, meta, part, width, window):
    n_blocks, rows, columns = len(logits), logits[0].shape[0], work.shape[1]
    grads = shape_of((n_blocks, rows, columns), BF16)
    flipped = shape_of((columns, n_blocks * rows), BF16)
    out_shape = [grads, grads, flipped, flipped, shape_of((1, 128), F32)] + spread_shapes(n_blocks, rows, part)
    operands = list(logits) + list(target) + list(stats)
    return pl.pallas_call(
        functools.partial(grads_kernel, n_blocks, len(stats), columns, part, width, window),
        out_shape=out_shape,
        in_specs=[IN_SMEM] * 2 + [IN_PLACE] + [IN_VMEM] * len(operands),
        out_specs=[IN_VMEM] * len(out_shape),
        scratch_shapes=weight_slots(1, part, columns),
        compiler_params=params(),
        cost_estimate=cost(4 * n_blocks * rows * part * columns, 8 * part * columns),
    )(meta, small, work, *operands)


def spread_call(flipped_own, flipped_far, work, k_ids, part, width, rows):
    columns, n_rows = flipped_own.shape
    n_parts = len(k_ids)
    out_shape = spread_shapes(n_rows // rows, rows, part) * n_parts
    outs = pl.pallas_call(
        functools.partial(spread_kernel, part, width, n_parts),
        out_shape=out_shape,
        in_specs=[IN_SMEM] + [IN_PLACE] + [IN_VMEM] * 2,
        out_specs=[IN_VMEM] * len(out_shape),
        scratch_shapes=weight_slots(n_parts, part, columns),
        compiler_params=params(),
        cost_estimate=cost(4 * n_parts * n_rows * part * columns, 4 * n_parts * part * columns),
    )(jnp.stack(k_ids).astype(jnp.int32), work, flipped_own, flipped_far)
    each = len(outs) // n_parts
    return [(outs[i * each], list(outs[i * each + 1:(i + 1) * each])) for i in range(n_parts)]


def either_kernel(a, b, out):
    out[...] = a[...] + b[...]


def either(a, b):
    return pl.pallas_call(
        either_kernel,
        out_shape=shape_of(a.shape, a.dtype),
        in_specs=[IN_VMEM] * 2,
        out_specs=IN_VMEM,
        compiler_params=params(),
        cost_estimate=cost(a.size, 6 * a.size),
    )(a, b)


def stack_kernel(*refs):
    *arrays, out, sems = refs
    copies = [pltpu.make_async_copy(a, out.at[i], sems.at[i]) for i, a in enumerate(arrays)]
    for copy in copies:
        copy.start()
    for copy in copies:
        copy.wait()


def stack_call(arrays):
    return pl.pallas_call(
        stack_kernel,
        out_shape=shape_of((len(arrays),) + arrays[0].shape, arrays[0].dtype),
        in_specs=[IN_PLACE] * len(arrays),
        out_specs=IN_PLACE,
        scratch_shapes=[pltpu.SemaphoreType.DMA((len(arrays),))],
        compiler_params=params(),
        cost_estimate=cost(1, 4 * len(arrays) * arrays[0].size),
    )(*arrays)


def merge_kernel(turns, *refs):
    *seen, out = refs
    n_blocks, _, rows = seen[0].shape
    out[...] = jnp.zeros_like(out)
    for b in range(n_blocks):
        these = [s[(b - t) % n_blocks] for t, s in zip(turns, seen)]
        top = these[0][0:1, :]
        for s in these[1:]:
            top = jnp.maximum(top, s[0:1, :])
        at = slice(b * rows, (b + 1) * rows)
        out[0:1, at] = top
        out[1:2, at] = sum(s[1:2, :] * jnp.exp(s[0:1, :] - top) for s in these)
        out[2:3, at] = sum(s[2:3, :] for s in these)


def merge_call(turns, seen):
    n_blocks, lines, rows = seen[0].shape
    return pl.pallas_call(
        functools.partial(merge_kernel, turns),
        out_shape=shape_of((lines, n_blocks * rows), F32),
        in_specs=[IN_VMEM] * len(seen),
        out_specs=IN_VMEM,
        compiler_params=params(),
        cost_estimate=cost(1, 4 * len(seen) * n_blocks * lines * rows),
    )(*seen)


def add_kernel(turned, kept, *refs):
    total = kept[...]
    for a in refs[:-1]:
        total += a[...].astype(F32)
    refs[-1][...] = (total.T if turned else total).astype(BF16)


def add_call(kept, arrived, turned=False):
    shape = kept.shape[::-1] if turned else kept.shape
    return pl.pallas_call(
        functools.partial(add_kernel, turned),
        out_shape=shape_of(shape, BF16),
        in_specs=[IN_VMEM] * (1 + len(arrived)),
        out_specs=IN_VMEM,
        compiler_params=params(),
        cost_estimate=cost(kept.size, 4 * kept.size),
    )(kept, *arrived)


def head_kernel(slots_here, near_keys, far_keys, part, has_out, meta, *refs):
    refs = list(refs)
    grads = [refs.pop(0), refs.pop(0)]
    near = {k: refs.pop(0) for k in near_keys}
    stacks = [refs.pop(0) for _ in far_keys]
    far = {k: stack.at[i] for stack, keys in zip(stacks, far_keys) for i, k in enumerate(keys)}
    out, ready, sems = refs[has_out:]
    n_blocks, rows, columns = grads[0].shape
    right = jnp.concatenate([g[...].reshape(n_blocks * rows, columns) for g in grads])
    copies = []
    for n, i in enumerate(slots_here):
        left = jnp.concatenate([x[t, i][...] for x in (near, far) for t in range(n_blocks)])
        product = lax.dot_general(left, right, (((0,), (0,)), ((), ())), preferred_element_type=F32)
        if n >= 2:
            copies[n - 2].wait()
        ready[n % 2] = product.astype(BF16)
        start = pl.multiple_of(meta[i] * part, part)
        copies.append(pltpu.make_async_copy(ready.at[n % 2], out.at[pl.ds(start, part), :], sems.at[n % 2]))
        copies[-1].start()
    for copy in copies[-2:]:
        copy.wait()


def head_call(slots_here, near, far, grads, meta, out=None):
    n_blocks, rows, columns = grads[0].shape
    n_parts = len(near) // n_blocks
    part = near[0, 0].shape[1]
    near = {k: c for k, c in near.items() if k[1] in slots_here}
    far = [(keys, stack) for keys, stack in far if any(k[1] in slots_here for k in keys)]
    operands = list(grads) + list(near.values()) + [stack for _, stack in far]
    here = [] if out is None else [out]
    return pl.pallas_call(
        functools.partial(head_kernel, slots_here, list(near), [keys for keys, _ in far], part, len(here)),
        out_shape=shape_of((n_parts * part, columns), BF16),
        in_specs=[IN_SMEM] + [IN_VMEM] * len(operands) + [IN_PLACE] * len(here),
        out_specs=IN_PLACE,
        scratch_shapes=[pltpu.VMEM((2, part, columns), BF16), pltpu.SemaphoreType.DMA((2,))],
        input_output_aliases={1 + len(operands): 0} if here else {},
        compiler_params=pltpu.CompilerParams(vmem_limit_bytes=16 * 1024 * 1024),
        cost_estimate=cost(
            4 * n_blocks * rows * len(slots_here) * part * columns,
            4 * n_blocks * len(slots_here) * rows * part + 2 * len(slots_here) * part * columns,
        ),
    )(meta, *operands, *here)


def together(*groups):
    flat = lax.optimization_barrier([a for group in groups for a in group])
    out = []
    for group in groups:
        out.append(flat[:len(group)])
        flat = flat[len(group):]
    return out


def shards(hidden, head_weight, targets, response_start, other_sums, ref_logp, loss_cotangent):
    n_voc, n_ctx, n_dp = lax.axis_size("vocab"), lax.axis_size("ctx"), lax.axis_size("dp")
    me_voc, me_ctx, me_dp = lax.axis_index("vocab"), lax.axis_index("ctx"), lax.axis_index("dp")
    part, _, sides, window = hidden.shape
    rows = sides * window
    columns = head_weight.shape[1]
    line = n_voc == 4
    beyond = list(range(1, n_ctx))
    dp_swap = lambda a: lax.ppermute(a, "dp", ring(n_dp, 1))
    along = lambda a, by: lax.ppermute(a, "vocab", by)

    if line:
        table = [[0, 1, 2, 3], [1, 0, 2, 3], [2, 3, 1, 0], [3, 2, 1, 0]]
        part_of = [sum(jnp.where(me_voc == z, table[z][i], 0) for z in range(n_voc)) for i in range(n_voc)]
    else:
        part_of = [(me_voc - s) % n_voc for s in range(n_voc)]
    firsts = [
        ((me_voc * n_ctx + me_ctx) * n_dp + owner) * columns for owner in (me_dp, (me_dp + 1) % n_dp)
    ]
    came_from = [(me_voc - i) % n_voc for i in range(n_voc)]
    meta = jnp.stack(came_from + firsts).astype(jnp.int32)

    far_weights = dp_swap(head_weight)
    work = hold(head_weight)
    width = head_weight.shape[0]

    def mine(a):
        pair = lax.broadcasted_iota(jnp.int32, a.shape, 0)
        return jnp.sum(jnp.where(pair == me_dp, a, jnp.zeros_like(a)), axis=0)

    blocks = [mine(targets)[:, b * window:(b + 1) * window].reshape(rows) for b in range(n_ctx)]
    wanted = []
    for t in range(n_ctx):
        at = (me_ctx - t) % n_ctx
        wanted.append(sum(jnp.where(at == b, blocks[b], 0) for b in range(n_ctx))[:, None])

    own = hidden.transpose(1, 2, 3, 0).reshape(rows, part)
    final = n_voc - 1
    call = lambda *args, **more: logits_call(*args, meta=meta, part=part, n_voc=n_voc, **more)
    cross = lambda a: [lax.ppermute(a, "ctx", ring(n_ctx, t)) for t in beyond]
    chunk = {}

    def arrive(i, near, over):
        chunk[0, i] = near
        for t, a in zip(beyond, over):
            chunk[t, i] = a

    scalars = [response_start, other_sums, ref_logp, loss_cotangent]

    def prepare(begin, others, refer, cotangent):
        ratio = mine(others) - mine(refer)
        small = jnp.stack([ratio[0] - ratio[1], mine(cotangent)])
        return [small, jnp.stack([part_of[final]] + firsts + [me_ctx, mine(begin)]).astype(jnp.int32)]

    near = sorted({1, n_voc - 1})
    rest = [i for i in range(1, n_voc) if i not in near]
    came = [along(own, ring(n_voc, i)) for i in near]
    came, over, (work, meta, again) = together(came, cross(own), [work, meta, own])
    arrive(0, own, over)
    over = [cross(c) for c in came]
    for i, c, o in zip(near, came, over):
        arrive(i, c, o)
    came = [along(again, ring(n_voc, i)) for i in rest]
    logits, work = call([(0, {i: chunk[0, i] for i in [0] + near}, None, None)], work, far=far_weights)
    (logits,), raw = together([logits], scalars)
    came, wanted, (logits, small, meta_grads), *over = together(came, wanted, [logits] + prepare(*raw), *over)
    for i, o in zip(near, over):
        arrive(i, chunk[0, i], o)
    for i, c in zip(rest, came):
        arrive(i, c, cross(c))

    late = [(t, i) for i in rest for t in beyond]
    soon = [k for k in chunk if k not in late]
    done = call([(0, {i: chunk[0, i] for i in rest}, logits, wanted[0])], work)
    last, (near_logits, stats), (stacked,) = together(
        [chunk[k] for k in late], list(done), [stack_call([chunk[k] for k in soon])]
    )
    chunk.update(zip(late, last))
    *logits, stats = call(
        [(t, {i: chunk[t, i] for i in range(n_voc)}, None, wanted[t]) for t in beyond], work, earlier=[stats]
    )
    logits = [near_logits] + logits
    far_soon = dp_swap(stacked)

    if line and n_ctx == 2:
        corner = [(2 * a + c, 2 * b + (1 - c)) for a, b in PAIRS_OUT for c in range(2)]
        diagonal = lax.ppermute(stats, ("vocab", "ctx"), corner)
        merged = merge_call([0, 1, 0, 1], [stats, cross(stats)[0], along(stats, PAIRS_OUT), diagonal])
        all_stats = [merged, along(merged, SWAP_HALVES)]
    else:
        merged = merge_call([0] + beyond, [stats] + cross(stats))
        all_stats = [merged] + [along(merged, ring(n_voc, s)) for s in range(1, n_voc)]

    grads_own, grads_far, flipped_own, flipped_far, loss, kept, *send = grads_call(
        logits, wanted, all_stats, small, work, meta_grads, part, width, window
    )
    theirs, far_loss = dp_swap(grads_far), dp_swap(loss)
    far_late = dp_swap(jnp.stack(together([chunk[k] for k in late], [kept])[0]))

    back = lambda cs: [lax.ppermute(c, "ctx", ring(n_ctx, -t)) for t, c in zip(beyond, cs)]
    shares = {final: (kept, list(send))}

    def more_shares(slots):
        done = spread_call(flipped_own, flipped_far, work, [part_of[i] for i in slots], part, width, rows)
        shares.update(zip(slots, done))
        return [a for i in slots for a in [shares[i][0]] + shares[i][1]]

    def set_shares(slots, flat):
        for i in slots:
            shares[i] = (flat[0], list(flat[1:n_ctx]))
            flat = flat[n_ctx:]

    over = {}
    near_over = lambda i, *more: add_call(shares[i][0], over[i] + list(more))
    landed, grad_head = [], None
    for i in range(n_voc)[::-1]:
        over[i] = back(shares[i][1])
        came, beside = [], []
        if not line:
            came = [along(near_over(i + 1), ring(n_voc, -(i + 1)))] if i < final else []
        elif i == 2:
            came = [along(near_over(3), FROM_ENDS)]
        elif i == 1:
            came = [along(near_over(3, landed[0]), PAIR_IN), along(near_over(2), FROM_ENDS)]
        elif i == 0:
            outer = near_over(1, landed[0])
            (outer,), landed = together([outer], landed)
            came = [along(outer, PAIRS_OUT), along(near_over(2, landed[1]), PAIR_IN)]
        if i:
            beside = more_shares([i - 1])
        else:
            grad_head = head_call(list(range(n_voc)), chunk, [(soon, far_soon), (late, far_late)], [grads_own, theirs], meta)
            beside = [grad_head]
        swapped = [theirs, far_loss, far_late] if i == final - 1 else []
        over[i], came, beside, swapped = together(over[i], came, beside, swapped)
        landed = came if line else landed + came
        if i:
            set_shares([i - 1], beside)
        else:
            grad_head, = beside
        if swapped:
            theirs, far_loss, far_late = swapped
    kept = shares[0][0]
    summed = add_call(kept, over[0] + landed, turned=True)
    grad_hidden = summed.reshape(1, sides, window, part).transpose(3, 0, 1, 2)

    owner = lax.broadcasted_iota(jnp.int32, (n_dp,), 0)
    pair_loss = jnp.where(owner == me_dp, loss[0, :n_dp], far_loss[0, :n_dp])
    return (grad_hidden, grad_head, pair_loss)


def solution(mesh):
    placed = (
        P("vocab", ("groups", "dp"), None, "ctx"),
        P(None, ("vocab", "ctx", "dp")),
        P("groups", None, None),
        P("groups"),
        P("groups", None),
        P("groups", None),
        P("groups"),
    )
    return jax.shard_map(
        shards,
        mesh=mesh,
        in_specs=placed,
        out_specs=(
            P("vocab", ("groups", "dp"), None, "ctx"),
            P("groups", ("vocab", "ctx", "dp")),
            P("groups"),
        ),
        check_vma=False,
    )
```

```python
import functools

import jax
import jax.numpy as jnp
from jax import lax
from jax.experimental import pallas as pl
from jax.experimental.pallas import tpu as pltpu
from jax.sharding import PartitionSpec as P

BETA = 0.1
F32, BF16 = jnp.float32, jnp.bfloat16
VMEM_BYTES = 16 * 1024 * 1024
WORK_BYTES = 52 * 1024 * 1024
IN_VMEM = pl.BlockSpec(memory_space=pltpu.VMEM)
IN_SMEM = pl.BlockSpec(memory_space=pltpu.SMEM)
IN_PLACE = pl.BlockSpec(memory_space=pl.ANY)
PAIRS_OUT = [(0, 1), (1, 0), (2, 3), (3, 2)]
PAIR_IN = [(1, 2), (2, 1)]
TO_ENDS = [(1, 0), (2, 3)]
FROM_ENDS = [(0, 1), (3, 2)]
SWAP_HALVES = [(0, 2), (2, 0), (1, 3), (3, 1)]


def ring(count, shift):
    return [(i, (i + shift) % count) for i in range(count)]


def params():
    return pltpu.CompilerParams(vmem_limit_bytes=VMEM_BYTES)


def cost(flops, moved):
    return pl.CostEstimate(flops=int(flops), bytes_accessed=int(moved), transcendentals=0)


def shape_of(shape, kind):
    return jax.ShapeDtypeStruct(shape, kind)


def work_shape(w):
    times = max(2, -(-WORK_BYTES // (w.size * w.dtype.itemsize)))
    return shape_of((times * w.shape[0], w.shape[1]), w.dtype)


def hold_kernel(w, out, sem):
    copy = pltpu.make_async_copy(w, out.at[pl.ds(0, w.shape[0]), :], sem)
    copy.start()
    copy.wait()


def hold(w):
    return pl.pallas_call(
        hold_kernel,
        out_shape=work_shape(w),
        in_specs=[IN_PLACE],
        out_specs=IN_PLACE,
        scratch_shapes=[pltpu.SemaphoreType.DMA],
        compiler_params=params(),
        cost_estimate=cost(1, 4 * w.size),
    )(w)


def fetch(work, width, start, part, slots, i, sems, own_only=False):
    copies = []
    for j in range(1 if own_only else 2):
        source = work.at[pl.ds(j * width + start, part), :]
        copies.append(pltpu.make_async_copy(source, slots.at[i, j], sems.at[i, j]))
        copies[-1].start()
    return copies


def row_stats(own, far, wanted, first_own, first_far):
    top = jnp.max(jnp.maximum(own, far), axis=1, keepdims=True)
    total = jnp.sum(jnp.exp(own - top) + jnp.exp(far - top), axis=1, keepdims=True)
    column = lax.broadcasted_iota(jnp.int32, own.shape, 1)
    zero = jnp.zeros_like(own)
    picked = jnp.sum(
        jnp.where(column + first_own == wanted, own, zero) + jnp.where(column + first_far == wanted, far, zero),
        axis=1,
        keepdims=True,
    )
    lane = lax.broadcasted_iota(jnp.int32, (own.shape[0], 128), 1)
    return jnp.where(lane == 0, top, jnp.where(lane == 1, total, picked)).T[:8, :]


def logits_kernel(plan, columns, part, n_voc, fresh, n_earlier, meta, work, *refs):
    refs = list(refs)
    width = part * n_voc
    far = refs.pop(0) if fresh else None
    chunks = {(t, i): refs.pop(0) for t, parts, _, _ in plan for i in parts}
    accs = {t: refs.pop(0) for t, _, has_acc, _ in plan if has_acc}
    wanted = {t: refs.pop(0) for t, _, _, done in plan if done}
    earlier = [refs.pop(0) for _ in range(n_earlier)]
    used = sorted({i for _, parts, _, _ in plan for i in parts})
    starts = [pl.multiple_of(meta[i] * part, part) for i in used]
    if fresh:
        held, far_sems = refs[-2:]
        refs = refs[:-2]
        into = pltpu.make_async_copy(far, held, far_sems.at[0])
        into.start()
    slots, sems = refs[-2:]
    coming = [fetch(work, width, start, part, slots, n, sems, fresh) for n, start in enumerate(starts)]
    if fresh:
        into.wait()
        kept = pltpu.make_async_copy(held, refs[-3].at[pl.ds(width, width), :], far_sems.at[1])
        kept.start()
    outs = {t: refs.pop(0) for t, _, _, _ in plan}
    for n, i in enumerate(used):
        for copy in coming[n]:
            copy.wait()
        for t, parts, has_acc, _ in plan:
            if i not in parts:
                continue
            x = chunks[t, i][...]
            for j in range(2):
                at = slice(j * columns, (j + 1) * columns)
                w = held[pl.ds(starts[n], part), :] if fresh and j else slots[n, j]
                product = jnp.dot(x, w, preferred_element_type=F32)
                if i != parts[0]:
                    product += outs[t][:, at]
                elif has_acc:
                    product += accs[t][:, at]
                outs[t][:, at] = product
    if wanted:
        stats = refs[0]
        for n, a in enumerate(earlier):
            stats[n] = a[0]
        for n, t in enumerate(wanted, n_earlier):
            own, beside = outs[t][:, :columns], outs[t][:, columns:]
            stats[n] = row_stats(own, beside, wanted[t][...], meta[n_voc], meta[n_voc + 1])
    if fresh:
        kept.wait()


def logits_call(plan, work, meta, part, n_voc, far=None, earlier=()):
    columns = work.shape[1]
    accs = [acc for _, _, acc, _ in plan if acc is not None]
    wanted = [w for _, _, _, w in plan if w is not None]
    chunks = [parts[i] for _, parts, _, _ in plan for i in sorted(parts)]
    rows = chunks[0].shape[0]
    out_shape = [shape_of((rows, 2 * columns), F32)] * len(plan)
    if wanted:
        out_shape.append(shape_of((len(earlier) + len(wanted), 8, rows), F32))
    out_specs = [IN_VMEM] * len(out_shape)
    kernel_plan = [(t, sorted(parts), acc is not None, w is not None) for t, parts, acc, w in plan]
    n_used = len({i for _, parts, _, _ in plan for i in parts})
    fresh = far is not None
    in_place = [work] + ([far] if fresh else [])
    if fresh:
        out_shape.append(shape_of(work.shape, work.dtype))
        out_specs.append(IN_PLACE)
    operands = chunks + accs + wanted + list(earlier)
    return pl.pallas_call(
        functools.partial(logits_kernel, kernel_plan, columns, part, n_voc, fresh, len(earlier)),
        out_shape=out_shape,
        in_specs=[IN_SMEM] + [IN_PLACE] * len(in_place) + [IN_VMEM] * len(operands),
        out_specs=out_specs,
        scratch_shapes=[pltpu.VMEM((n_used, 2 - fresh, part, columns), BF16), pltpu.SemaphoreType.DMA((n_used, 2))]
        + ([pltpu.VMEM((part * n_voc, columns), BF16), pltpu.SemaphoreType.DMA((2,))] if fresh else []),
        input_output_aliases={1: len(out_shape) - 1} if fresh else {},
        compiler_params=params(),
        cost_estimate=cost(4 * len(chunks) * rows * part * columns, n_used * 4 * part * columns),
    )(meta, *in_place, *operands)


def spread(flipped_own, flipped_far, w_own, w_far, kept, send):
    rows = kept.shape[1]
    here = jnp.dot(w_own, flipped_own, preferred_element_type=F32)
    here += jnp.dot(w_far, flipped_far, preferred_element_type=F32)
    kept[...] = here[:, :rows]
    for t, out in enumerate(send, 1):
        out[...] = here[:, t * rows:(t + 1) * rows].astype(BF16)


def grads_kernel(n_blocks, n_stats, columns, part, width, window, meta, small, work, *refs):
    refs = list(refs)
    logits = [refs.pop(0) for _ in range(n_blocks)]
    target = [refs.pop(0) for _ in range(n_blocks)]
    stats = [refs.pop(0) for _ in range(n_stats)]
    slots, sems = refs[-2:]
    grads_own, grads_far, flipped_own, flipped_far, loss, kept = refs[:6]
    send = refs[6:-2]
    coming = fetch(work, width, pl.multiple_of(meta[0] * part, part), part, slots, 0, sems)
    rows = logits[0].shape[0]
    me_ctx, start = meta[3], meta[4]
    top = stats[0][0:1, :]
    for s in stats[1:]:
        top = jnp.maximum(top, s[0:1, :])
    total = jnp.zeros_like(top)
    picked = jnp.zeros_like(top)
    for s in stats:
        total += s[1:2, :] * jnp.exp(s[0:1, :] - top)
        picked += s[2:3, :]
    row = lax.broadcasted_iota(jnp.int32, (1, rows), 1)
    masks = []
    for t in range(n_blocks):
        block = lax.rem(me_ctx + (n_blocks - t), n_blocks)
        seen = lax.rem(row, window) + block * window >= start
        masks.append(jnp.where(seen, jnp.where(row < window, 1.0, -1.0), 0.0))
    signed_mask = jnp.concatenate(masks, axis=1)
    token_logp = picked - top - jnp.log(total)
    zeros = jnp.zeros((1, 128), F32)
    margin = BETA * (jnp.sum(signed_mask * token_logp, axis=1, keepdims=True) + (zeros + small[0]))
    loss[...] = jnp.maximum(-margin, 0.0) + jnp.log1p(jnp.exp(-jnp.abs(margin)))
    factor = -BETA * (1.0 / (1.0 + jnp.exp(margin))) * small[1]
    weight = factor[:, 0:1] * signed_mask
    lines = lax.broadcasted_iota(jnp.int32, (128, top.shape[1]), 0)
    packed = jnp.where(lines == 0, top, jnp.where(lines == 1, weight, 1.0 / total)).T
    for t in range(n_blocks):
        at = slice(t * rows, (t + 1) * rows)
        top_t, weight_t, inverse_t = packed[at, 0:1], packed[at, 1:2], packed[at, 2:3]
        wanted = target[t][...]
        for j, (grads, flipped) in enumerate(((grads_own, flipped_own), (grads_far, flipped_far))):
            l = logits[t][:, j * columns:(j + 1) * columns]
            column = lax.broadcasted_iota(jnp.int32, l.shape, 1) + meta[1 + j]
            hit = jnp.where(column == wanted, 1.0, 0.0)
            g = weight_t * (hit - jnp.exp(l - top_t) * inverse_t)
            grads[t] = g.astype(BF16)
            flipped[:, at] = g.T.astype(BF16)
    for copy in coming:
        copy.wait()
    spread(flipped_own[...], flipped_far[...], slots[0, 0], slots[0, 1], kept, send)


def spread_kernel(part, width, n_parts, meta, work, flipped_own, flipped_far, *refs):
    outs, slots, sems = refs[:-2], refs[-2], refs[-1]
    each = len(outs) // n_parts
    coming = [
        fetch(work, width, pl.multiple_of(meta[i] * part, part), part, slots, i, sems) for i in range(n_parts)
    ]
    for i in range(n_parts):
        for copy in coming[i]:
            copy.wait()
        kept, *send = outs[i * each:(i + 1) * each]
        spread(flipped_own[...], flipped_far[...], slots[i, 0], slots[i, 1], kept, send)


def spread_shapes(n_blocks, rows, part):
    return [shape_of((part, rows), F32)] + [shape_of((part, rows), BF16)] * (n_blocks - 1)


def weight_slots(n_parts, part, columns):
    return [pltpu.VMEM((n_parts, 2, part, columns), BF16), pltpu.SemaphoreType.DMA((n_parts, 2))]


def grads_call(logits, target, stats, small, work, meta, part, width, window):
    n_blocks, rows, columns = len(logits), logits[0].shape[0], work.shape[1]
    grads = shape_of((n_blocks, rows, columns), BF16)
    flipped = shape_of((columns, n_blocks * rows), BF16)
    out_shape = [grads, grads, flipped, flipped, shape_of((1, 128), F32)] + spread_shapes(n_blocks, rows, part)
    operands = list(logits) + list(target) + list(stats)
    return pl.pallas_call(
        functools.partial(grads_kernel, n_blocks, len(stats), columns, part, width, window),
        out_shape=out_shape,
        in_specs=[IN_SMEM] * 2 + [IN_PLACE] + [IN_VMEM] * len(operands),
        out_specs=[IN_VMEM] * len(out_shape),
        scratch_shapes=weight_slots(1, part, columns),
        compiler_params=params(),
        cost_estimate=cost(4 * n_blocks * rows * part * columns, 8 * part * columns),
    )(meta, small, work, *operands)


def spread_call(flipped_own, flipped_far, work, k_ids, part, width, rows):
    columns, n_rows = flipped_own.shape
    n_parts = len(k_ids)
    out_shape = spread_shapes(n_rows // rows, rows, part) * n_parts
    outs = pl.pallas_call(
        functools.partial(spread_kernel, part, width, n_parts),
        out_shape=out_shape,
        in_specs=[IN_SMEM] + [IN_PLACE] + [IN_VMEM] * 2,
        out_specs=[IN_VMEM] * len(out_shape),
        scratch_shapes=weight_slots(n_parts, part, columns),
        compiler_params=params(),
        cost_estimate=cost(4 * n_parts * n_rows * part * columns, 4 * n_parts * part * columns),
    )(jnp.stack(k_ids).astype(jnp.int32), work, flipped_own, flipped_far)
    each = len(outs) // n_parts
    return [(outs[i * each], list(outs[i * each + 1:(i + 1) * each])) for i in range(n_parts)]


def either_kernel(a, b, out):
    out[...] = a[...] + b[...]


def either(a, b):
    return pl.pallas_call(
        either_kernel,
        out_shape=shape_of(a.shape, a.dtype),
        in_specs=[IN_VMEM] * 2,
        out_specs=IN_VMEM,
        compiler_params=params(),
        cost_estimate=cost(a.size, 6 * a.size),
    )(a, b)


def stack_kernel(*refs):
    *arrays, out, sems = refs
    copies = [pltpu.make_async_copy(a, out.at[i], sems.at[i]) for i, a in enumerate(arrays)]
    for copy in copies:
        copy.start()
    for copy in copies:
        copy.wait()


def stack_call(arrays):
    return pl.pallas_call(
        stack_kernel,
        out_shape=shape_of((len(arrays),) + arrays[0].shape, arrays[0].dtype),
        in_specs=[IN_PLACE] * len(arrays),
        out_specs=IN_PLACE,
        scratch_shapes=[pltpu.SemaphoreType.DMA((len(arrays),))],
        compiler_params=params(),
        cost_estimate=cost(1, 4 * len(arrays) * arrays[0].size),
    )(*arrays)


def merge_kernel(turns, *refs):
    *seen, out = refs
    n_blocks, _, rows = seen[0].shape
    out[...] = jnp.zeros_like(out)
    for b in range(n_blocks):
        these = [s[(b - t) % n_blocks] for t, s in zip(turns, seen)]
        top = these[0][0:1, :]
        for s in these[1:]:
            top = jnp.maximum(top, s[0:1, :])
        at = slice(b * rows, (b + 1) * rows)
        out[0:1, at] = top
        out[1:2, at] = sum(s[1:2, :] * jnp.exp(s[0:1, :] - top) for s in these)
        out[2:3, at] = sum(s[2:3, :] for s in these)


def merge_call(turns, seen):
    n_blocks, lines, rows = seen[0].shape
    return pl.pallas_call(
        functools.partial(merge_kernel, turns),
        out_shape=shape_of((lines, n_blocks * rows), F32),
        in_specs=[IN_VMEM] * len(seen),
        out_specs=IN_VMEM,
        compiler_params=params(),
        cost_estimate=cost(1, 4 * len(seen) * n_blocks * lines * rows),
    )(*seen)


def add_kernel(turned, kept, *refs):
    total = kept[...]
    for a in refs[:-1]:
        total += a[...].astype(F32)
    refs[-1][...] = (total.T if turned else total).astype(BF16)


def add_call(kept, arrived, turned=False):
    shape = kept.shape[::-1] if turned else kept.shape
    return pl.pallas_call(
        functools.partial(add_kernel, turned),
        out_shape=shape_of(shape, BF16),
        in_specs=[IN_VMEM] * (1 + len(arrived)),
        out_specs=IN_VMEM,
        compiler_params=params(),
        cost_estimate=cost(kept.size, 4 * kept.size),
    )(kept, *arrived)


def head_kernel(slots_here, keys_of, part, meta, *refs):
    refs = list(refs)
    grads = [refs.pop(0), refs.pop(0)]
    near, far = {}, {}
    for chunks in (near, far):
        for keys in keys_of:
            stack = refs.pop(0)
            chunks.update((k, stack.at[i]) for i, k in enumerate(keys))
    out, ready, sems = refs
    n_blocks, rows, columns = grads[0].shape
    right = jnp.concatenate([g[...].reshape(n_blocks * rows, columns) for g in grads])
    copies = []
    for n, i in enumerate(slots_here):
        left = jnp.concatenate([x[t, i][...] for x in (near, far) for t in range(n_blocks)])
        product = lax.dot_general(left, right, (((0,), (0,)), ((), ())), preferred_element_type=F32)
        if n >= 2:
            copies[n - 2].wait()
        ready[n % 2] = product.astype(BF16)
        start = pl.multiple_of(meta[i] * part, part)
        copies.append(pltpu.make_async_copy(ready.at[n % 2], out.at[pl.ds(start, part), :], sems.at[n % 2]))
        copies[-1].start()
    for copy in copies[-2:]:
        copy.wait()


def head_call(keys_of, near, far, grads, meta):
    n_blocks, rows, columns = grads[0].shape
    n_parts = sum(len(keys) for keys in keys_of) // n_blocks
    part = near[0].shape[2]
    slots_here = list(range(n_parts))
    operands = list(grads) + list(near) + list(far)
    return pl.pallas_call(
        functools.partial(head_kernel, slots_here, keys_of, part),
        out_shape=shape_of((n_parts * part, columns), BF16),
        in_specs=[IN_SMEM] + [IN_VMEM] * len(operands),
        out_specs=IN_PLACE,
        scratch_shapes=[pltpu.VMEM((2, part, columns), BF16), pltpu.SemaphoreType.DMA((2,))],
        compiler_params=params(),
        cost_estimate=cost(
            4 * n_blocks * rows * n_parts * part * columns,
            4 * n_blocks * n_parts * rows * part + 2 * n_parts * part * columns,
        ),
    )(meta, *operands)


def together(*groups):
    flat = lax.optimization_barrier([a for group in groups for a in group])
    out = []
    for group in groups:
        out.append(flat[:len(group)])
        flat = flat[len(group):]
    return out


def shards(hidden, head_weight, targets, response_start, other_sums, ref_logp, loss_cotangent):
    n_voc, n_ctx, n_dp = lax.axis_size("vocab"), lax.axis_size("ctx"), lax.axis_size("dp")
    me_voc, me_ctx, me_dp = lax.axis_index("vocab"), lax.axis_index("ctx"), lax.axis_index("dp")
    part, _, sides, window = hidden.shape
    rows = sides * window
    columns = head_weight.shape[1]
    line = n_voc == 4
    beyond = list(range(1, n_ctx))
    dp_swap = lambda a: lax.ppermute(a, "dp", ring(n_dp, 1))
    along = lambda a, by: lax.ppermute(a, "vocab", by)

    if line:
        table = [[0, 1, 2, 3], [1, 0, 2, 3], [2, 3, 1, 0], [3, 2, 1, 0]]
        part_of = [sum(jnp.where(me_voc == z, table[z][i], 0) for z in range(n_voc)) for i in range(n_voc)]
    else:
        part_of = [(me_voc - s) % n_voc for s in range(n_voc)]
    firsts = [
        ((me_voc * n_ctx + me_ctx) * n_dp + owner) * columns for owner in (me_dp, (me_dp + 1) % n_dp)
    ]
    came_from = [(me_voc - i) % n_voc for i in range(n_voc)]
    meta = jnp.stack(came_from + firsts).astype(jnp.int32)

    far_weights = dp_swap(head_weight)
    work = hold(head_weight)
    width = head_weight.shape[0]

    def mine(a):
        pair = lax.broadcasted_iota(jnp.int32, a.shape, 0)
        return jnp.sum(jnp.where(pair == me_dp, a, jnp.zeros_like(a)), axis=0)

    blocks = [mine(targets)[:, b * window:(b + 1) * window].reshape(rows) for b in range(n_ctx)]
    wanted = []
    for t in range(n_ctx):
        at = (me_ctx - t) % n_ctx
        wanted.append(sum(jnp.where(at == b, blocks[b], 0) for b in range(n_ctx))[:, None])

    own = hidden.transpose(1, 2, 3, 0).reshape(rows, part)
    final = n_voc - 1
    call = lambda *args, **more: logits_call(*args, meta=meta, part=part, n_voc=n_voc, **more)
    cross = lambda a: [lax.ppermute(a, "ctx", ring(n_ctx, t)) for t in beyond]
    chunk = {}

    def arrive(i, near, over):
        chunk[0, i] = near
        for t, a in zip(beyond, over):
            chunk[t, i] = a

    scalars = [response_start, other_sums, ref_logp, loss_cotangent]

    def prepare(begin, others, refer, cotangent):
        ratio = mine(others) - mine(refer)
        small = jnp.stack([ratio[0] - ratio[1], mine(cotangent)])
        return [small, jnp.stack([part_of[final]] + firsts + [me_ctx, mine(begin)]).astype(jnp.int32)]

    near = sorted({1, n_voc - 1})
    rest = [i for i in range(1, n_voc) if i not in near]
    came = [along(own, ring(n_voc, i)) for i in near]
    came, over, (work, meta, again) = together(came, cross(own), [work, meta, own])
    arrive(0, own, over)
    over = [cross(c) for c in came]
    for i, c, o in zip(near, came, over):
        arrive(i, c, o)
    came = [along(again, ring(n_voc, i)) for i in rest]
    logits, work = call([(0, {i: chunk[0, i] for i in [0] + near}, None, None)], work, far=far_weights)
    (logits,), raw = together([logits], scalars)
    came, wanted, (logits, small, meta_grads), *over = together(came, wanted, [logits] + prepare(*raw), *over)
    for i, o in zip(near, over):
        arrive(i, chunk[0, i], o)
    for i, c in zip(rest, came):
        arrive(i, c, cross(c))

    late = [(t, i) for i in rest for t in beyond]
    soon = [k for k in chunk if k not in late]
    done = call([(0, {i: chunk[0, i] for i in rest}, logits, wanted[0])], work)
    last, (near_logits, stats), (stacked,) = together(
        [chunk[k] for k in late], list(done), [stack_call([chunk[k] for k in soon])]
    )
    chunk.update(zip(late, last))
    *logits, stats = call(
        [(t, {i: chunk[t, i] for i in range(n_voc)}, None, wanted[t]) for t in beyond], work, earlier=[stats]
    )
    logits = [near_logits] + logits
    far_soon = dp_swap(stacked)

    if line and n_ctx == 2:
        corner = [(2 * a + c, 2 * b + (1 - c)) for a, b in PAIRS_OUT for c in range(2)]
        diagonal = lax.ppermute(stats, ("vocab", "ctx"), corner)
        merged = merge_call([0, 1, 0, 1], [stats, cross(stats)[0], along(stats, PAIRS_OUT), diagonal])
        all_stats = [merged, along(merged, SWAP_HALVES)]
    else:
        merged = merge_call([0] + beyond, [stats] + cross(stats))
        all_stats = [merged] + [along(merged, ring(n_voc, s)) for s in range(1, n_voc)]

    grads_own, grads_far, flipped_own, flipped_far, loss, kept, *send = grads_call(
        logits, wanted, all_stats, small, work, meta_grads, part, width, window
    )
    theirs, far_loss = dp_swap(grads_far), dp_swap(loss)
    near_late = jnp.stack(together([chunk[k] for k in late], [kept])[0])
    far_late = dp_swap(near_late)

    back = lambda cs: [lax.ppermute(c, "ctx", ring(n_ctx, -t)) for t, c in zip(beyond, cs)]
    shares = {final: (kept, list(send))}

    def more_shares(slots):
        done = spread_call(flipped_own, flipped_far, work, [part_of[i] for i in slots], part, width, rows)
        shares.update(zip(slots, done))
        return [a for i in slots for a in [shares[i][0]] + shares[i][1]]

    def set_shares(slots, flat):
        for i in slots:
            shares[i] = (flat[0], list(flat[1:n_ctx]))
            flat = flat[n_ctx:]

    over = {}
    near_over = lambda i, *more: add_call(shares[i][0], over[i] + list(more))
    landed, grad_head = [], None
    for i in range(n_voc)[::-1]:
        over[i] = back(shares[i][1])
        came, beside = [], []
        if not line:
            came = [along(near_over(i + 1), ring(n_voc, -(i + 1)))] if i < final else []
        elif i == 2:
            came = [along(near_over(3), FROM_ENDS)]
        elif i == 1:
            came = [along(near_over(3, landed[0]), PAIR_IN), along(near_over(2), FROM_ENDS)]
        elif i == 0:
            outer = near_over(1, landed[0])
            (outer,), landed = together([outer], landed)
            came = [along(outer, PAIRS_OUT), along(near_over(2, landed[1]), PAIR_IN)]
        if i:
            beside = more_shares([i - 1])
        else:
            grad_head = head_call([soon, late], [stacked, near_late], [far_soon, far_late], [grads_own, theirs], meta)
            beside = [grad_head]
        swapped = [theirs, far_loss, far_late] if i == final - 1 else []
        over[i], came, beside, swapped = together(over[i], came, beside, swapped)
        landed = came if line else landed + came
        if i:
            set_shares([i - 1], beside)
        else:
            grad_head, = beside
        if swapped:
            theirs, far_loss, far_late = swapped
    kept = shares[0][0]
    summed = add_call(kept, over[0] + landed, turned=True)
    grad_hidden = summed.reshape(1, sides, window, part).transpose(3, 0, 1, 2)

    owner = lax.broadcasted_iota(jnp.int32, (n_dp,), 0)
    pair_loss = jnp.where(owner == me_dp, loss[0, :n_dp], far_loss[0, :n_dp])
    return (grad_hidden, grad_head, pair_loss)


def solution(mesh):
    placed = (
        P("vocab", ("groups", "dp"), None, "ctx"),
        P(None, ("vocab", "ctx", "dp")),
        P("groups", None, None),
        P("groups"),
        P("groups", None),
        P("groups", None),
        P("groups"),
    )
    return jax.shard_map(
        shards,
        mesh=mesh,
        in_specs=placed,
        out_specs=(
            P("vocab", ("groups", "dp"), None, "ctx"),
            P("groups", ("vocab", "ctx", "dp")),
            P("groups"),
        ),
        check_vma=False,
    )
```

```python
import functools

import jax
import jax.numpy as jnp
from jax import lax
from jax.experimental import pallas as pl
from jax.experimental.pallas import tpu as pltpu
from jax.sharding import PartitionSpec as P

BETA = 0.1
F32, BF16 = jnp.float32, jnp.bfloat16
VMEM_BYTES = 16 * 1024 * 1024
IN_VMEM = pl.BlockSpec(memory_space=pltpu.VMEM)
IN_SMEM = pl.BlockSpec(memory_space=pltpu.SMEM)
IN_PLACE = pl.BlockSpec(memory_space=pl.ANY)
PAIRS_OUT = [(0, 1), (1, 0), (2, 3), (3, 2)]
PAIR_IN = [(1, 2), (2, 1)]
FROM_ENDS = [(0, 1), (3, 2)]
SWAP_HALVES = [(0, 2), (2, 0), (1, 3), (3, 1)]


def ring(count, shift):
    return [(i, (i + shift) % count) for i in range(count)]


def params():
    return pltpu.CompilerParams(vmem_limit_bytes=VMEM_BYTES)


def cost(flops, moved):
    return pl.CostEstimate(flops=int(flops), bytes_accessed=int(moved), transcendentals=0)


def shape_of(shape, kind):
    return jax.ShapeDtypeStruct(shape, kind)


def fetch(w_own, w_far, start, part, slots, i, sems):
    copies = []
    for j, w in enumerate((w_own, w_far)):
        copies.append(pltpu.make_async_copy(w.at[pl.ds(start, part), :], slots.at[i, j], sems.at[i, j]))
        copies[-1].start()
    return copies


def row_stats(own, far, wanted, first_own, first_far):
    top = jnp.max(jnp.maximum(own, far), axis=1, keepdims=True)
    total = jnp.sum(jnp.exp(own - top) + jnp.exp(far - top), axis=1, keepdims=True)
    column = lax.broadcasted_iota(jnp.int32, own.shape, 1)
    zero = jnp.zeros_like(own)
    picked = jnp.sum(
        jnp.where(column + first_own == wanted, own, zero) + jnp.where(column + first_far == wanted, far, zero),
        axis=1,
        keepdims=True,
    )
    lane = lax.broadcasted_iota(jnp.int32, (own.shape[0], 128), 1)
    return jnp.where(lane == 0, top, jnp.where(lane == 1, total, picked)).T[:8, :]


def logits_kernel(plan, columns, part, n_voc, meta, w_own, w_far, *refs):
    refs = list(refs)
    chunks = {(t, i): refs.pop(0) for t, parts, _, _ in plan for i in parts}
    accs = {t: refs.pop(0) for t, _, has_acc, _ in plan if has_acc}
    wanted = {t: refs.pop(0) for t, _, _, done in plan if done}
    slots, sems = refs[-2:]
    used = sorted({i for _, parts, _, _ in plan for i in parts})
    coming = [fetch(w_own, w_far, pl.multiple_of(meta[i] * part, part), part, slots, n, sems) for n, i in enumerate(used)]
    outs = {}
    stats = {}
    for t, _, _, done in plan:
        outs[t] = refs.pop(0)
        if done:
            stats[t] = refs.pop(0)
    for n, i in enumerate(used):
        for copy in coming[n]:
            copy.wait()
        for t, parts, has_acc, _ in plan:
            if i not in parts:
                continue
            x = chunks[t, i][...]
            for j in range(2):
                at = slice(j * columns, (j + 1) * columns)
                product = jnp.dot(x, slots[n, j], preferred_element_type=F32)
                if i != parts[0]:
                    product += outs[t][:, at]
                elif has_acc:
                    product += accs[t][:, at]
                outs[t][:, at] = product
    for t in stats:
        own, far = outs[t][:, :columns], outs[t][:, columns:]
        stats[t][...] = row_stats(own, far, wanted[t][...], meta[n_voc], meta[n_voc + 1])


def logits_call(plan, meta, weights, part, n_voc):
    columns = weights[0].shape[1]
    chunks = [c for _, parts, _, _ in plan for c in parts.values()]
    accs = [acc for _, _, acc, _ in plan if acc is not None]
    wanted = [w for _, _, _, w in plan if w is not None]
    rows = chunks[0].shape[0]
    out_shape = []
    for _, _, _, w in plan:
        out_shape.append(shape_of((rows, 2 * columns), F32))
        if w is not None:
            out_shape.append(shape_of((8, rows), F32))
    kernel_plan = [(t, sorted(parts), acc is not None, w is not None) for t, parts, acc, w in plan]
    chunks = [parts[i] for _, parts, _, _ in plan for i in sorted(parts)]
    n_used = len({i for _, parts, _, _ in plan for i in parts})
    operands = chunks + accs + wanted
    return pl.pallas_call(
        functools.partial(logits_kernel, kernel_plan, columns, part, n_voc),
        out_shape=out_shape,
        in_specs=[IN_SMEM, IN_PLACE, IN_PLACE] + [IN_VMEM] * len(operands),
        out_specs=[IN_VMEM] * len(out_shape),
        scratch_shapes=[pltpu.VMEM((n_used, 2, part, columns), BF16), pltpu.SemaphoreType.DMA((n_used, 2))],
        compiler_params=params(),
        cost_estimate=cost(4 * len(chunks) * rows * part * columns, n_used * 4 * part * columns),
    )(meta, *weights, *operands)


def spread(flipped_own, flipped_far, w_own, w_far, kept, send):
    rows = kept.shape[1]
    here = jnp.dot(w_own, flipped_own, preferred_element_type=F32)
    here += jnp.dot(w_far, flipped_far, preferred_element_type=F32)
    kept[...] = here[:, :rows]
    for t, out in enumerate(send, 1):
        out[...] = here[:, t * rows:(t + 1) * rows].astype(BF16)


def grads_kernel(n_blocks, n_stats, columns, part, window, meta, start, sums, refer, cotangent, w_own, w_far, *refs):
    refs = list(refs)
    logits = [refs.pop(0) for _ in range(n_blocks)]
    target = refs.pop(0)
    stats = [refs.pop(0) for _ in range(n_stats)]
    slots, sems = refs[-2:]
    grads_own, grads_far, flipped_own, flipped_far, loss, kept = refs[:6]
    send = refs[6:-2]
    coming = fetch(w_own, w_far, pl.multiple_of(meta[0] * part, part), part, slots, 0, sems)
    rows = logits[0].shape[0]
    pair, me_ctx = meta[3], meta[4]
    top = stats[0][0:1, :]
    for s in stats[1:]:
        top = jnp.maximum(top, s[0:1, :])
    total = jnp.zeros_like(top)
    picked = jnp.zeros_like(top)
    for s in stats:
        total += s[1:2, :] * jnp.exp(s[0:1, :] - top)
        picked += s[2:3, :]
    row = lax.broadcasted_iota(jnp.int32, (1, rows), 1)
    masks = []
    for t in range(n_blocks):
        block = lax.rem(me_ctx + (n_blocks - t), n_blocks)
        seen = lax.rem(row, window) + block * window >= start[pair]
        masks.append(jnp.where(seen, jnp.where(row < window, 1.0, -1.0), 0.0))
    signed_mask = jnp.concatenate(masks, axis=1)
    token_logp = picked - top - jnp.log(total)
    offset = (sums[pair, 0] - refer[pair, 0]) - (sums[pair, 1] - refer[pair, 1])
    zeros = jnp.zeros((1, 128), F32)
    margin = BETA * (jnp.sum(signed_mask * token_logp, axis=1, keepdims=True) + (zeros + offset))
    loss[...] = jnp.maximum(-margin, 0.0) + jnp.log1p(jnp.exp(-jnp.abs(margin)))
    factor = -BETA * (1.0 / (1.0 + jnp.exp(margin))) * cotangent[pair]
    weight = factor[:, 0:1] * signed_mask
    lines = lax.broadcasted_iota(jnp.int32, (128, top.shape[1]), 0)
    packed = jnp.where(lines == 0, top, jnp.where(lines == 1, weight, 1.0 / total)).T
    for t in range(n_blocks):
        at = slice(t * rows, (t + 1) * rows)
        top_t, weight_t, inverse_t = packed[at, 0:1], packed[at, 1:2], packed[at, 2:3]
        wanted = target[at, :]
        for j, (grads, flipped) in enumerate(((grads_own, flipped_own), (grads_far, flipped_far))):
            l = logits[t][:, j * columns:(j + 1) * columns]
            column = lax.broadcasted_iota(jnp.int32, l.shape, 1) + meta[1 + j]
            hit = jnp.where(column == wanted, 1.0, 0.0)
            g = weight_t * (hit - jnp.exp(l - top_t) * inverse_t)
            grads[t] = g.astype(BF16)
            flipped[:, at] = g.T.astype(BF16)
    for copy in coming:
        copy.wait()
    spread(flipped_own[...], flipped_far[...], slots[0, 0], slots[0, 1], kept, send)


def spread_kernel(part, meta, w_own, w_far, flipped_own, flipped_far, kept, *rest):
    send, slots, sems = rest[:-2], rest[-2], rest[-1]
    coming = fetch(w_own, w_far, pl.multiple_of(meta[0] * part, part), part, slots, 0, sems)
    for copy in coming:
        copy.wait()
    spread(flipped_own[...], flipped_far[...], slots[0, 0], slots[0, 1], kept, send)


def spread_shapes(n_blocks, rows, part):
    return [shape_of((part, rows), F32)] + [shape_of((part, rows), BF16)] * (n_blocks - 1)


def weight_slots(part, columns):
    return [pltpu.VMEM((1, 2, part, columns), BF16), pltpu.SemaphoreType.DMA((1, 2))]


def grads_call(logits, target, stats, small, weights, meta, part, window):
    n_blocks, rows, columns = len(logits), logits[0].shape[0], weights[0].shape[1]
    grads = shape_of((n_blocks, rows, columns), BF16)
    flipped = shape_of((columns, n_blocks * rows), BF16)
    out_shape = [grads, grads, flipped, flipped, shape_of((1, 128), F32)] + spread_shapes(n_blocks, rows, part)
    operands = list(logits) + [target] + list(stats)
    return pl.pallas_call(
        functools.partial(grads_kernel, n_blocks, len(stats), columns, part, window),
        out_shape=out_shape,
        in_specs=[IN_SMEM] * 5 + [IN_PLACE] * 2 + [IN_VMEM] * len(operands),
        out_specs=[IN_VMEM] * len(out_shape),
        scratch_shapes=weight_slots(part, columns),
        compiler_params=params(),
        cost_estimate=cost(4 * n_blocks * rows * part * columns, 8 * part * columns),
    )(meta, *small, *weights, *operands)


def spread_call(flipped_own, flipped_far, weights, k_id, part, rows):
    columns, n_rows = flipped_own.shape
    out_shape = spread_shapes(n_rows // rows, rows, part)
    return pl.pallas_call(
        functools.partial(spread_kernel, part),
        out_shape=out_shape,
        in_specs=[IN_SMEM] + [IN_PLACE] * 2 + [IN_VMEM] * 2,
        out_specs=[IN_VMEM] * len(out_shape),
        scratch_shapes=weight_slots(part, columns),
        compiler_params=params(),
        cost_estimate=cost(4 * n_rows * part * columns, 4 * part * columns),
    )(k_id.reshape(1).astype(jnp.int32), *weights, flipped_own, flipped_far)


def add_kernel(turned, kept, *refs):
    total = kept[...]
    for a in refs[:-1]:
        total += a[...].astype(F32)
    refs[-1][...] = (total.T if turned else total).astype(BF16)


def add_call(kept, arrived, turned=False):
    shape = kept.shape[::-1] if turned else kept.shape
    return pl.pallas_call(
        functools.partial(add_kernel, turned),
        out_shape=shape_of(shape, BF16),
        in_specs=[IN_VMEM] * (1 + len(arrived)),
        out_specs=IN_VMEM,
        compiler_params=params(),
        cost_estimate=cost(kept.size, 4 * kept.size),
    )(kept, *arrived)


def head_kernel(near_keys, far_keys, n_parts, part, meta, *refs):
    refs = list(refs)
    grads = [refs.pop(0), refs.pop(0)]
    near = {k: refs.pop(0) for k in near_keys}
    stacks = [refs.pop(0) for _ in far_keys]
    far = {k: stack.at[i] for stack, keys in zip(stacks, far_keys) for i, k in enumerate(keys)}
    out, slots, sems = refs
    n_blocks, rows, columns = grads[0].shape
    right = jnp.concatenate([g[...].reshape(n_blocks * rows, columns) for g in grads])
    copies = []
    for i in range(n_parts):
        left = jnp.concatenate([x[t, i][...] for x in (near, far) for t in range(n_blocks)])
        product = lax.dot_general(left, right, (((0,), (0,)), ((), ())), preferred_element_type=F32)
        if i >= 2:
            copies[i - 2].wait()
        slots[i % 2] = product.astype(BF16)
        start = pl.multiple_of(meta[i] * part, part)
        copies.append(pltpu.make_async_copy(slots.at[i % 2], out.at[pl.ds(start, part), :], sems.at[i % 2]))
        copies[-1].start()
    for copy in copies[-2:]:
        copy.wait()


def head_call(near, far, grads, meta):
    n_blocks, rows, columns = grads[0].shape
    n_parts = len(near) // n_blocks
    part = near[0, 0].shape[1]
    operands = list(grads) + list(near.values()) + [stack for _, stack in far]
    return pl.pallas_call(
        functools.partial(head_kernel, list(near), [keys for keys, _ in far], n_parts, part),
        out_shape=shape_of((n_parts * part, columns), BF16),
        in_specs=[IN_SMEM] + [IN_VMEM] * len(operands),
        out_specs=pl.BlockSpec(memory_space=pl.ANY),
        scratch_shapes=[pltpu.VMEM((2, part, columns), BF16), pltpu.SemaphoreType.DMA((2,))],
        compiler_params=params(),
        cost_estimate=cost(
            4 * n_blocks * rows * n_parts * part * columns,
            4 * n_blocks * n_parts * rows * part + 2 * n_parts * part * columns,
        ),
    )(meta, *operands)


def together(*groups):
    flat = lax.optimization_barrier([a for group in groups for a in group])
    out = []
    for group in groups:
        out.append(flat[:len(group)])
        flat = flat[len(group):]
    return out


def shards(hidden, head_weight, targets, response_start, other_sums, ref_logp, loss_cotangent):
    n_voc, n_ctx, n_dp = lax.axis_size("vocab"), lax.axis_size("ctx"), lax.axis_size("dp")
    me_voc, me_ctx, me_dp = lax.axis_index("vocab"), lax.axis_index("ctx"), lax.axis_index("dp")
    part, _, sides, window = hidden.shape
    rows = sides * window
    columns = head_weight.shape[1]
    line = n_voc == 4
    beyond = list(range(1, n_ctx))
    dp_swap = lambda a: lax.ppermute(a, "dp", ring(n_dp, 1))
    along = lambda a, by: lax.ppermute(a, "vocab", by)

    if line:
        table = [[0, 1, 2, 3], [1, 0, 2, 3], [2, 3, 1, 0], [3, 2, 1, 0]]
        part_of = [sum(jnp.where(me_voc == z, table[z][i], 0) for z in range(n_voc)) for i in range(n_voc)]
    else:
        part_of = [(me_voc - s) % n_voc for s in range(n_voc)]
    firsts = [
        ((me_voc * n_ctx + me_ctx) * n_dp + owner) * columns for owner in (me_dp, (me_dp + 1) % n_dp)
    ]
    came_from = [(me_voc - i) % n_voc for i in range(n_voc)]
    meta = jnp.stack(came_from + firsts).astype(jnp.int32)

    weights = (head_weight, dp_swap(head_weight))

    own = hidden.transpose(1, 2, 3, 0).reshape(rows, part)
    chunk = {(0, 0): own}
    call = functools.partial(logits_call, meta=meta, weights=weights, part=part, n_voc=n_voc)
    cross = lambda a: [lax.ppermute(a, "ctx", ring(n_ctx, t)) for t in beyond]
    near = sorted({1, n_voc - 1})
    rest = [i for i in range(1, n_voc) if i not in near]

    def arrive(i, c, over):
        chunk[0, i] = c
        for t, o in zip(beyond, over):
            chunk[t, i] = o

    came, over, (again,) = together([along(own, ring(n_voc, i)) for i in near], cross(own), [own])
    arrive(0, own, over)
    over = [cross(c) for c in came]
    for i, c, o in zip(near, came, over):
        arrive(i, c, o)
    came = [along(again, ring(n_voc, i)) for i in rest]
    (again,), (raw,) = together([again], [targets])
    pair = lax.broadcasted_iota(jnp.int32, targets.shape, 0)
    mine = jnp.sum(jnp.where(pair == me_dp, raw, 0), axis=0)
    blocks = [mine[:, b * window:(b + 1) * window].reshape(rows) for b in range(n_ctx)]
    wanted = []
    for t in range(n_ctx):
        at = (me_ctx - t) % n_ctx
        wanted.append(sum(jnp.where(at == b, blocks[b], 0) for b in range(n_ctx))[:, None])
    target = jnp.concatenate(wanted)
    logits = call(
        [(0, {i: chunk[0, i] for i in [0] + near}, None, None)] + [(t, {0: chunk[t, 0]}, None, None) for t in beyond]
    )
    came, logits, *over = together(came, list(logits), *over)
    for i, o in zip(near, over):
        arrive(i, chunk[0, i], o)
    for i, c in zip(rest, came):
        arrive(i, c, cross(c))
    late = [(t, i) for i in rest for t in beyond]
    soon = [k for k in chunk if k not in late]
    done = list(call(
        [(0, {i: chunk[0, i] for i in rest}, logits[0], wanted[0])]
        + [(t, {i: chunk[t, i] for i in near}, logits[t], None) for t in beyond]
    ))
    last, done = together([chunk[k] for k in late], done)
    chunk.update(zip(late, last))
    stats = [done.pop(1)]
    logits = done
    final = n_voc - 1
    done = call([(t, {i: chunk[t, i] for i in rest}, logits[t], wanted[t]) for t in beyond])
    logits = [logits[0]] + list(done[0::2])
    stats = stats + list(done[1::2])

    far_soon = dp_swap(jnp.stack([chunk[k] for k in soon]))

    def merge(seen):
        merged = []
        for b in range(n_ctx):
            these = [a[(b - t) % n_ctx] for t, a in seen]
            top = these[0][0]
            for a in these[1:]:
                top = jnp.maximum(top, a[0])
            total = sum(a[1] * jnp.exp(a[0] - top) for a in these)
            picked = sum(a[2] for a in these)
            merged.append(jnp.pad(jnp.stack([top, total, picked]), ((0, 5), (0, 0))))
        return jnp.concatenate(merged, axis=1)

    stats = jnp.stack(stats)
    if line and n_ctx == 2:
        corner = [(2 * a + c, 2 * b + (1 - c)) for a, b in PAIRS_OUT for c in range(2)]
        diagonal = lax.ppermute(stats, ("vocab", "ctx"), corner)
        merged = merge([(0, stats), (1, cross(stats)[0]), (0, along(stats, PAIRS_OUT)), (1, diagonal)])
        all_stats = [merged, along(merged, SWAP_HALVES)]
    else:
        merged = merge([(0, stats)] + list(zip(beyond, cross(stats))))
        all_stats = [merged] + [along(merged, ring(n_voc, i)) for i in range(1, n_voc)]

    meta_grads = jnp.stack([part_of[final]] + firsts + [me_dp, me_ctx]).astype(jnp.int32)
    small = (response_start, other_sums, ref_logp, loss_cotangent)
    grads_own, grads_far, flipped_own, flipped_far, loss, kept, *send = grads_call(
        logits, target, all_stats, small, weights, meta_grads, part, window
    )
    theirs = dp_swap(grads_far)
    far_late = dp_swap(jnp.stack(together([chunk[k] for k in late], [kept])[0]))
    back = lambda cs: [lax.ppermute(c, "ctx", ring(n_ctx, -t)) for t, c in zip(beyond, cs)]
    landed = []
    for step in range(n_voc):
        slot = final - step
        over = back(send)
        came = []
        if line:
            if step == 1:
                sum_3 = (kept_before, arrived)
                came = [along(add_call(*sum_3), FROM_ENDS)]
            elif step == 2:
                sum_2 = (kept_before, arrived)
                came = [along(add_call(*sum_2), FROM_ENDS), along(add_call(sum_3[0], sum_3[1] + landed), PAIR_IN)]
            elif step == 3:
                came = [
                    along(add_call(kept_before, arrived + landed[1:]), PAIRS_OUT),
                    along(add_call(sum_2[0], sum_2[1] + landed[:1]), PAIR_IN),
                ]
        elif step:
            came = [along(add_call(kept_before, arrived), ring(n_voc, -(slot + 1)))]
        kept_before = kept
        if step < n_voc - 1:
            kept, *send = spread_call(flipped_own, flipped_far, weights, part_of[slot - 1], part, rows)
            arrived, came, send = together(over, came, send)
        else:
            grad_head = head_call(chunk, [(soon, far_soon), (late, far_late)], [grads_own, theirs], meta)
            arrived, came, (grad_head,) = together(over, came, [grad_head])
        landed = came if line else landed + came
    summed = add_call(kept_before, arrived + landed, turned=True)
    grad_hidden = summed.reshape(1, sides, window, part).transpose(3, 0, 1, 2)

    far_loss = dp_swap(loss)
    pair = lax.broadcasted_iota(jnp.int32, (n_dp,), 0)
    pair_loss = jnp.where(pair == me_dp, loss[0, :n_dp], far_loss[0, :n_dp])
    return (grad_hidden, grad_head, pair_loss)


def solution(mesh):
    placed = (
        P("vocab", ("groups", "dp"), None, "ctx"),
        P(None, ("vocab", "ctx", "dp")),
        P("groups", None, None),
        P("groups"),
        P("groups", None),
        P("groups", None),
        P("groups"),
    )
    return jax.shard_map(
        shards,
        mesh=mesh,
        in_specs=placed,
        out_specs=(
            P("vocab", ("groups", "dp"), None, "ctx"),
            P("groups", ("vocab", "ctx", "dp")),
            P("groups"),
        ),
        check_vma=False,
    )
```
